32 devices in a mesh: fsdp: 4 (over y, x), ctx: 4 (over z), tp: 2 (over core).
Axes of the slice: x: 2, y: 2, z: 4, core: 2. Of those that a mesh axis runs over, the one named last changes fastest.
Arguments:
- tokens: bfloat16 [3072, 2048], P(('fsdp', 'ctx')), may hold values from -6 to 6
- cotangent: bfloat16 [3072, 2048], P(('fsdp', 'ctx')), may hold values from -6 to 6
- attn_ids: int32 [3072, 2], P(('fsdp', 'ctx')), may hold values from 0 to 3, all different within a row; in each aligned block of 192 rows (0 to 191, 192 to 383, ...) at most 144 rows name the same one
- mlp_ids: int32 [3072, 2], P(('fsdp', 'ctx')), may hold values from 0 to 3, all different within a row; in each aligned block of 192 rows (0 to 191, 192 to 383, ...) at most 144 rows name the same one
- span_ids: int32 [4, 2], replicated, may hold values from 0 to 7, as said below
- attn_gain: bfloat16 [2048], P('ctx'), may hold values from 0.25 to 1.75
- attn_router: bfloat16 [2048, 4], P('ctx'), may hold values from -0.09375 to 0.09375
- kv_weight: bfloat16 [2, 2048, 2048], P(None, 'ctx', ('fsdp', 'tp')), may hold values from -0.125 to 0.125
- query_weight: bfloat16 [4, 2048, 2048], P(None, 'ctx', ('fsdp', 'tp')), may hold values from -0.125 to 0.125
- output_weight: bfloat16 [4, 2048, 2048], P(None, 'ctx', ('fsdp', 'tp')), may hold values from -2 to 2
- mlp_gain: bfloat16 [2048], P('ctx'), may hold values from 0.25 to 1.75
- mlp_router: bfloat16 [2048, 4], P('ctx'), may hold values from -0.09375 to 0.09375
- gate_up_weight: bfloat16 [4, 2, 2048, 5632], P(None, None, 'ctx', ('fsdp', 'tp')), may hold values from -0.125 to 0.125
- down_weight: bfloat16 [4, 2048, 5632], P(None, 'ctx', ('fsdp', 'tp')), may hold values from -0.078125 to 0.078125
Outputs:
- layer_out: bfloat16 [3072, 2048], P(('fsdp', 'ctx'))
- grad_tokens: bfloat16 [3072, 2048], P(('fsdp', 'ctx'))
- grad_attn_gain: float32 [2048], P(('fsdp', 'ctx'))
- grad_attn_router: float32 [2048, 4], P(('fsdp', 'ctx'))
- grad_kv_weight: float32 [2, 2048, 2048], P(None, 'ctx', ('fsdp', 'tp'))
- grad_query_weight: float32 [4, 2048, 2048], P(None, 'ctx', ('fsdp', 'tp'))
- grad_output_weight: float32 [4, 2048, 2048], P(None, 'ctx', ('fsdp', 'tp'))
- grad_mlp_gain: float32 [2048], P(('fsdp', 'ctx'))
- grad_mlp_router: float32 [2048, 4], P(('fsdp', 'ctx'))
- grad_gate_up: float32 [4, 2, 2048, 5632], P(None, None, 'ctx', ('fsdp', 'tp'))
- grad_down: float32 [4, 2048, 5632], P(None, 'ctx', ('fsdp', 'tp'))
The draws below stay inside these ranges and needn't reach their ends.
Inputs may be any that keep to these rules, and one draw needn't show every extreme that they name: `attn_ids`: each row names two different experts; among the 192 rows of one device no expert is named more than 144 times, a bound that some block reaches. `mlp_ids`: each row names two different experts; among the 192 rows of one device no expert is named more than 144 times, a bound that some block reaches. `span_ids`: row c holds p and 2 * 4 - 1 - p for a p below 4; every span number appears once.
All inputs are finite; a program needn't handle non-finite values.
Results may differ from the reference program's by a relative error of at most 0.025.
Values may be sent and summed in bfloat16 or wider, within the bound.
A program may use at most 448 MiB of HBM per device.

```python
import math
from functools import partial
import jax
import jax.numpy as jnp
import numpy as np
from jax import lax

D = 2048
HEADS = 16
DH = 128
FF = 5632
EA = 4
EM = 4
TOK_DEV = 192
HD = 2048
CAP = 144
SEQ = 768
TOKENS = 3072
N_FSDP = 4
N_CTX = 4


def draw_span_ids(key, part):
    key = jax.random.fold_in(key, 7)
    order = jax.random.permutation(key, N_CTX).astype(jnp.int32)
    return jnp.stack([order, 2 * N_CTX - 1 - order], axis=1).astype(jnp.int32)


def shard_levels(stream_key, shape, split, smallest, high):
    loudness = 1.0
    for axis_at, blocks in split:
        draws = jax.random.uniform(jax.random.fold_in(jax.random.fold_in(stream_key, 6), axis_at), (blocks,), jnp.float32, smallest / len(split), high / len(split))
        loudness = loudness * jnp.repeat(jnp.exp(draws), shape[axis_at] // blocks).reshape((-1,) + (1,) * (len(shape) - 1 - axis_at))
    return loudness


def deal_out(rng, own, number, rows, amount, top, limit, slope):
    order = jax.random.permutation(rng, amount)
    packed, common = shares(amount, rows * top, limit, slope, True), shares(amount, rows * top, limit, slope, False)
    places = jnp.arange(amount)

    def named(tallies, turn):
        used = int((tallies > 0).sum())
        fixed = max(1, used // 4)
        passed = fixed + (places - fixed + turn * (used - fixed)) % max(1, amount - fixed)
        return jnp.zeros((amount,), jnp.int32).at[order[jnp.where(places < fixed, places, passed)]].set(jnp.asarray(tallies, jnp.int32))

    tallies = jnp.where(number % 4 == 0, named(packed, number // 4), named(common, number - number // 4 - 1))
    mixed = jax.random.permutation(jax.random.fold_in(own, 3), amount)
    giver, taker = mixed[0:amount // 2 * 2:2], mixed[1:amount // 2 * 2:2]
    slack = jnp.minimum(tallies[giver] - 1, limit - tallies[taker]) // 2
    slack = jnp.where((giver == order[0]) | (taker == order[0]) | (tallies[taker] == 0), 0, jnp.maximum(slack, 0))
    passed = jax.random.randint(jax.random.fold_in(own, 4), (amount // 2,), 0, 1 << 20) % (slack + 1)
    tallies = tallies.at[giver].add(-passed).at[taker].add(passed)
    labels = jnp.searchsorted(jnp.cumsum(tallies), jnp.arange(rows * top), side="right").astype(jnp.int32)
    grid = labels.reshape(top, rows).T
    grid = grid[jax.random.permutation(jax.random.fold_in(own, 1), rows)]
    turn = jax.random.randint(jax.random.fold_in(own, 2), (rows, 1), 0, top)
    return jnp.take_along_axis(grid, (jnp.arange(top)[None, :] + turn) % top, axis=1)


def shares(number_of, total, bound, skew, full):
    portions = [(1 << 20) // math.isqrt(rank ** skew) + 1 for rank in range(1, number_of + 1)]
    largest = bound if full else min(bound, max(-(-total // number_of), total * portions[0] // sum(portions)))
    least = 1 if total - largest >= number_of - 1 else 0
    holding, rest = [largest] + [least] * (number_of - 1), total - largest - least * (number_of - 1)
    while rest > 0:
        free = [i for i in range(1, number_of) if holding[i] < largest] or [i for i in range(1, number_of) if holding[i] < bound]
        mass, left = sum([portions[i] for i in free]), rest
        for i in free:
            extra = min(bound - holding[i], max(1, left * portions[i] // mass), rest)
            holding[i] = holding[i] + extra
            rest = rest - extra
    return np.array(holding)


def normal_values(stream_key, dims, scale, most, split=(), kind=jnp.bfloat16):
    drawn = jax.random.normal(stream_key, dims, jnp.float32) * scale
    if len(split) > 0:
        drawn = shard_levels(stream_key, dims, split, -0.22, 0.18) * drawn
    return jnp.clip(drawn, min=-most, max=most).astype(kind)


def setup_inputs(seed: int = 0) -> dict:
    splits = jax.random.split(jax.random.key(seed), 15)
    tokens = normal_values(splits[0], (TOKENS, D), 1.0, 6.0, ((0, 16),))
    cotangent = normal_values(splits[1], (TOKENS, D), 1.0, 6.0, ((0, 16),))
    attn_ids_keys = jax.random.split(jax.random.fold_in(splits[2], 1), TOKENS // TOK_DEV)
    attn_ids_turns = jax.random.permutation(jax.random.fold_in(splits[2], 3), TOKENS // TOK_DEV)
    attn_ids = jax.vmap(lambda own, number: deal_out(jax.random.fold_in(splits[2], 2), own, number, TOK_DEV, EA, 2, CAP, 1))(attn_ids_keys, attn_ids_turns).reshape((TOKENS, 2))
    mlp_ids_keys = jax.random.split(jax.random.fold_in(splits[3], 1), TOKENS // TOK_DEV)
    mlp_ids_turns = jax.random.permutation(jax.random.fold_in(splits[3], 3), TOKENS // TOK_DEV)
    mlp_ids = jax.vmap(lambda own, number: deal_out(jax.random.fold_in(splits[3], 2), own, number, TOK_DEV, EM, 2, CAP, 1))(mlp_ids_keys, mlp_ids_turns).reshape((TOKENS, 2))
    span_ids = draw_span_ids(jax.random.fold_in(splits[14], 71), 0)
    attn_gain = jnp.clip(1.0 + 0.15 * jax.random.normal(splits[5], (D,), jnp.float32), 0.25, 1.75).astype(jnp.bfloat16)
    attn_router = normal_values(splits[6], (D, EA), (2 * D) ** -0.5, 0.09375, ((0, 4),))
    kv_weight = normal_values(splits[7], (2, D, HD), D ** -0.5, 0.125, ((1, 4), (2, 8)))
    query_weight = normal_values(splits[8], (EA, D, HD), D ** -0.5, 0.125, ((1, 4), (2, 8)))
    output_weight = normal_values(splits[9], (EA, D, HD), 8 ** -0.5, 2.0, ((1, 4), (2, 8)))
    mlp_gain = jnp.clip(1.0 + 0.15 * jax.random.normal(splits[10], (D,), jnp.float32), 0.25, 1.75).astype(jnp.bfloat16)
    mlp_router = normal_values(splits[11], (D, EM), (2 * D) ** -0.5, 0.09375, ((0, 4),))
    gate_up_weight = normal_values(splits[12], (EM, 2, D, FF), D ** -0.5, 0.125, ((2, 4), (3, 8)))
    down_weight = normal_values(splits[13], (EM, D, FF), FF ** -0.5, 0.078125, ((1, 4), (2, 8)))
    return {"tokens": tokens, "cotangent": cotangent, "attn_ids": attn_ids, "mlp_ids": mlp_ids, "span_ids": span_ids, "attn_gain": attn_gain, "attn_router": attn_router, "kv_weight": kv_weight, "query_weight": query_weight, "output_weight": output_weight, "mlp_gain": mlp_gain, "mlp_router": mlp_router, "gate_up_weight": gate_up_weight, "down_weight": down_weight}


EPSILON = 1e-06
ROPE_BASE = 10000.0
MASKED = -1e+30
HIGH = lax.Precision.HIGHEST

@jax.custom_vjp
def low(v):
    return lax.optimization_barrier(v.astype(jnp.bfloat16)).astype(jnp.float32)

@jax.custom_vjp
def low_back(v):
    return v

def low_keep(v):
    return (low(v), None)

def low_pass(kept, grad):
    return (grad,)

def back_keep(v):
    return (v, None)

def back_low(kept, grad):
    return (low(grad),)
low.defvjp(low_keep, low_pass)
low_back.defvjp(back_keep, back_low)

def positions(span_ids):
    half_len = TOK_DEV // 2
    offsets = jnp.arange(TOK_DEV, dtype=jnp.int32)
    upper_part = (offsets >= half_len).astype(jnp.int32)
    within = offsets - upper_part * half_len
    span_of = span_ids[:, 0:1] * (1 - upper_part)[None, :] + span_ids[:, 1:2] * upper_part[None, :]
    return (span_of * half_len + within[None, :]).reshape(-1).astype(jnp.int32)

def rotation(place):
    freqs = ROPE_BASE ** (-jnp.arange(DH // 2, dtype=jnp.float32) / (DH // 2))
    angles = place.astype(jnp.float32)[:, None] * freqs[None, :]
    return (jnp.cos(angles), jnp.sin(angles))

def rope(values, cosine_table, sine_table):
    row_count = values.shape[0]
    halves = values.reshape(row_count, -1, 2, DH // 2)
    lower_half = halves[:, :, 0]
    upper_half = halves[:, :, 1]
    cosine_wide = cosine_table[:, None, :]
    sine_wide = sine_table[:, None, :]
    turned = jnp.stack([lower_half * cosine_wide - upper_half * sine_wide, upper_half * cosine_wide + lower_half * sine_wide], axis=2)
    return turned.reshape(row_count, -1)

def chosen_gates(normed, router, onehot):
    logits = jnp.dot(normed, router, precision=HIGH)
    picked = jnp.einsum('ne,nke->nk', logits, onehot, precision=HIGH)
    return jax.nn.softmax(picked, axis=-1)

def head_attention(operands, causal):
    query_h, key_h, value_h = operands
    scale_factor = 1.0 / math.sqrt(DH)
    scores = low_back(jnp.dot(query_h, key_h.T, precision=HIGH) * scale_factor)
    scores = jnp.where(causal, scores, MASKED)
    probs = jax.nn.softmax(scores, axis=-1)
    return jnp.dot(low(probs), value_h, precision=HIGH)

def sequence_layer(params, operands, cosine_table, sine_table, cosine_slots, sine_slots, causal):
    gain_one, router_attn, kv_full, query_full, output_full, gain_two, router_mlp, gate_up_full, down_full = params
    inputs, attn_hot, mlp_hot = operands
    length = inputs.shape[0]
    inverse_one = lax.rsqrt(lax.optimization_barrier(jnp.mean(inputs * inputs, axis=-1, keepdims=True)) + EPSILON)
    normed_one = low(inputs * inverse_one * gain_one)
    attn_gates = chosen_gates(normed_one, router_attn, attn_hot)
    keys = low(rope(low_back(jnp.dot(normed_one, kv_full[0], precision=HIGH)), cosine_table, sine_table))
    values = low(low_back(jnp.dot(normed_one, kv_full[1], precision=HIGH)))
    query_all = jnp.einsum('nd,edh->neh', normed_one, query_full, precision=HIGH)
    query_sel = jnp.einsum('nke,neh->nkh', attn_hot, query_all, precision=HIGH).reshape(2 * length, HD)
    queries = low(rope(low_back(query_sel), cosine_slots, sine_slots))
    query_heads = queries.reshape(2 * length, HEADS, DH).transpose(1, 0, 2)
    key_heads = keys.reshape(length, HEADS, DH).transpose(1, 0, 2)
    value_heads = values.reshape(length, HEADS, DH).transpose(1, 0, 2)
    attended = lax.map(jax.checkpoint(partial(head_attention, causal=causal)), (query_heads, key_heads, value_heads))
    mixed = low(low_back(attended.transpose(1, 0, 2).reshape(length, 2, HD)))
    branch_all = jnp.einsum('nkh,edh->nked', mixed, output_full, precision=HIGH)
    branch = low_back(jnp.einsum('nke,nked->nkd', attn_hot, branch_all, precision=HIGH))
    residual = inputs + lax.optimization_barrier(jnp.sum(attn_gates[:, :, None] * branch, axis=1))
    inverse_two = lax.rsqrt(lax.optimization_barrier(jnp.mean(residual * residual, axis=-1, keepdims=True)) + EPSILON)
    normed_two = low(residual * inverse_two * gain_two)
    mlp_gates = chosen_gates(normed_two, router_mlp, mlp_hot)
    expert_share = jnp.einsum('nk,nke->en', mlp_gates, mlp_hot, precision=HIGH)

    def expert_step(running, pieces):
        both_weights, weight_down, share = pieces
        gate_pre = low_back(jnp.dot(normed_two, both_weights[0], precision=HIGH))
        up_pre = low_back(jnp.dot(normed_two, both_weights[1], precision=HIGH))
        hidden = low(jax.nn.silu(gate_pre) * up_pre)
        branch_out = low_back(jnp.dot(hidden, weight_down.T, precision=HIGH))
        return (running + share[:, None] * branch_out, None)
    mlp_total = lax.scan(jax.checkpoint(expert_step), jnp.zeros_like(residual), (gate_up_full, down_full, expert_share))[0]
    return residual + mlp_total

def reference(tokens, cotangent, attn_ids, mlp_ids, span_ids, attn_gain, attn_router, kv_weight, query_weight, output_weight, mlp_gain, mlp_router, gate_up_weight, down_weight):
    place = positions(span_ids)
    cosine_table, sine_table = rotation(place)
    slot_place = jnp.repeat(place, 2)
    cosine_slots, sine_slots = rotation(slot_place)
    causal = place[None, :] <= slot_place[:, None]
    attn_hot = (attn_ids[:, :, None] == jnp.arange(EA, dtype=jnp.int32)[None, None, :]).astype(jnp.float32).reshape(N_FSDP, SEQ, 2, EA)
    mlp_hot = (mlp_ids[:, :, None] == jnp.arange(EM, dtype=jnp.int32)[None, None, :]).astype(jnp.float32).reshape(N_FSDP, SEQ, 2, EM)
    params = (attn_gain.astype(jnp.float32), attn_router.astype(jnp.float32), kv_weight.astype(jnp.float32), query_weight.astype(jnp.float32), output_weight.astype(jnp.float32), mlp_gain.astype(jnp.float32), mlp_router.astype(jnp.float32), gate_up_weight.astype(jnp.float32), down_weight.astype(jnp.float32))
    inputs = tokens.astype(jnp.float32).reshape(N_FSDP, SEQ, D)

    def forward(weights, values):
        layer = jax.checkpoint(partial(sequence_layer, weights, cosine_table=cosine_table, sine_table=sine_table, cosine_slots=cosine_slots, sine_slots=sine_slots, causal=causal))
        return lax.map(layer, (values, attn_hot, mlp_hot))
    output, pullback = jax.vjp(forward, params, inputs)
    grad_params, grad_inputs = pullback(cotangent.astype(jnp.float32).reshape(N_FSDP, SEQ, D))
    return (output.reshape(TOKENS, D).astype(jnp.bfloat16), grad_inputs.reshape(TOKENS, D).astype(jnp.bfloat16), grad_params[0], grad_params[1], grad_params[2], grad_params[3], grad_params[4], grad_params[5], grad_params[6], grad_params[7], grad_params[8])
```

```python
import functools
import math

import jax
import jax.numpy as jnp
from jax import lax
from jax.experimental import pallas as pl
from jax.experimental.pallas import tpu as pltpu
from jax.sharding import PartitionSpec as P

DH = 128
EPSILON = 1e-06
ROPE_BASE = 10000.0
MASKED = -1e30
HIGH = lax.Precision.HIGHEST
MESH = pl.DeviceIdType.MESH
AXES = ("fsdp", "ctx", "tp")
F32 = jnp.float32
BF16 = jnp.bfloat16
VMEM_LIMIT = 60 * 1024 * 1024
NT = (((1,), (1,)), ((), ()))
NN = (((1,), (0,)), ((), ()))
TN = (((0,), (0,)), ((), ()))


def dot(a, b, dims=NN):
    return lax.dot_general(a, b, dims, preferred_element_type=F32)


class Layout:
    def __init__(self, experts):
        self.nf = lax.axis_size("fsdp")
        self.nc = lax.axis_size("ctx")
        self.nt = lax.axis_size("tp")
        self.experts = experts
        self.rep = self.nc // experts
        self.seqs = self.nf // self.nt
        self.f = lax.axis_index("fsdp")
        self.c = lax.axis_index("ctx")
        self.t = lax.axis_index("tp")
        self.home = self.t == self.f // self.seqs
        self.sizes = (self.nf, self.nc, self.nt, self.seqs)

    def flat(self, f, c, t):
        return (f * self.nc + c) * self.nt + t


def home_pairs(lay, move):
    pairs = []
    for f in range(lay.nf):
        t = f // lay.seqs
        for c in range(lay.nc):
            f2, c2 = move(f, c)
            pairs.append((lay.flat(f, c, t), lay.flat(f2, c2, t)))
    return pairs


def collect_permute(lay, block_of, blocks, stride):
    got, last = [], None
    for j in range(blocks):
        partial = block_of(j, last)
        zeros = jnp.zeros((lay.nf,) + partial.shape[1:], partial.dtype)
        full = lax.dynamic_update_slice_in_dim(zeros, partial, lay.t * lay.seqs, 0)
        last = lax.psum_scatter(full, "fsdp", scatter_dimension=0, tiled=True)[0]
        if j > 0:
            pairs = home_pairs(lay, lambda f, c: (f, (c - stride * j) % lay.nc))
            last = lax.ppermute(last, AXES, pairs)
        got.append(last)
    return jnp.stack(got)


class Haul:
    def __init__(self, array, piece=None, shape=None, both=False):
        self.array, self.piece, self.both = array, piece, both
        self.shape = array.shape if shape is None else shape

    def out_shapes(self, nc):
        dims = self.shape if self.piece is None else (nc,) + self.shape
        return [jax.ShapeDtypeStruct(dims, self.array.dtype)] * (2 if self.both else 1)

    def scratch(self, nc):
        return [pltpu.SemaphoreType.DMA((nc,))] * (4 if self.both else 2)

    def bind(self, place, src, outs, sems):
        load = Load()
        load.piece, load.both, load.place = self.piece, self.both, place
        load.src, load.outs, load.sems = src, outs, sems
        return load


class Load:
    def along_ctx(self, j):
        nc, c, nt, t = self.place
        return pltpu.make_async_remote_copy(
            src_ref=self.piece(self.src, lax.rem(c + j, nc)),
            dst_ref=self.outs[0].at[c],
            send_sem=self.sems[0].at[j],
            recv_sem=self.sems[1].at[j],
            device_id={"ctx": lax.rem(c + j, nc)},
            device_id_type=MESH,
        )

    def landed(self, j):
        nc, c, nt, t = self.place
        here = self.outs[0].at[lax.rem(c - j + nc, nc)]
        return pltpu.make_async_remote_copy(
            src_ref=here,
            dst_ref=here,
            send_sem=self.sems[0].at[j],
            recv_sem=self.sems[1].at[j],
            device_id={"ctx": lax.rem(c + j, nc)},
            device_id_type=MESH,
        )

    def to_core(self, j):
        nc, c, nt, t = self.place
        if self.piece is None:
            src, dst, at = self.src, self.outs[0], 0
        else:
            source = lax.rem(c - j + nc, nc)
            src = self.piece(self.src, c) if j == 0 else self.outs[0].at[source]
            dst, at = self.outs[1].at[source], 2
        return pltpu.make_async_remote_copy(
            src_ref=src,
            dst_ref=dst,
            send_sem=self.sems[at].at[j],
            recv_sem=self.sems[at + 1].at[j],
            device_id={"tp": lax.rem(t + 1, nt)},
            device_id_type=MESH,
        )

    def keep(self):
        nc, c, nt, t = self.place
        return pltpu.make_async_copy(
            self.piece(self.src, c), self.outs[0].at[c], self.sems[0].at[0]
        )

    def start(self):
        if self.piece is None:
            self.to_core(0).start()
            return
        for j in range(1, self.place[0]):
            self.along_ctx(j).start()
        self.keep().start()
        if self.both:
            self.to_core(0).start()

    def pass_on(self):
        if self.piece is None:
            return
        for j in range(1, self.place[0]):
            self.landed(j).wait_recv()
            if self.both:
                self.to_core(j).start()

    def finish(self):
        if self.piece is None:
            self.to_core(0).wait()
            return
        self.keep().wait()
        for j in range(self.place[0]):
            if j > 0:
                self.along_ctx(j).wait_send()
            if self.both:
                self.to_core(j).wait()


class Relay:
    both = True

    def __init__(self, array):
        self.array = array

    def out_shapes(self, nc):
        return [jax.ShapeDtypeStruct((nc,) + self.array.shape, self.array.dtype)] * 2

    def scratch(self, nc):
        return [pltpu.SemaphoreType.DMA((2, nc))] * 2 + [pltpu.SemaphoreType.DMA((nc,))] * 2

    def bind(self, place, src, outs, sems):
        load = RelayLoad()
        load.place, load.src, load.outs, load.sems = place, src, outs, sems
        return load


def relay_step(place, way, k, src, dst, send_sem, recv_sem):
    nc, c = place[:2]
    step = 1 - 2 * way
    copy = pltpu.make_async_remote_copy(
        src_ref=src,
        dst_ref=dst,
        send_sem=send_sem.at[way, k],
        recv_sem=recv_sem.at[way, k],
        device_id={"ctx": lax.rem(c + step + nc, nc)},
        device_id_type=MESH,
    )
    sent = jnp.logical_and(c - step * k >= 0, c - step * k < nc)
    sent = jnp.logical_and(sent, jnp.logical_and(c + step >= 0, c + step < nc))
    return copy, sent


def relayed(place, way, k):
    nc, c = place[:2]
    source = c - (1 - 2 * way) * k
    return lax.rem(source + nc, nc), jnp.logical_and(source >= 0, source < nc)


class RelayLoad:
    def copy(self, way, k):
        source = relayed(self.place, way, k)[0]
        src = self.src if k == 0 else self.outs[0].at[source]
        return relay_step(self.place, way, k, src, self.outs[0].at[source], *self.sems[:2])

    def arrival(self, way, k):
        source, there = relayed(self.place, way, k)
        here = self.outs[0].at[source]
        return pltpu.make_async_remote_copy(
            src_ref=here,
            dst_ref=here,
            send_sem=self.sems[0].at[way, k],
            recv_sem=self.sems[1].at[way, k - 1],
            device_id={"ctx": lax.rem(self.place[1] + 1, self.place[0])},
            device_id_type=MESH,
        ), there

    def to_core(self, source):
        nc, c, nt, t = self.place
        return pltpu.make_async_remote_copy(
            src_ref=self.outs[0].at[source],
            dst_ref=self.outs[1].at[source],
            send_sem=self.sems[2].at[source],
            recv_sem=self.sems[3].at[source],
            device_id={"tp": lax.rem(t + 1, nt)},
            device_id_type=MESH,
        )

    def own_to_core(self):
        nc, c, nt, t = self.place
        return pltpu.make_async_remote_copy(
            src_ref=self.src,
            dst_ref=self.outs[1].at[c],
            send_sem=self.sems[2].at[c],
            recv_sem=self.sems[3].at[c],
            device_id={"tp": lax.rem(t + 1, nt)},
            device_id_type=MESH,
        )

    def keep(self):
        nc, c = self.place[:2]
        return pltpu.make_async_copy(self.src, self.outs[0].at[c], self.sems[0].at[0, nc - 1])

    def start(self):
        for way in range(2):
            copy, sent = self.copy(way, 0)
            pl.when(sent)(copy.start)
        self.keep().start()
        self.own_to_core().start()

    def pass_on(self):
        nc = self.place[0]
        for k in range(1, nc):
            for way in range(2):
                arrival, there = self.arrival(way, k)
                source = relayed(self.place, way, k)[0]
                copy, sent = self.copy(way, k)

                @pl.when(there)
                def _():
                    arrival.wait_recv()
                    self.to_core(source).start()

                if k < nc - 1:
                    pl.when(sent)(copy.start)

    def finish(self):
        nc, c = self.place[:2]
        self.keep().wait()
        for k in range(nc - 1):
            for way in range(2):
                copy, sent = self.copy(way, k)
                pl.when(sent)(copy.wait_send)
        for source in range(nc):

            @pl.when(c != source)
            def _():
                self.to_core(source).wait()

        self.own_to_core().wait()


class Share:
    both = False

    def __init__(self, lay, array):
        self.lay_sizes, self.array = lay.sizes, array

    def out_shapes(self, nc):
        nt, seqs = self.lay_sizes[2:]
        n, rows, width = self.array.shape
        return [jax.ShapeDtypeStruct((seqs, n, rows, nt * width), self.array.dtype)]

    def scratch(self, nc):
        nf, _, nt, seqs = self.lay_sizes
        return [pltpu.SemaphoreType.DMA((nf,)), pltpu.SemaphoreType.DMA((seqs, nt))]

    def bind(self, place, src, outs, sems):
        load = SharedLoad()
        load.lay_sizes, load.src, load.out, load.sems = self.lay_sizes, src, outs[0], sems
        return load


class SharedLoad:
    def target(self, slot, core):
        width = self.src.shape[-1]
        return self.out.at[slot, :, :, pl.ds(pl.multiple_of(core * width, 128), width)]

    def to_chip(self, k):
        nf, _, nt, seqs = self.lay_sizes
        f, t = lax.axis_index("fsdp"), lax.axis_index("tp")
        own = lax.rem(f, seqs)
        return pltpu.make_async_remote_copy(
            src_ref=self.src,
            dst_ref=self.target(own, t),
            send_sem=self.sems[0].at[k],
            recv_sem=self.sems[1].at[own, t],
            device_id={"fsdp": lax.rem(f + k, nf), "tp": f // seqs},
            device_id_type=MESH,
        )

    def keep(self):
        f, t = lax.axis_index("fsdp"), lax.axis_index("tp")
        own = lax.rem(f, self.lay_sizes[3])
        return pltpu.make_async_copy(self.src, self.target(own, t), self.sems[0].at[0])

    def at_home(self):
        return lax.axis_index("tp") == lax.axis_index("fsdp") // self.lay_sizes[3]

    def start(self):
        for k in range(1, self.lay_sizes[0]):
            self.to_chip(k).start()
        pl.when(self.at_home())(lambda: self.keep().start())
        pl.when(jnp.logical_not(self.at_home()))(lambda: self.to_chip(0).start())

    def pass_on(self):
        pass

    def finish(self):
        nf, _, nt, seqs = self.lay_sizes
        f, t = lax.axis_index("fsdp"), lax.axis_index("tp")
        for i in range(seqs):
            for core in range(nt):
                mine = jnp.logical_and(f == t * seqs + i, t == core)

                @pl.when(jnp.logical_not(mine))
                def _():
                    pltpu.make_async_remote_copy(
                        src_ref=self.target(i, core),
                        dst_ref=self.target(i, core),
                        send_sem=self.sems[0].at[0],
                        recv_sem=self.sems[1].at[i, core],
                        device_id={"fsdp": lax.rem(f + 1, nf)},
                        device_id_type=MESH,
                    ).wait_recv()

        for k in range(1, nf):
            self.to_chip(k).wait_send()
        pl.when(self.at_home())(lambda: self.keep().wait())
        pl.when(jnp.logical_not(self.at_home()))(lambda: self.to_chip(0).wait_send())


class Hauls:
    def __init__(self, lay, hauls):
        self.nc, self.hauls = lay.nc, list(hauls)
        self.operands = [h.array for h in self.hauls]
        self.shapes = [shape for h in self.hauls for shape in h.out_shapes(lay.nc)]
        self.scratch = [sem for h in self.hauls for sem in h.scratch(lay.nc)]
        anywhere = pl.BlockSpec(memory_space=pl.ANY)
        self.in_specs = [anywhere] * len(self.operands)
        self.out_specs = [anywhere] * len(self.shapes)

    def split(self, refs, n_in, n_out):
        more_in, more_out, sems = len(self.operands), len(self.shapes), len(self.scratch)
        ins, refs = refs[:n_in], refs[n_in:]
        srcs, refs = refs[:more_in], refs[more_in:]
        outs, refs = refs[:n_out], refs[n_out:]
        dsts, refs = refs[:more_out], refs[more_out:]
        scratch = refs[: len(refs) - sems]
        refs = refs[len(refs) - sems :]
        c, t = lax.axis_index("ctx"), lax.axis_index("tp")
        place = (self.nc, c, lax.axis_size("tp"), t)
        loads = []
        for haul, src in zip(self.hauls, srcs):
            count, held = len(haul.out_shapes(self.nc)), len(haul.scratch(self.nc))
            loads.append(haul.bind(place, src, dsts[:count], refs[:held]))
            dsts, refs = dsts[count:], refs[held:]
        return ins, outs, scratch, loads


def start_all(loads):
    for load in loads:
        load.start()


def finish_all(loads):
    for load in loads:
        load.pass_on()
    for load in loads:
        load.finish()


def greet(nf, nc, nt, whole_plane=False):
    f, c, t = lax.axis_index("fsdp"), lax.axis_index("ctx"), lax.axis_index("tp")
    barrier = pltpu.get_barrier_semaphore()
    peers = [{"ctx": lax.rem(c + gap, nc)} for gap in range(1, nc)]
    for k in range(nf):
        for u in range(nt):
            if (k, u) != (0, 0) and (k == 0 or u == 0 or whole_plane):
                peers.append({"fsdp": lax.rem(f + k, nf), "tp": lax.rem(t + u, nt)})
    for peer in peers:
        pl.semaphore_signal(barrier, inc=1, device_id=peer, device_id_type=MESH)
    pl.semaphore_wait(barrier, len(peers))


def params(call_id):
    return pltpu.CompilerParams(
        collective_id=call_id, has_side_effects=True, vmem_limit_bytes=VMEM_LIMIT
    )


def opening_body(lay_sizes, experts, hauls, *refs):
    nf, nc, nt, seqs = lay_sizes
    (src, small, later), (out, smalls, mine, stage), sems, loads = hauls.split(refs, 3, 4)
    zsend, zrecv, psend, precv, ssend, srecv, lsend, lrecv, here = sems
    f, c, t = lax.axis_index("fsdp"), lax.axis_index("ctx"), lax.axis_index("tp")
    place = (nc, c, nt, t)
    own = lax.rem(f, seqs)
    home = t == f // seqs
    rows, width = stage.shape[1], mine.shape[2]
    greet(nf, nc, nt, True)

    def half(ref, core):
        return ref.at[pl.ds(pl.multiple_of(core * rows, 16), rows)]

    def relay(way, k):
        source = relayed(place, way, k)[0]
        from_ref = half(src, t) if k == 0 else stage.at[source]
        return relay_step(place, way, k, from_ref, stage.at[source], zsend, zrecv)

    def in_plane(source, k, first):
        return pltpu.make_async_remote_copy(
            src_ref=half(src, t) if first else stage.at[source],
            dst_ref=half(out.at[own, source], t),
            send_sem=psend.at[source, k],
            recv_sem=precv.at[own, source, t],
            device_id={"fsdp": lax.rem(f + k, nf), "tp": f // seqs},
            device_id_type=MESH,
        )

    def keep(source, first):
        from_ref = half(src, t) if first else stage.at[source]
        return pltpu.make_async_copy(from_ref, half(out.at[own, source], t), here.at[source])

    def share(source, first=False):
        for k in range(1, nf):
            in_plane(source, k, first).start()
        pl.when(home)(lambda: keep(source, first).start())
        pl.when(jnp.logical_not(home))(lambda: in_plane(source, 0, first).start())

    def small_along_ctx(j, source):
        return pltpu.make_async_remote_copy(
            src_ref=small,
            dst_ref=smalls.at[source],
            send_sem=ssend.at[j],
            recv_sem=srecv.at[j],
            device_id={"ctx": lax.rem(c + j, nc)},
            device_id_type=MESH,
        )

    def later_along_ctx(j):
        return pltpu.make_async_remote_copy(
            src_ref=later.at[j, :, pl.ds(pl.multiple_of(t * width, 128), width)],
            dst_ref=mine.at[j],
            send_sem=lsend.at[j],
            recv_sem=lrecv.at[j],
            device_id={"ctx": lax.rem(c + (nc // experts) * j, nc)},
            device_id_type=MESH,
        )

    def keep_later():
        src_ref = later.at[0, :, pl.ds(pl.multiple_of(t * width, 128), width)]
        return pltpu.make_async_copy(src_ref, mine.at[0], lsend.at[0])

    for way in range(2):
        copy, sent = relay(way, 0)
        pl.when(sent)(lambda: copy.start())
    for j in range(1, nc):
        small_along_ctx(j, c).start()
    keep_small = pltpu.make_async_copy(small, smalls.at[c], ssend.at[0])
    keep_small.start()
    share(c, True)
    keep_later().start()

    for k in range(1, nc):
        for way in range(2):
            source, there = relayed(place, way, k)

            @pl.when(there)
            def _():
                pltpu.make_async_remote_copy(
                    src_ref=stage.at[source],
                    dst_ref=stage.at[source],
                    send_sem=zsend.at[way, k],
                    recv_sem=zrecv.at[way, k - 1],
                    device_id={"ctx": lax.rem(c + 1, nc)},
                    device_id_type=MESH,
                ).wait_recv()
                if k < nc - 1:
                    copy, sent = relay(way, k)
                    pl.when(sent)(lambda: copy.start())
                share(source)

    start_all(loads)
    for j in range(1, experts):
        later_along_ctx(j).start()

    for i in range(seqs):
        for core in range(nt):
            mine_here = jnp.logical_and(f == t * seqs + i, t == core)

            @pl.when(jnp.logical_not(mine_here))
            def _():
                for source in range(nc):
                    landing = half(out.at[i, source], core)
                    pltpu.make_async_remote_copy(
                        src_ref=landing,
                        dst_ref=landing,
                        send_sem=psend.at[source, 0],
                        recv_sem=precv.at[i, source, core],
                        device_id={"fsdp": lax.rem(f + 1, nf)},
                        device_id_type=MESH,
                    ).wait_recv()

    for j in range(1, nc):
        small_along_ctx(j, lax.rem(c - j + nc, nc)).wait_recv()
        small_along_ctx(j, c).wait_send()
    keep_small.wait()
    keep_later().wait()
    for k in range(nc - 1):
        for way in range(2):
            copy, sent = relay(way, k)
            pl.when(sent)(lambda: copy.wait_send())
    for source in range(nc):
        for k in range(1, nf):
            in_plane(source, k, False).wait_send()
        pl.when(home)(lambda: keep(source, False).wait())
        pl.when(jnp.logical_not(home))(lambda: in_plane(source, 0, False).wait_send())
    for j in range(1, experts):
        later_along_ctx(j).wait()
    finish_all(loads)


def opening(lay, rows, small, later, call_id, hauls):
    count, width = rows.shape
    nf, nc, nt, seqs = lay.sizes
    hauls = Hauls(lay, hauls)
    experts = lay.experts
    dma = pltpu.SemaphoreType.DMA
    anywhere = pl.BlockSpec(memory_space=pl.ANY)
    shapes = [
        jax.ShapeDtypeStruct((seqs, nc, count, width), rows.dtype),
        jax.ShapeDtypeStruct((nc,) + small.shape, small.dtype),
        jax.ShapeDtypeStruct(later.shape[:2] + (later.shape[2] // nt,), later.dtype),
        jax.ShapeDtypeStruct((nc, count // nt, width), rows.dtype),
    ]
    return pl.pallas_call(
        functools.partial(opening_body, lay.sizes, experts, hauls),
        out_shape=shapes + hauls.shapes,
        in_specs=[anywhere] * 3 + hauls.in_specs,
        out_specs=[anywhere] * 4 + hauls.out_specs,
        scratch_shapes=[
            dma((2, nc)),
            dma((2, nc)),
            dma((nc, nf)),
            dma((seqs, nc, nt)),
            dma((nc,)),
            dma((nc,)),
            dma((experts,)),
            dma((experts,)),
            dma((nc,)),
        ]
        + hauls.scratch,
        compiler_params=params(call_id),
        name=f"opening{call_id}",
    )(rows, small, later, *hauls.operands)


def spread_body(lay_sizes, stride, blocks, hauls, *refs):
    nf, nc, nt, seqs = lay_sizes
    (src,), (out,), (zsend, zrecv, psend, precv, here), loads = hauls.split(refs, 1, 1)
    f, c, t = lax.axis_index("fsdp"), lax.axis_index("ctx"), lax.axis_index("tp")
    own = lax.rem(f, seqs)
    home = t == f // seqs
    greet(nf, nc, nt)

    def along_ctx(j):
        return pltpu.make_async_remote_copy(
            src_ref=src.at[j],
            dst_ref=out.at[own, j],
            send_sem=zsend.at[j],
            recv_sem=zrecv.at[j],
            device_id={"ctx": lax.rem(c + stride * j, nc)},
            device_id_type=MESH,
        )

    def in_plane(j, k):
        return pltpu.make_async_remote_copy(
            src_ref=src.at[0] if j == 0 else out.at[own, j],
            dst_ref=out.at[own, j],
            send_sem=psend.at[j, k],
            recv_sem=precv.at[own, j],
            device_id={"fsdp": lax.rem(f + k, nf)},
            device_id_type=MESH,
        )

    keep = pltpu.make_async_copy(src.at[0], out.at[own, 0], here)

    @pl.when(home)
    def _():
        for j in range(1, blocks):
            along_ctx(j).start()
        for k in range(1, nf):
            in_plane(0, k).start()
        keep.start()

    start_all(loads)

    @pl.when(home)
    def _():
        for j in range(1, blocks):
            along_ctx(j).wait_recv()
            for k in range(1, nf):
                in_plane(j, k).start()
        keep.wait()

    for i in range(seqs):

        @pl.when(jnp.logical_not(jnp.logical_and(home, own == i)))
        def _():
            for j in range(blocks):
                pltpu.make_async_remote_copy(
                    src_ref=out.at[i, j],
                    dst_ref=out.at[i, j],
                    send_sem=psend.at[j, 0],
                    recv_sem=precv.at[i, j],
                    device_id={"fsdp": lax.rem(f + 1, nf)},
                    device_id_type=MESH,
                ).wait_recv()

    @pl.when(home)
    def _():
        for j in range(1, blocks):
            along_ctx(j).wait_send()
        for j in range(blocks):
            for k in range(1, nf):
                in_plane(j, k).wait_send()

    finish_all(loads)


def spread(lay, rows, stride, call_id, hauls=()):
    blocks = rows.shape[0]
    hauls = Hauls(lay, hauls)
    dma = pltpu.SemaphoreType.DMA
    anywhere = pl.BlockSpec(memory_space=pl.ANY)
    return pl.pallas_call(
        functools.partial(spread_body, lay.sizes, stride, blocks, hauls),
        out_shape=[jax.ShapeDtypeStruct((lay.seqs,) + rows.shape, rows.dtype)] + hauls.shapes,
        in_specs=[anywhere] + hauls.in_specs,
        out_specs=[anywhere] + hauls.out_specs,
        scratch_shapes=[
            dma((blocks,)),
            dma((blocks,)),
            dma((blocks, lay.nf)),
            dma((lay.seqs, blocks)),
            dma,
        ]
        + hauls.scratch,
        compiler_params=params(call_id),
        name=f"spread{call_id}",
    )(rows, *hauls.operands)


def collect_body(lay_sizes, stride, blocks, by_plane, dims, sets, n_a, n_w, hauls, *refs):
    nf, nc, nt, seqs = lay_sizes
    ins, (out,), scratch, loads = hauls.split(refs, n_a + n_w, 1)
    lefts, rights = ins[:n_a], ins[n_a:]
    part, came, psend, precv, zsend, zrecv = scratch
    f, c, t = lax.axis_index("fsdp"), lax.axis_index("ctx"), lax.axis_index("tp")
    own = lax.rem(f, seqs)
    home = t == f // seqs
    greet(nf, nc, nt)
    start_all(loads)
    wide = part.shape[-1]
    rows = part.shape[-2] // blocks

    def to_chip(n, slot, s):
        chip = t * seqs + slot
        gap = lax.rem(f - chip + nf, nf) - 1
        return pltpu.make_async_remote_copy(
            src_ref=part.at[n, slot, s],
            dst_ref=came.at[n, gap, s],
            send_sem=psend.at[n, slot, s],
            recv_sem=precv.at[n, gap, s],
            device_id={"fsdp": chip},
            device_id_type=MESH,
        )

    def block(j):
        at = lax.rem(c - j + nc, nc) if by_plane else j
        return pl.ds(pl.multiple_of(at * rows, 16), rows)

    def to_owner(n, s, j):
        return pltpu.make_async_remote_copy(
            src_ref=part.at[n, own, s, block(j)],
            dst_ref=out.at[n, j, :, pl.ds(pl.multiple_of(s * wide, wide), wide)],
            send_sem=zsend.at[n, s, j],
            recv_sem=zrecv.at[n, s, j],
            device_id={"ctx": lax.rem(c - stride * j + nc, nc)},
            device_id_type=MESH,
        )

    for n, terms in enumerate(sets):

        @pl.loop(0, seqs * nc)
        def _(i):
            s = lax.rem(i, nc)
            slot = lax.rem(own + 1 + i // nc, seqs)
            acc = None
            for which, lead, first, size, weight, row in terms:
                right = rights[weight][s] if row is None else rights[weight][s, row]
                term = dot(lefts[which][lead, slot, :, first : first + size], right, dims)
                acc = term if acc is None else acc + term
            part[n, slot, s] = acc.astype(BF16)

            @pl.when(t * seqs + slot != f)
            def _():
                to_chip(n, slot, s).start()

    for n in range(len(sets)):

        @pl.when(home)
        def _():
            @pl.loop(0, nc)
            def _(s):
                for r in range(nf - 1):
                    pltpu.make_async_remote_copy(
                        src_ref=came.at[n, r, s],
                        dst_ref=came.at[n, r, s],
                        send_sem=psend.at[n, 0, s],
                        recv_sem=precv.at[n, r, s],
                        device_id={"fsdp": lax.rem(f + 1, nf)},
                        device_id_type=MESH,
                    ).wait_recv()
                for j in reversed(range(blocks)):
                    where = block(j)
                    summed = part[n, own, s, where].astype(F32)
                    for r in range(nf - 1):
                        summed = summed + came[n, r, s, where].astype(F32)
                    if j == 0:
                        out[n, 0, :, pl.ds(pl.multiple_of(s * wide, wide), wide)] = summed.astype(BF16)
                    else:
                        part[n, own, s, where] = summed.astype(BF16)
                        to_owner(n, s, j).start()

    @pl.when(home)
    def _():
        for n in range(len(sets)):
            for s in range(nc):
                for j in range(1, blocks):
                    to_owner(n, s, j).wait()

    @pl.when(jnp.logical_not(home))
    def _():
        out[...] = jnp.zeros_like(out)

    for slot in range(seqs):

        @pl.when(t * seqs + slot != f)
        def _():
            for n in range(len(sets)):
                for s in range(nc):
                    to_chip(n, slot, s).wait_send()

    finish_all(loads)


def collect(lay, lefts, rights, sets, stride, blocks, call_id, dims=NT, hauls=(), by_plane=False):
    seqs, count = lefts[0].shape[1:3]
    nc, wide = rights[0].shape[0], rights[0].shape[-2 if dims == NT else -1]
    rows, width = count // blocks, nc * wide
    held = len(sets) * (seqs + lay.nf) * count * width * 2
    held += sum(a.size for a in lefts) * 9 // 4 + sum(w.size for w in rights) * 2
    if held > VMEM_LIMIT:

        def block_of(terms, j, last):
            at = (lay.c - j) % nc if by_plane else j
            here = [lax.dynamic_slice_in_dim(a, at * rows, rows, 2) for a in lefts]
            if last is not None:
                here = lax.optimization_barrier((here, last))[0]
            partial = 0.0
            for which, lead, first, size, weight, row in terms:
                partial = partial + jnp.einsum(
                    "srh,pdh->srpd" if dims == NT else "srh,phd->srpd",
                    here[which][lead, :, :, first : first + size],
                    rights[weight] if row is None else rights[weight][:, row],
                    preferred_element_type=F32,
                )
            return partial.astype(BF16).reshape(seqs, rows, width)

        sums = [
            collect_permute(lay, functools.partial(block_of, terms), blocks, stride) for terms in sets
        ]
        return [jnp.stack(sums), *haul_alone(lay, hauls, call_id)]
    hauls = Hauls(lay, hauls)
    dma = pltpu.SemaphoreType.DMA
    in_vmem = pl.BlockSpec(memory_space=pltpu.VMEM)
    return pl.pallas_call(
        functools.partial(
            collect_body,
            lay.sizes,
            stride,
            blocks,
            by_plane,
            dims,
            sets,
            len(lefts),
            len(rights),
            hauls,
        ),
        out_shape=[jax.ShapeDtypeStruct((len(sets), blocks, rows, width), BF16)] + hauls.shapes,
        in_specs=[in_vmem] * (len(lefts) + len(rights)) + hauls.in_specs,
        out_specs=[in_vmem] + hauls.out_specs,
        scratch_shapes=[
            pltpu.VMEM((len(sets), seqs, nc, count, wide), BF16),
            pltpu.VMEM((len(sets), lay.nf - 1, nc, count, wide), BF16),
            dma((len(sets), seqs, nc)),
            dma((len(sets), lay.nf - 1, nc)),
            dma((len(sets), nc, blocks)),
            dma((len(sets), nc, blocks)),
        ]
        + hauls.scratch,
        compiler_params=params(call_id),
        name=f"collect{call_id}",
    )(*lefts, *rights, *hauls.operands)


def haul_alone_body(lay_sizes, hauls, *refs):
    nf, nc, nt, seqs = lay_sizes
    loads = hauls.split(refs, 0, 0)[3]
    greet(nf, nc, nt)
    start_all(loads)
    finish_all(loads)


def haul_alone(lay, hauls, call_id):
    if not hauls:
        return []
    hauls = Hauls(lay, hauls)
    return pl.pallas_call(
        functools.partial(haul_alone_body, lay.sizes, hauls),
        out_shape=hauls.shapes,
        in_specs=hauls.in_specs,
        out_specs=hauls.out_specs,
        scratch_shapes=hauls.scratch,
        compiler_params=params(call_id),
        name=f"haul{call_id}",
    )(*hauls.operands)


def finish_body(lay_sizes, hauls, *refs):
    nf, nc, nt, seqs = lay_sizes
    (terms, grad), (sums, grad_out), scratch, loads = hauls.split(refs, 2, 2)
    landed, middle, total, zsend, zrecv, psend, precv, tsend, trecv = scratch
    f, c, t = lax.axis_index("fsdp"), lax.axis_index("ctx"), lax.axis_index("tp")
    home = t == f // seqs
    barrier = pltpu.get_barrier_semaphore()
    others = [(k, u) for k in range(nf) for u in range(nt) if (k, u) != (0, 0)]
    for j in range(1, nc):
        pl.semaphore_signal(
            barrier, inc=1, device_id={"ctx": lax.rem(c + j, nc)}, device_id_type=MESH
        )
    for k, u in others:
        pl.semaphore_signal(
            barrier,
            inc=1,
            device_id={"fsdp": lax.rem(f + k, nf), "tp": lax.rem(t + u, nt)},
            device_id_type=MESH,
        )
    pl.semaphore_wait(barrier, nc - 1 + len(others))

    def along_ctx(j):
        return pltpu.make_async_remote_copy(
            src_ref=terms.at[lax.rem(c + j, nc)],
            dst_ref=middle.at[j],
            send_sem=zsend.at[j],
            recv_sem=zrecv.at[j],
            device_id={"ctx": lax.rem(c + j, nc)},
            device_id_type=MESH,
        )

    def in_plane(k, u):
        chip = lax.rem(f + k, nf)
        return pltpu.make_async_remote_copy(
            src_ref=total.at[chip],
            dst_ref=landed.at[f],
            send_sem=psend.at[k, u],
            recv_sem=precv.at[f],
            device_id={"fsdp": chip, "tp": lax.rem(t + u, nt)},
            device_id_type=MESH,
        )

    def to_core(u):
        return pltpu.make_async_remote_copy(
            src_ref=grad,
            dst_ref=grad_out,
            send_sem=tsend.at[u],
            recv_sem=trecv.at[0],
            device_id={"tp": lax.rem(t + u, nt)},
            device_id_type=MESH,
        )

    @pl.when(home)
    def _():
        for j in range(1, nc):
            along_ctx(j).start()
        for u in range(1, nt):
            to_core(u).start()

    start_all(loads)

    @pl.when(home)
    def _():
        grad_out[...] = grad[...]
        summed = terms[c]
        for j in range(1, nc):
            along_ctx(j).wait_recv()
            summed = summed + middle[j]
        total[...] = summed
        for k, u in others:
            in_plane(k, u).start()
        landed[f] = total[f]

    for chip in range(nf):

        @pl.when(jnp.logical_not(jnp.logical_and(home, f == chip)))
        def _():
            pltpu.make_async_remote_copy(
                src_ref=landed.at[chip],
                dst_ref=landed.at[chip],
                send_sem=psend.at[0, 0],
                recv_sem=precv.at[chip],
                device_id={"fsdp": lax.rem(f + 1, nf)},
                device_id_type=MESH,
            ).wait_recv()

    sums[...] = jnp.sum(landed[...], axis=0)

    @pl.when(home)
    def _():
        for j in range(1, nc):
            along_ctx(j).wait_send()
        for k, u in others:
            in_plane(k, u).wait_send()
        for u in range(1, nt):
            to_core(u).wait_send()

    @pl.when(jnp.logical_not(home))
    def _():
        to_core(1).wait_recv()

    finish_all(loads)


def finish(lay, terms, grad, call_id, hauls=()):
    lines, width = terms.shape
    part = width // (lay.nf * lay.nc)
    terms = terms.reshape(lines, lay.nf, lay.nc, part).transpose(2, 1, 0, 3)
    hauls = Hauls(lay, hauls)
    dma = pltpu.SemaphoreType.DMA
    in_vmem = pl.BlockSpec(memory_space=pltpu.VMEM)
    return pl.pallas_call(
        functools.partial(finish_body, lay.sizes, hauls),
        out_shape=[
            jax.ShapeDtypeStruct((lines, part), F32),
            jax.ShapeDtypeStruct(grad.shape, grad.dtype),
        ]
        + hauls.shapes,
        in_specs=[in_vmem] * 2 + hauls.in_specs,
        out_specs=[in_vmem] * 2 + hauls.out_specs,
        scratch_shapes=[
            pltpu.VMEM((lay.nf, lines, part), F32),
            pltpu.VMEM((lay.nc, lay.nf, lines, part), F32),
            pltpu.VMEM((lay.nf, lines, part), F32),
            dma((lay.nc,)),
            dma((lay.nc,)),
            dma((lay.nf, lay.nt)),
            dma((lay.nf,)),
            dma((lay.nt,)),
            dma((1,)),
        ]
        + hauls.scratch,
        compiler_params=params(call_id),
        name=f"finish{call_id}",
    )(terms, grad, *hauls.operands)


def turn(values, cosine, sine):
    return values * cosine + pltpu.roll(values, DH // 2, axis=1) * sine


def chunk_dot(a_ref, weights, row=None, dims=NN):
    planes, wide = weights.shape[0], weights.shape[-2 if dims == NN else -1]
    acc = None
    for s in range(planes):
        weight = weights[s] if row is None else weights[s, row]
        term = dot(a_ref[:, s * wide : (s + 1) * wide], weight, dims)
        acc = term if acc is None else acc + term
    return acc


def pick_columns(ids, expert, planes, cap):
    count = ids.shape[0]
    rows = count // lax.axis_size("ctx")
    member = jnp.where(jnp.logical_or(ids[:, 0:1] == expert, ids[:, 1:2] == expert), 1.0, 0.0)
    before = lax.broadcasted_iota(jnp.int32, (rows, rows), 1)
    before = (before < lax.broadcasted_iota(jnp.int32, (rows, rows), 0)).astype(BF16)
    places = []
    for plane in range(count // rows):
        here = member[plane * rows : (plane + 1) * rows]
        rank = dot(before, jnp.broadcast_to(here, (rows, DH)).astype(BF16))[:, 0:1]
        first = -1.0
        for n, chosen in enumerate(planes):
            first = jnp.where(chosen == plane, float(n * cap), first)
        places.append(jnp.where(jnp.logical_and(here > 0.5, first >= 0.0), rank + first, -1.0))
    place = jnp.concatenate(places, axis=0)
    columns = lax.broadcasted_iota(jnp.int32, (count, len(planes) * cap), 1).astype(F32)
    return jnp.where(place == columns, 1.0, 0.0)


def attend_body(lay_sizes, rep, hauls, *refs):
    nf, nc, nt, seqs = lay_sizes
    ins, outs, scratch, loads = hauls.split(refs, 10, 8)
    x_ref, ids_ref, small_ref, q0, q1, kv0, kv1, cos_ref, sin_ref, pos_ref = ins
    normed_ref, q_ref, k_ref, v_ref, mixed_ref, put_ref, qpos_ref, other_ref = outs
    c = lax.axis_index("ctx")
    expert = c // rep

    @pl.when(pl.program_id(0) == 0)
    def _():
        greet(nf, nc, nt, True)
        start_all(loads)

    wide = small_ref.shape[-1]
    total = 0.0
    for s in range(nc):
        x = x_ref[0, :, s * wide : (s + 1) * wide].astype(F32)
        total = total + jnp.sum(x * x, axis=-1, keepdims=True)
    inverse = lax.rsqrt(total * (1.0 / (nc * wide)) + EPSILON)
    for s in range(nc):
        columns = slice(s * wide, (s + 1) * wide)
        gain = small_ref[s, 0:1].astype(F32)
        normed_ref[0, :, columns] = (x_ref[0, :, columns].astype(F32) * inverse * gain).astype(BF16)
    normed = normed_ref.at[0]

    cap = qpos_ref.shape[-1] * rep // nc
    planes = [lax.rem(c - rep * j + nc, nc) for j in range(nc // rep)]
    ids = ids_ref[0].astype(F32)
    pick = pick_columns(ids[:, 0:2], expert.astype(F32), planes, cap)
    put_ref[0] = pick.astype(BF16)
    qpos_ref[0] = jnp.sum(pick * pos_ref[...], axis=0, keepdims=True)
    seen = pos_ref[...] <= qpos_ref[0]
    pick_m = pick_columns(ids[:, 2:4], expert.astype(F32), planes, cap).astype(BF16)
    other = jnp.where(ids[:, 2:3] == expert.astype(F32), ids[:, 3:4], ids[:, 2:3])
    other = dot(pick_m, jnp.broadcast_to(other, (other.shape[0], DH)).astype(BF16), TN)
    other_ref[0] = other[:, 0:1]

    cosine, sine = cos_ref[...], sin_ref[...]
    half = q0.shape[-1]
    for side, (query, key_value) in enumerate(((q0, kv0), (q1, kv1))):
        v_ref[0, :, side * half : (side + 1) * half] = chunk_dot(normed, key_value, 1).astype(BF16)
        keys = chunk_dot(normed, key_value, 0)
        queries = chunk_dot(normed, query)
        for h in range(half // DH):
            cols = slice(side * half + h * DH, side * half + (h + 1) * DH)
            here = slice(h * DH, (h + 1) * DH)
            k_ref[0, :, cols] = turn(keys[:, here], cosine, sine).astype(BF16)
            turned = turn(queries[:, here], cosine, sine).astype(BF16)
            q_ref[0, :, cols] = dot(put_ref[0], turned, TN).astype(BF16)
    for h in range(2 * half // DH):
        cols = slice(h * DH, (h + 1) * DH)
        scores = dot(k_ref[0, :, cols], q_ref[0, :, cols], NT) * (1.0 / math.sqrt(DH))
        scores = jnp.where(seen, scores, MASKED)
        powers = jnp.exp(scores - jnp.max(scores, axis=0, keepdims=True))
        probs = (powers / jnp.sum(powers, axis=0, keepdims=True)).astype(BF16)
        mixed_ref[0, :, cols] = dot(probs, v_ref[0, :, cols], TN).astype(BF16)

    @pl.when(pl.program_id(0) == seqs - 1)
    def _():
        finish_all(loads)


def attend(lay, x, small, weights, cosine, sine, pos, cap, call_id, hauls):
    seqs, count = x.shape[:2]
    width = lay.nc * small.shape[-1]
    heads = 2 * weights[0].shape[-1]
    picked = lay.experts * cap
    hauls = Hauls(lay, hauls)
    per_seq = lambda i: (i, 0, 0)
    once = pl.Buffered(1)
    weight_specs = [
        pl.BlockSpec(w.shape, lambda i, n=w.ndim: (0,) * n, pipeline_mode=once) for w in weights
    ]
    results = [
        ((count, width), BF16),
        ((picked, heads), BF16),
        ((count, heads), BF16),
        ((count, heads), BF16),
        ((picked, heads), BF16),
        ((count, picked), BF16),
        ((1, picked), F32),
        ((picked, 1), F32),
    ]
    return pl.pallas_call(
        functools.partial(attend_body, lay.sizes, lay.rep, hauls),
        grid=(seqs,),
        in_specs=[
            pl.BlockSpec((1, count, width), per_seq),
            pl.BlockSpec((1, count, DH), lambda i: (i, 0, width // DH)),
            pl.BlockSpec(small.shape, lambda i: (0, 0, 0)),
            *weight_specs,
            pl.BlockSpec((count, DH), lambda i: (0, 0)),
            pl.BlockSpec((count, DH), lambda i: (0, 0)),
            pl.BlockSpec((count, 1), lambda i: (0, 0)),
        ]
        + hauls.in_specs,
        out_specs=[pl.BlockSpec((1,) + dims, per_seq) for dims, _ in results] + hauls.out_specs,
        out_shape=[jax.ShapeDtypeStruct((seqs,) + dims, kind) for dims, kind in results]
        + hauls.shapes,
        scratch_shapes=hauls.scratch,
        compiler_params=params(call_id),
        name="attend",
    )(x, x, small, *weights, cosine, sine, pos, *hauls.operands)


def experts_body(rep, experts, n_ref, g_ref, small_ref, other_ref, *refs):
    weights, (ge_ref, hidden_ref, gate_ref, up_ref) = refs[:6], refs[6:]
    c = lax.axis_index("ctx")
    lanes = lax.broadcasted_iota(jnp.int32, (1, small_ref.shape[0]), 1) - (2 + experts)
    logits = dot(n_ref[0], small_ref[...], NT)
    mine = jnp.sum(jnp.where(lanes == c // rep, logits, 0.0), axis=-1, keepdims=True)
    theirs = jnp.where(lanes.astype(F32) == other_ref[0], logits, 0.0)
    theirs = jnp.sum(theirs, axis=-1, keepdims=True)
    ge_ref[0] = (jax.nn.sigmoid(mine - theirs) * g_ref[0].astype(F32)).astype(BF16)
    for side in range(2):
        gate_weight, up_weight, down_weight = weights[side::2]
        gate_pre = chunk_dot(n_ref.at[0], gate_weight, None, NT)
        up_pre = chunk_dot(n_ref.at[0], up_weight, None, NT)
        grad_hidden = chunk_dot(ge_ref.at[0], down_weight, None, NT)
        sigmoid_gate = jax.nn.sigmoid(gate_pre)
        silu_gate = gate_pre * sigmoid_gate
        hidden_ref[side, 0] = (silu_gate * up_pre).astype(BF16)
        silu_slope = sigmoid_gate + silu_gate * (1.0 - sigmoid_gate)
        gate_ref[side, 0] = (grad_hidden * up_pre * silu_slope).astype(BF16)
        up_ref[side, 0] = (grad_hidden * silu_gate).astype(BF16)


def experts_apply(lay, n2, g, small, other, *weights):
    seqs, count, width = n2.shape
    ff = weights[0].shape[-2]
    per_seq = lambda i: (i, 0, 0)
    once = pl.Buffered(1)
    wide = pl.BlockSpec((2, 1, count, ff), lambda i: (0, i, 0, 0))
    return pl.pallas_call(
        functools.partial(experts_body, lay.rep, lay.experts),
        grid=(seqs,),
        in_specs=[
            pl.BlockSpec((1, count, width), per_seq),
            pl.BlockSpec((1, count, width), per_seq),
            pl.BlockSpec(small.shape, lambda i: (0, 0)),
            pl.BlockSpec((1, count, 1), per_seq),
        ]
        + [pl.BlockSpec(w.shape, lambda i: (0, 0, 0), pipeline_mode=once) for w in weights],
        out_specs=[pl.BlockSpec((1, count, width), per_seq), wide, wide, wide],
        out_shape=[jax.ShapeDtypeStruct(n2.shape, BF16)]
        + [jax.ShapeDtypeStruct((2, seqs, count, ff), BF16)] * 3,
        compiler_params=pltpu.CompilerParams(vmem_limit_bytes=VMEM_LIMIT),
        name="experts",
    )(n2, g, small, other, *weights)


def core_exchange(refs, nt):
    away, came, send_sem, recv_sem = refs

    def copy(s):
        return pltpu.make_async_remote_copy(
            src_ref=away.at[s],
            dst_ref=came.at[s],
            send_sem=send_sem.at[s],
            recv_sem=recv_sem.at[s],
            device_id={"tp": lax.rem(lax.axis_index("tp") + 1, nt)},
            device_id_type=MESH,
        )

    return copy


def greet_core(nt):
    barrier = pltpu.get_barrier_semaphore()
    other = lax.rem(lax.axis_index("tp") + 1, nt)
    pl.semaphore_signal(barrier, inc=1, device_id={"tp": other}, device_id_type=MESH)
    pl.semaphore_wait(barrier, 1)


def mlp_grads_body(nc, nt, n_ref, ge_ref, hidden_ref, gate_ref, up_ref, *refs):
    outs, (away, came) = refs[:5], refs[5:7]
    copy = core_exchange(refs[5:], nt)
    wide = away.shape[-1]
    half = outs[1].shape[1]
    pairs = ((gate_ref, n_ref), (up_ref, n_ref), (hidden_ref, ge_ref))
    greet_core(nt)

    @pl.loop(0, nc)
    def _(s):
        columns = pl.ds(pl.multiple_of(s * wide, wide), wide)
        for i, (left, right) in enumerate(pairs):
            away[s, i] = dot(left[1], right[:, columns], TN).astype(BF16)
        copy(s).start()

    @pl.loop(0, nc)
    def _(s):
        columns = pl.ds(pl.multiple_of(s * wide, wide), wide)
        copy(s).wait_recv()
        for i, (left, right) in enumerate(pairs):
            own = dot(left[0], right[:, columns], TN)
            grad = (own + came[s, i].astype(F32)).astype(BF16)
            if i == 0:
                outs[0][s] = grad
            else:
                outs[2 * i - 1][s] = grad[:half]
                outs[2 * i][s] = grad[half:]

    @pl.loop(0, nc)
    def _(s):
        copy(s).wait_send()


def mlp_grads(lay, n2, ge, hidden, gate, up, call_id):
    width, ff, nc = n2.shape[1], hidden.shape[-1], lay.nc
    piece = (3, ff, width // nc)
    in_vmem = pl.BlockSpec(memory_space=pltpu.VMEM)
    whole = jax.ShapeDtypeStruct((nc, ff, width // nc), BF16)
    half = jax.ShapeDtypeStruct((nc, ff // 2, width // nc), BF16)
    return pl.pallas_call(
        functools.partial(mlp_grads_body, nc, lay.nt),
        in_specs=[in_vmem] * 5,
        out_specs=[in_vmem] * 5,
        out_shape=[whole] + [half] * 4,
        scratch_shapes=[
            pltpu.VMEM((nc,) + piece, BF16),
            pltpu.VMEM((nc,) + piece, BF16),
            pltpu.SemaphoreType.DMA((nc,)),
            pltpu.SemaphoreType.DMA((nc,)),
        ],
        compiler_params=params(call_id),
        name="mlp_grads",
    )(n2, ge, hidden, gate, up)


def attn_grads_body(lay_sizes, hauls, *refs):
    nf, nc, nt, seqs = lay_sizes
    (x_ref, d_ref, g_ref, mixed_ref), outs, scratch, loads = hauls.split(refs, 4, 4)
    kept, away, came = scratch[:3]
    copy = core_exchange(scratch[1:], nt)
    wide, half = away.shape[-2:]
    greet(nf, nc, nt)
    start_all(loads)

    @pl.loop(0, nc)
    def _(s):
        columns = pl.ds(pl.multiple_of(s * wide, wide), wide)
        first = dot(x_ref[:, columns], d_ref[...], TN)
        last = dot(g_ref[:, columns], mixed_ref[...], TN)
        for i in range(4):
            part, at = (first, i) if i < 3 else (last, 0)
            step = 3 if i < 3 else 1
            kept[s, i] = part[:, at * half : (at + 1) * half]
            away[s, i] = part[:, (step + at) * half : (step + at + 1) * half].astype(BF16)
        copy(s).start()

    @pl.loop(0, nc)
    def _(s):
        copy(s).wait_recv()
        for i in range(4):
            outs[i][s] = (kept[s, i] + came[s, i].astype(F32)).astype(BF16)

    @pl.loop(0, nc)
    def _(s):
        copy(s).wait_send()

    finish_all(loads)


def attn_grads(lay, x, grads, g, mixed, call_id, hauls):
    width, heads, nc = x.shape[1], mixed.shape[-1], lay.nc
    piece = (width // nc, heads // 2)
    hauls = Hauls(lay, hauls)
    in_vmem = pl.BlockSpec(memory_space=pltpu.VMEM)
    return pl.pallas_call(
        functools.partial(attn_grads_body, lay.sizes, hauls),
        in_specs=[in_vmem] * 4 + hauls.in_specs,
        out_specs=[in_vmem] * 4 + hauls.out_specs,
        out_shape=[jax.ShapeDtypeStruct((nc,) + piece, BF16)] * 4 + hauls.shapes,
        scratch_shapes=[
            pltpu.VMEM((nc, 4) + piece, F32),
            pltpu.VMEM((nc, 4) + piece, BF16),
            pltpu.VMEM((nc, 4) + piece, BF16),
            pltpu.SemaphoreType.DMA((nc,)),
            pltpu.SemaphoreType.DMA((nc,)),
        ]
        + hauls.scratch,
        compiler_params=params(call_id),
        name="attn_grads",
    )(x, grads, g, mixed, *hauls.operands)


def attend_back_body(lay_sizes, hauls, *refs):
    nf, nc, nt, seqs = lay_sizes
    ins, (out_ref,), scratch, loads = hauls.split(refs, 11, 1)
    q_ref, k_ref, v_ref, g_ref, wo0, wo1, qpos_ref, kpos_ref, cosine, sine, put = ins

    @pl.when(pl.program_id(0) == 0)
    def _():
        greet(nf, nc, nt)
        start_all(loads)

    scale = 1.0 / math.sqrt(DH)
    seen = kpos_ref[...] <= qpos_ref[0]
    half = wo0.shape[-1]
    for side, weight in enumerate((wo0, wo1)):
        grad_mixed = chunk_dot(g_ref.at[0], weight).astype(BF16)
        for h in range(half // DH):
            cols = slice(side * half + h * DH, side * half + (h + 1) * DH)
            q, k, v = q_ref[0, :, cols], k_ref[0, :, cols], v_ref[0, :, cols]
            g = grad_mixed[:, h * DH : (h + 1) * DH]
            scores = jnp.where(seen, dot(k, q, NT) * scale, MASKED)
            powers = jnp.exp(scores - jnp.max(scores, axis=0, keepdims=True))
            probs = powers / jnp.sum(powers, axis=0, keepdims=True)
            grad_probs = dot(v, g, NT)
            centre = jnp.sum(probs * grad_probs, axis=0, keepdims=True)
            grad_scores = (probs * (grad_probs - centre)).astype(BF16)

            def at(part):
                first = (3 * side + part) * half + h * DH
                return slice(first, first + DH)

            out_ref[0, :, at(2)] = dot(probs.astype(BF16), g).astype(BF16)
            dk = dot(grad_scores, q) * scale
            out_ref[0, :, at(1)] = turn(dk, cosine[...], -sine[...]).astype(BF16)
            dq = dot(grad_scores, k, TN) * scale
            high = dq.astype(BF16)
            low = (dq - high.astype(F32)).astype(BF16)
            dq = dot(put[0], high) + dot(put[0], low)
            out_ref[0, :, at(0)] = turn(dq, cosine[...], -sine[...]).astype(BF16)

    @pl.when(pl.program_id(0) == seqs - 1)
    def _():
        finish_all(loads)


def attend_back(lay, q, k, v, g, weights, qpos, kpos, cosine, sine, put, call_id, hauls):
    seqs, count, heads = q.shape
    width = g.shape[-1]
    length = k.shape[1]
    hauls = Hauls(lay, hauls)
    per_seq = lambda s: (s, 0, 0)
    once = lambda s: (0, 0)
    return pl.pallas_call(
        functools.partial(attend_back_body, lay.sizes, hauls),
        grid=(seqs,),
        in_specs=[
            pl.BlockSpec((1, count, heads), per_seq),
            pl.BlockSpec((1, length, heads), per_seq),
            pl.BlockSpec((1, length, heads), per_seq),
            pl.BlockSpec((1, count, width), per_seq),
            pl.BlockSpec(weights[0].shape, lambda s: (0, 0, 0)),
            pl.BlockSpec(weights[1].shape, lambda s: (0, 0, 0)),
            pl.BlockSpec((1, 1, count), per_seq),
            pl.BlockSpec((length, 1), once),
            pl.BlockSpec((length, DH), once),
            pl.BlockSpec((length, DH), once),
            pl.BlockSpec((1, length, count), per_seq),
        ]
        + hauls.in_specs,
        out_specs=[pl.BlockSpec((1, length, 3 * heads), per_seq)] + hauls.out_specs,
        out_shape=[jax.ShapeDtypeStruct((seqs, length, 3 * heads), BF16)] + hauls.shapes,
        scratch_shapes=hauls.scratch,
        compiler_params=params(call_id),
        name="attend_back",
    )(q, k, v, g, *weights, qpos, kpos, cosine, sine, put, *hauls.operands)


def unpack_body(gate, up_a, up_b, down_a, down_b, gate_up, down):
    half = up_a.shape[1]

    def total(ref):
        return jnp.sum(ref[...].astype(F32), axis=0)

    gate_up[0, 0] = total(gate)
    gate_up[0, 1, 0:half] = total(up_a)
    gate_up[0, 1, half:] = total(up_b)
    down[0, 0:half] = total(down_a)
    down[0, half:] = total(down_b)


def unpack(lay, *parts):
    ff, wide = parts[0].shape[1:]
    experts, rep = lay.experts, lay.rep
    return pl.pallas_call(
        unpack_body,
        grid=(experts,),
        in_specs=[pl.BlockSpec((rep,) + p.shape[1:], lambda e: (e, 0, 0)) for p in parts],
        out_specs=[
            pl.BlockSpec((1, 2, ff, wide), lambda e: (e, 0, 0, 0)),
            pl.BlockSpec((1, ff, wide), lambda e: (e, 0, 0)),
        ],
        out_shape=[
            jax.ShapeDtypeStruct((experts, 2, ff, wide), F32),
            jax.ShapeDtypeStruct((experts, ff, wide), F32),
        ],
        compiler_params=pltpu.CompilerParams(vmem_limit_bytes=VMEM_LIMIT),
        name="unpack",
    )(*parts)


def ranks_of(member):
    count = member.shape[-1]
    before = (jnp.arange(count)[:, None] < jnp.arange(count)[None, :]).astype(BF16)
    return jnp.einsum("...m,mn->...n", member.astype(BF16), before, preferred_element_type=F32)


def pick_maps(ids, expert, cap):
    member = jnp.any(ids == expert[..., None, None], axis=-1)
    rank = ranks_of(member).astype(jnp.int32)
    place = jnp.arange(cap, dtype=jnp.int32)[:, None]
    return jnp.logical_and(member[..., None, :], rank[..., None, :] == place)


def choose_maps(pick, ids, expert):
    chosen = ids.T[:, None, :] == expert[None, :, None]
    maps = jnp.logical_and(pick[None], chosen[:, :, None, :])
    slots, experts, cap, rows = maps.shape
    return maps.transpose(0, 3, 1, 2).reshape(slots, rows, experts * cap).astype(BF16)


def chosen_gates(normed, router, expert_ids, experts):
    logits = jnp.dot(normed, router, preferred_element_type=F32)
    onehot = (expert_ids[:, :, None] == jnp.arange(experts, dtype=jnp.int32)).astype(F32)
    picked = jnp.sum(onehot * logits[:, None, :], axis=-1)
    return jax.nn.softmax(picked, axis=-1), onehot


def router_back(gates, grad_gates, onehot):
    inner = gates * (grad_gates - jnp.sum(gates * grad_gates, axis=-1, keepdims=True))
    return jnp.sum(onehot * inner[:, :, None], axis=1)


def per_device(
    tokens,
    cotangent,
    attn_ids,
    mlp_ids,
    span_ids,
    attn_gain,
    attn_router,
    kv_weight,
    query_weight,
    output_weight,
    mlp_gain,
    mlp_router,
    gate_up_weight,
    down_weight,
):
    experts = query_weight.shape[0]
    lay = Layout(experts)
    nf, nc, rep, seqs = lay.nf, lay.nc, lay.rep, lay.seqs
    rows, width = tokens.shape
    cap = 3 * rows // 4
    expert = lay.c // rep

    def to_planes(array, index_of, both=False):
        index = index_of(0)
        shape = array.shape[len(index) :]
        return Haul(array, lambda ref, d: ref.at[index_of(d)] if index else ref, shape, both)

    expert_of = (expert + jnp.arange(experts)) % experts
    pick_own_m = pick_maps(jnp.broadcast_to(mlp_ids, (experts, rows, 2)), expert_of, cap)

    def dispatch(pick, values):
        return jnp.einsum(
            "jrn,nd->jrd", pick.astype(BF16), values, preferred_element_type=F32
        ).astype(BF16)

    ids = jnp.concatenate([attn_ids, mlp_ids], axis=1).astype(BF16)
    payload = jnp.concatenate([tokens, jnp.pad(ids, ((0, 0), (0, 124)))], axis=1)
    small = jnp.concatenate([attn_gain[None], mlp_gain[None], attn_router.T, mlp_router.T])
    small = jnp.pad(small, ((0, -small.shape[0] % 16), (0, 0)))
    g_own = dispatch(pick_own_m, cotangent)
    by_plane = lambda *more: lambda d: (d // rep,) + more
    x_all, small_all, g_mine, _, q_own, q_sib, kv_own, kv_sib = opening(
        lay,
        payload,
        small,
        g_own,
        1,
        [to_planes(query_weight, by_plane(), True), Relay(kv_weight)],
    )
    smalls = small_all.transpose(1, 0, 2).reshape(-1, width)
    gain_one, gain_two = smalls[0:1].astype(F32), smalls[1:2].astype(F32)
    router_one = smalls[2 : 2 + experts].T
    router_two = smalls[2 + experts : 2 + 2 * experts].T

    gate_up_turned = gate_up_weight.swapaxes(-1, -2)
    down_turned = down_weight.swapaxes(-1, -2)

    pick_own_a = pick_maps(jnp.broadcast_to(attn_ids, (experts, rows, 2)), expert_of, cap)
    choose_a = choose_maps(pick_own_a, attn_ids, expert_of)
    choose_m = choose_maps(pick_own_m, mlp_ids, expert_of)

    def by_slot(choose, values):
        flat = values.reshape(-1, values.shape[-1])
        return jnp.einsum("knr,rd->knd", choose, flat, preferred_element_type=F32)

    half_len = rows // 2
    offsets = jnp.arange(rows, dtype=jnp.int32)
    pos = jnp.where(
        offsets[None, :] < half_len,
        span_ids[:, 0:1] * half_len + offsets[None, :],
        span_ids[:, 1:2] * half_len + offsets[None, :] - half_len,
    )
    pos = pos.astype(F32).reshape(-1, 1)
    freqs = ROPE_BASE ** (-jnp.arange(DH // 2, dtype=F32) / (DH // 2))

    cosine, sine = jnp.cos(pos * freqs), jnp.sin(pos * freqs)
    cosine = jnp.concatenate([cosine, cosine], axis=-1)
    sine = jnp.concatenate([-sine, sine], axis=-1)

    inputs = tokens.astype(F32)
    inverse_one = lax.rsqrt(jnp.mean(inputs * inputs, axis=-1, keepdims=True) + EPSILON)
    scaled_one = inputs * inverse_one
    normed_one = (scaled_one * gain_one).astype(BF16)
    attn_gates, attn_hot = chosen_gates(normed_one, router_one, attn_ids, experts)

    normed_all, q, k, v, mixed, put, pos_q, other, o_own, o_sib, gate_own, gate_sib, g_blocks = attend(
        lay,
        x_all.reshape(seqs, nc * rows, -1),
        small_all,
        [q_own, q_sib, kv_own, kv_sib],
        cosine,
        sine,
        pos,
        cap,
        9,
        [
            to_planes(output_weight, by_plane(), True),
            to_planes(gate_up_turned, by_plane(0), True),
            Share(lay, g_mine),
        ],
    )
    g_blocks = g_blocks.reshape(seqs, experts * cap, width)
    heads = q.shape[-1]
    half = heads // 2
    branch_rows, up_own, up_sib = collect(
        lay,
        [mixed[None]],
        [o_own, o_sib],
        [((0, 0, 0, half, 0, None), (0, 0, half, half, 1, None))],
        rep,
        experts,
        2,
        hauls=[to_planes(gate_up_turned, by_plane(1), True)],
    )
    branch = by_slot(choose_a, branch_rows[0])
    residual = inputs + jnp.sum(attn_gates.T[:, :, None] * branch, axis=0)
    inverse_two = lax.rsqrt(jnp.mean(residual * residual, axis=-1, keepdims=True) + EPSILON)
    scaled_two = residual * inverse_two
    normed_two = (scaled_two * gain_two).astype(BF16)
    mlp_gates, mlp_hot = chosen_gates(normed_two, router_two, mlp_ids, experts)

    n2, down_own, down_sib = spread(
        lay,
        dispatch(pick_own_m, normed_two),
        rep,
        3,
        [to_planes(down_turned, by_plane(), True)],
    )
    n2 = n2.reshape(seqs, experts * cap, width)
    grad_expert, hidden, grad_gate, grad_up = experts_apply(
        lay,
        n2,
        g_blocks,
        smalls,
        other,
        gate_own,
        gate_sib,
        up_own,
        up_sib,
        down_own,
        down_sib,
    )
    ff = hidden.shape[-1]
    gate_grads, up_a, up_b, down_a, down_b = mlp_grads(
        lay,
        n2.reshape(-1, width),
        grad_expert.reshape(-1, width),
        *(a.reshape(2, -1, ff) for a in (hidden, grad_gate, grad_up)),
        4,
    )
    by_piece = lambda d: (d,)
    back_rows, gate_back = collect(
        lay,
        [hidden, grad_gate, grad_up],
        [gate_own, up_own, down_own, gate_sib, up_sib, down_sib],
        [
            tuple((0, side, 0, ff, 3 * side + 2, None) for side in range(2)),
            tuple((1 + i, side, 0, ff, 3 * side + i, None) for side in range(2) for i in range(2)),
        ],
        rep,
        experts,
        5,
        NN,
        [to_planes(gate_grads, by_piece)],
    )
    expert_rows, grad_rows = back_rows[0], back_rows[1]
    expert_out = by_slot(choose_m, expert_rows)
    layer_out = residual + jnp.sum(mlp_gates.T[:, :, None] * expert_out, axis=0)
    layer_out = layer_out.astype(BF16)
    upstream = cotangent.astype(F32)
    grad_choice_m = jnp.sum(upstream[None] * expert_out, axis=-1).T
    grad_logits_two = router_back(mlp_gates, grad_choice_m, mlp_hot)
    grad_normed_two = jnp.sum(by_slot(choose_m, grad_rows), axis=0) + jnp.dot(
        grad_logits_two, router_two.astype(F32).T, precision=HIGH
    )
    grad_scaled_two = grad_normed_two * gain_two
    grad_residual = upstream + inverse_two * (
        grad_scaled_two
        - scaled_two * jnp.mean(grad_scaled_two * scaled_two, axis=-1, keepdims=True)
    )

    gate_rows_a = jnp.zeros((experts, rows), F32)
    for slot in range(2):
        gate_rows_a = gate_rows_a + jnp.where(
            attn_ids[None, :, slot] == expert_of[:, None], attn_gates[None, :, slot], 0.0
        )
    grad_branch_own = jnp.einsum(
        "jrn,jnd->jrd",
        pick_own_a.astype(BF16),
        (gate_rows_a[:, :, None] * grad_residual[None]).astype(BF16),
        preferred_element_type=F32,
    ).astype(BF16)
    gb, up_a = spread(lay, grad_branch_own, rep, 6, [to_planes(up_a, by_piece)])
    gb = gb.reshape(seqs, experts * cap, width)
    dqkv, up_b = attend_back(
        lay,
        q,
        k,
        v,
        gb,
        [o_own, o_sib],
        pos_q,
        pos,
        cosine,
        sine,
        put,
        11,
        [to_planes(up_b, by_piece)],
    )
    q_grads, k_grads, v_grads, o_grads, down_a = attn_grads(
        lay,
        normed_all.reshape(-1, width),
        dqkv.reshape(-1, 3 * heads),
        gb.reshape(-1, width),
        mixed.reshape(-1, heads),
        10,
        [to_planes(down_a, by_piece)],
    )
    grad_one_rows, down_b, o_back = collect(
        lay,
        [dqkv[None]],
        [q_own, kv_own, q_sib, kv_sib],
        [
            tuple(
                (0, 0, (3 * s + i) * half, half, 2 * s + (i > 0), None if i == 0 else i - 1)
                for i in range(3)
                for s in range(2)
            )
        ],
        1,
        nc,
        7,
        hauls=[to_planes(down_b, by_piece), to_planes(o_grads, by_piece)],
        by_plane=True,
    )

    grad_choice_a = jnp.sum(grad_residual[None] * branch, axis=-1).T
    grad_logits_one = router_back(attn_gates, grad_choice_a, attn_hot)
    grad_normed_one = jnp.sum(grad_one_rows[0].astype(F32), axis=0) + jnp.dot(
        grad_logits_one, router_one.astype(F32).T, precision=HIGH
    )
    grad_scaled_one = grad_normed_one * gain_one
    grad_tokens = grad_residual + inverse_one * (
        grad_scaled_one
        - scaled_one * jnp.mean(grad_scaled_one * scaled_one, axis=-1, keepdims=True)
    )
    grad_tokens = grad_tokens.astype(BF16)
    terms = jnp.concatenate(
        [
            jnp.sum(grad_normed_one * scaled_one, axis=0)[None],
            jnp.sum(grad_normed_two * scaled_two, axis=0)[None],
            jnp.dot(grad_logits_one.T, normed_one.astype(F32), precision=HIGH),
            jnp.dot(grad_logits_two.T, normed_two.astype(F32), precision=HIGH),
        ]
    )
    terms = jnp.pad(terms, ((0, -terms.shape[0] % 8), (0, 0)))
    terms, both_out, q_back, k_back, v_back = finish(
        lay,
        terms,
        jnp.stack([layer_out, grad_tokens]),
        8,
        [to_planes(grads, by_piece) for grads in (q_grads, k_grads, v_grads)],
    )
    layer_out, grad_tokens = both_out[0], both_out[1]

    def by_expert(came):
        out = came.astype(F32)
        if rep > 1:
            out = jnp.sum(out.reshape((experts, rep) + out.shape[1:]), axis=1)
        return out

    grad_query_weight, grad_output_weight = by_expert(q_back), by_expert(o_back)
    grad_kv_weight = jnp.stack([jnp.sum(g.astype(F32), axis=0) for g in (k_back, v_back)])
    grad_gate_up, grad_down = unpack(lay, gate_back, up_a, up_b, down_a, down_b)
    grad_gate_up, grad_down = grad_gate_up.swapaxes(-1, -2), grad_down.swapaxes(-1, -2)
    return (
        layer_out,
        grad_tokens,
        terms[0],
        terms[2 : 2 + experts].T,
        grad_kv_weight,
        grad_query_weight,
        grad_output_weight,
        terms[1],
        terms[2 + experts : 2 + 2 * experts].T,
        grad_gate_up,
        grad_down,
    )


def solution(mesh):
    placed = (
        P(("fsdp", "ctx"), None),
        P(("fsdp", "ctx"), None),
        P(("fsdp", "ctx"), None),
        P(("fsdp", "ctx"), None),
        P(),
        P("ctx"),
        P("ctx", None),
        P(None, "ctx", ("fsdp", "tp")),
        P(None, "ctx", ("fsdp", "tp")),
        P(None, "ctx", ("fsdp", "tp")),
        P("ctx"),
        P("ctx", None),
        P(None, None, "ctx", ("fsdp", "tp")),
        P(None, "ctx", ("fsdp", "tp")),
    )
    return jax.shard_map(
        per_device,
        mesh=mesh,
        in_specs=placed,
        out_specs=(
            P(("fsdp", "ctx"), None),
            P(("fsdp", "ctx"), None),
            P(("fsdp", "ctx")),
            P(("fsdp", "ctx"), None),
            P(None, "ctx", ("fsdp", "tp")),
            P(None, "ctx", ("fsdp", "tp")),
            P(None, "ctx", ("fsdp", "tp")),
            P(("fsdp", "ctx")),
            P(("fsdp", "ctx"), None),
            P(None, None, "ctx", ("fsdp", "tp")),
            P(None, "ctx", ("fsdp", "tp")),
        ),
        check_vma=False,
    )
```

```python
import functools
import math

import jax
import jax.numpy as jnp
from jax import lax
from jax.experimental import pallas as pl
from jax.experimental.pallas import tpu as pltpu
from jax.sharding import PartitionSpec as P

DH = 128
EPSILON = 1e-06
ROPE_BASE = 10000.0
MASKED = -1e30
HIGH = lax.Precision.HIGHEST
MESH = pl.DeviceIdType.MESH
AXES = ("fsdp", "ctx", "tp")
F32 = jnp.float32
BF16 = jnp.bfloat16
VMEM_LIMIT = 60 * 1024 * 1024
NT = (((1,), (1,)), ((), ()))
NN = (((1,), (0,)), ((), ()))
TN = (((0,), (0,)), ((), ()))


def dot(a, b, dims=NN):
    return lax.dot_general(a, b, dims, preferred_element_type=F32)


class Layout:
    def __init__(self, experts):
        self.nf = lax.axis_size("fsdp")
        self.nc = lax.axis_size("ctx")
        self.nt = lax.axis_size("tp")
        self.experts = experts
        self.rep = self.nc // experts
        self.seqs = self.nf // self.nt
        self.f = lax.axis_index("fsdp")
        self.c = lax.axis_index("ctx")
        self.t = lax.axis_index("tp")
        self.home = self.t == self.f // self.seqs
        self.sizes = (self.nf, self.nc, self.nt, self.seqs)

    def flat(self, f, c, t):
        return (f * self.nc + c) * self.nt + t


def home_pairs(lay, move):
    pairs = []
    for f in range(lay.nf):
        t = f // lay.seqs
        for c in range(lay.nc):
            f2, c2 = move(f, c)
            pairs.append((lay.flat(f, c, t), lay.flat(f2, c2, t)))
    return pairs


def ctx_shift(lay, array, shift):
    return lax.ppermute(array, "ctx", [(c, (c + shift) % lay.nc) for c in range(lay.nc)])


def collect_permute(lay, block_of, blocks, stride):
    got, last = [], None
    for j in range(blocks):
        partial = block_of(j, last)
        zeros = jnp.zeros((lay.nf,) + partial.shape[1:], partial.dtype)
        full = lax.dynamic_update_slice_in_dim(zeros, partial, lay.t * lay.seqs, 0)
        last = lax.psum_scatter(full, "fsdp", scatter_dimension=0, tiled=True)[0]
        if j > 0:
            pairs = home_pairs(lay, lambda f, c: (f, (c - stride * j) % lay.nc))
            last = lax.ppermute(last, AXES, pairs)
        got.append(last)
    return jnp.stack(got)


class Haul:
    def __init__(self, array, piece=None, shape=None, both=False):
        self.array, self.piece, self.both = array, piece, both
        self.shape = array.shape if shape is None else shape

    def out_shapes(self, nc):
        dims = self.shape if self.piece is None else (nc,) + self.shape
        return [jax.ShapeDtypeStruct(dims, self.array.dtype)] * (2 if self.both else 1)

    def scratch(self, nc):
        return [pltpu.SemaphoreType.DMA((nc,))] * (4 if self.both else 2)

    def bind(self, place, src, outs, sems):
        load = Load()
        load.piece, load.both, load.place = self.piece, self.both, place
        load.src, load.outs, load.sems = src, outs, sems
        return load


def farthest_first(at, size):
    order = []
    for gap in range(size - 1, 0, -1):
        order += [(gap, at + gap < size), (size - gap, at - gap >= 0)]
    return order


def nearest_first(at, size):
    order = []
    for gap in range(1, size):
        order += [(gap, at - gap >= 0), (size - gap, at + gap < size)]
    return order


class Load:
    def along_ctx(self, j):
        nc, c, nt, t = self.place
        return pltpu.make_async_remote_copy(
            src_ref=self.piece(self.src, lax.rem(c + j, nc)),
            dst_ref=self.outs[0].at[c],
            send_sem=self.sems[0].at[j],
            recv_sem=self.sems[1].at[j],
            device_id={"ctx": lax.rem(c + j, nc)},
            device_id_type=MESH,
        )

    def landed(self, j):
        nc, c, nt, t = self.place
        here = self.outs[0].at[lax.rem(c - j + nc, nc)]
        return pltpu.make_async_remote_copy(
            src_ref=here,
            dst_ref=here,
            send_sem=self.sems[0].at[j],
            recv_sem=self.sems[1].at[j],
            device_id={"ctx": lax.rem(c + j, nc)},
            device_id_type=MESH,
        )

    def to_core(self, j):
        nc, c, nt, t = self.place
        if self.piece is None:
            src, dst, at = self.src, self.outs[0], 0
        else:
            source = lax.rem(c - j + nc, nc)
            src = self.piece(self.src, c) if j == 0 else self.outs[0].at[source]
            dst, at = self.outs[1].at[source], 2
        return pltpu.make_async_remote_copy(
            src_ref=src,
            dst_ref=dst,
            send_sem=self.sems[at].at[j],
            recv_sem=self.sems[at + 1].at[j],
            device_id={"tp": lax.rem(t + 1, nt)},
            device_id_type=MESH,
        )

    def keep(self):
        nc, c, nt, t = self.place
        return pltpu.make_async_copy(
            self.piece(self.src, c), self.outs[0].at[c], self.sems[0].at[0]
        )

    def start(self):
        if self.piece is None:
            self.to_core(0).start()
            return
        for j, there in farthest_first(self.place[1], self.place[0]):
            pl.when(there)(lambda j=j: self.along_ctx(j).start())
        self.keep().start()
        if self.both:
            self.to_core(0).start()

    def pass_on(self):
        if self.piece is None:
            return
        for j, there in nearest_first(self.place[1], self.place[0]):

            @pl.when(there)
            def _():
                self.landed(j).wait_recv()
                if self.both:
                    self.to_core(j).start()

    def finish(self):
        if self.piece is None:
            self.to_core(0).wait()
            return
        self.keep().wait()
        for j in range(self.place[0]):
            if j > 0:
                self.along_ctx(j).wait_send()
            if self.both:
                self.to_core(j).wait()


class Relay:
    both = True

    def __init__(self, array):
        self.array = array

    def out_shapes(self, nc):
        return [jax.ShapeDtypeStruct((nc,) + self.array.shape, self.array.dtype)] * 2

    def scratch(self, nc):
        return [pltpu.SemaphoreType.DMA((2, nc))] * 2 + [pltpu.SemaphoreType.DMA((nc,))] * 2

    def bind(self, place, src, outs, sems):
        load = RelayLoad()
        load.place, load.src, load.outs, load.sems = place, src, outs, sems
        return load


def relay_step(place, way, k, src, dst, send_sem, recv_sem):
    nc, c = place[:2]
    step = 1 - 2 * way
    copy = pltpu.make_async_remote_copy(
        src_ref=src,
        dst_ref=dst,
        send_sem=send_sem.at[way, k],
        recv_sem=recv_sem.at[way, k],
        device_id={"ctx": lax.rem(c + step + nc, nc)},
        device_id_type=MESH,
    )
    sent = jnp.logical_and(c - step * k >= 0, c - step * k < nc)
    sent = jnp.logical_and(sent, jnp.logical_and(c + step >= 0, c + step < nc))
    return copy, sent


def relayed(place, way, k):
    nc, c = place[:2]
    source = c - (1 - 2 * way) * k
    return lax.rem(source + nc, nc), jnp.logical_and(source >= 0, source < nc)


class RelayLoad:
    def copy(self, way, k):
        source = relayed(self.place, way, k)[0]
        src = self.src if k == 0 else self.outs[0].at[source]
        return relay_step(self.place, way, k, src, self.outs[0].at[source], *self.sems[:2])

    def arrival(self, way, k):
        source, there = relayed(self.place, way, k)
        here = self.outs[0].at[source]
        return pltpu.make_async_remote_copy(
            src_ref=here,
            dst_ref=here,
            send_sem=self.sems[0].at[way, k],
            recv_sem=self.sems[1].at[way, k - 1],
            device_id={"ctx": lax.rem(self.place[1] + 1, self.place[0])},
            device_id_type=MESH,
        ), there

    def to_core(self, source):
        nc, c, nt, t = self.place
        return pltpu.make_async_remote_copy(
            src_ref=self.outs[0].at[source],
            dst_ref=self.outs[1].at[source],
            send_sem=self.sems[2].at[source],
            recv_sem=self.sems[3].at[source],
            device_id={"tp": lax.rem(t + 1, nt)},
            device_id_type=MESH,
        )

    def own_to_core(self):
        nc, c, nt, t = self.place
        return pltpu.make_async_remote_copy(
            src_ref=self.src,
            dst_ref=self.outs[1].at[c],
            send_sem=self.sems[2].at[c],
            recv_sem=self.sems[3].at[c],
            device_id={"tp": lax.rem(t + 1, nt)},
            device_id_type=MESH,
        )

    def keep(self):
        nc, c = self.place[:2]
        return pltpu.make_async_copy(self.src, self.outs[0].at[c], self.sems[0].at[0, nc - 1])

    def start(self):
        for way in range(2):
            copy, sent = self.copy(way, 0)
            pl.when(sent)(copy.start)
        self.keep().start()
        self.own_to_core().start()

    def pass_on(self):
        nc = self.place[0]
        for k in range(1, nc):
            for way in range(2):
                arrival, there = self.arrival(way, k)
                source = relayed(self.place, way, k)[0]
                copy, sent = self.copy(way, k)

                @pl.when(there)
                def _():
                    arrival.wait_recv()
                    self.to_core(source).start()

                if k < nc - 1:
                    pl.when(sent)(copy.start)

    def finish(self):
        nc, c = self.place[:2]
        self.keep().wait()
        for k in range(nc - 1):
            for way in range(2):
                copy, sent = self.copy(way, k)
                pl.when(sent)(copy.wait_send)
        for source in range(nc):

            @pl.when(c != source)
            def _():
                self.to_core(source).wait()

        self.own_to_core().wait()


class Share:
    both = False

    def __init__(self, lay, array):
        self.lay_sizes, self.array = lay.sizes, array

    def out_shapes(self, nc):
        nt, seqs = self.lay_sizes[2:]
        n, rows, width = self.array.shape
        return [jax.ShapeDtypeStruct((seqs, n, rows, nt * width), self.array.dtype)]

    def scratch(self, nc):
        nf, _, nt, seqs = self.lay_sizes
        return [pltpu.SemaphoreType.DMA((nf,)), pltpu.SemaphoreType.DMA((seqs, nt))]

    def bind(self, place, src, outs, sems):
        load = SharedLoad()
        load.lay_sizes, load.src, load.out, load.sems = self.lay_sizes, src, outs[0], sems
        return load


class SharedLoad:
    def target(self, slot, core):
        width = self.src.shape[-1]
        return self.out.at[slot, :, :, pl.ds(pl.multiple_of(core * width, 128), width)]

    def to_chip(self, k):
        nf, _, nt, seqs = self.lay_sizes
        f, t = lax.axis_index("fsdp"), lax.axis_index("tp")
        own = lax.rem(f, seqs)
        return pltpu.make_async_remote_copy(
            src_ref=self.src,
            dst_ref=self.target(own, t),
            send_sem=self.sems[0].at[k],
            recv_sem=self.sems[1].at[own, t],
            device_id={"fsdp": lax.rem(f + k, nf), "tp": f // seqs},
            device_id_type=MESH,
        )

    def keep(self):
        f, t = lax.axis_index("fsdp"), lax.axis_index("tp")
        own = lax.rem(f, self.lay_sizes[3])
        return pltpu.make_async_copy(self.src, self.target(own, t), self.sems[0].at[0])

    def at_home(self):
        return lax.axis_index("tp") == lax.axis_index("fsdp") // self.lay_sizes[3]

    def start(self):
        for k in range(1, self.lay_sizes[0]):
            self.to_chip(k).start()
        pl.when(self.at_home())(lambda: self.keep().start())
        pl.when(jnp.logical_not(self.at_home()))(lambda: self.to_chip(0).start())

    def pass_on(self):
        pass

    def finish(self):
        nf, _, nt, seqs = self.lay_sizes
        f, t = lax.axis_index("fsdp"), lax.axis_index("tp")
        for i in range(seqs):
            for core in range(nt):
                mine = jnp.logical_and(f == t * seqs + i, t == core)

                @pl.when(jnp.logical_not(mine))
                def _():
                    pltpu.make_async_remote_copy(
                        src_ref=self.target(i, core),
                        dst_ref=self.target(i, core),
                        send_sem=self.sems[0].at[0],
                        recv_sem=self.sems[1].at[i, core],
                        device_id={"fsdp": lax.rem(f + 1, nf)},
                        device_id_type=MESH,
                    ).wait_recv()

        for k in range(1, nf):
            self.to_chip(k).wait_send()
        pl.when(self.at_home())(lambda: self.keep().wait())
        pl.when(jnp.logical_not(self.at_home()))(lambda: self.to_chip(0).wait_send())


class Hauls:
    def __init__(self, lay, hauls):
        self.nc, self.hauls = lay.nc, list(hauls)
        self.operands = [h.array for h in self.hauls]
        self.shapes = [shape for h in self.hauls for shape in h.out_shapes(lay.nc)]
        self.scratch = [sem for h in self.hauls for sem in h.scratch(lay.nc)]
        anywhere = pl.BlockSpec(memory_space=pl.ANY)
        self.in_specs = [anywhere] * len(self.operands)
        self.out_specs = [anywhere] * len(self.shapes)

    def split(self, refs, n_in, n_out):
        more_in, more_out, sems = len(self.operands), len(self.shapes), len(self.scratch)
        ins, refs = refs[:n_in], refs[n_in:]
        srcs, refs = refs[:more_in], refs[more_in:]
        outs, refs = refs[:n_out], refs[n_out:]
        dsts, refs = refs[:more_out], refs[more_out:]
        scratch = refs[: len(refs) - sems]
        refs = refs[len(refs) - sems :]
        c, t = lax.axis_index("ctx"), lax.axis_index("tp")
        place = (self.nc, c, lax.axis_size("tp"), t)
        loads = []
        for haul, src in zip(self.hauls, srcs):
            count, held = len(haul.out_shapes(self.nc)), len(haul.scratch(self.nc))
            loads.append(haul.bind(place, src, dsts[:count], refs[:held]))
            dsts, refs = dsts[count:], refs[held:]
        return ins, outs, scratch, loads


def start_all(loads):
    for load in loads:
        load.start()


def finish_all(loads):
    for load in loads:
        load.pass_on()
    for load in loads:
        load.finish()


def greet(nf, nc, nt, whole_plane=False):
    f, c, t = lax.axis_index("fsdp"), lax.axis_index("ctx"), lax.axis_index("tp")
    barrier = pltpu.get_barrier_semaphore()
    peers = [{"ctx": lax.rem(c + gap, nc)} for gap in range(1, nc)]
    for k in range(nf):
        for u in range(nt):
            if (k, u) != (0, 0) and (k == 0 or u == 0 or whole_plane):
                peers.append({"fsdp": lax.rem(f + k, nf), "tp": lax.rem(t + u, nt)})
    for peer in peers:
        pl.semaphore_signal(barrier, inc=1, device_id=peer, device_id_type=MESH)
    pl.semaphore_wait(barrier, len(peers))


def params(call_id):
    return pltpu.CompilerParams(
        collective_id=call_id, has_side_effects=True, vmem_limit_bytes=VMEM_LIMIT
    )


def opening_body(lay_sizes, experts, hauls, *refs):
    nf, nc, nt, seqs = lay_sizes
    (src, small, later), (out, smalls, mine, stage), sems, loads = hauls.split(refs, 3, 4)
    zsend, zrecv, psend, precv, ssend, srecv, lsend, lrecv, here = sems
    f, c, t = lax.axis_index("fsdp"), lax.axis_index("ctx"), lax.axis_index("tp")
    place = (nc, c, nt, t)
    own = lax.rem(f, seqs)
    home = t == f // seqs
    rows, width = stage.shape[1], mine.shape[2]
    greet(nf, nc, nt, True)

    def half(ref, core):
        return ref.at[pl.ds(pl.multiple_of(core * rows, 16), rows)]

    def relay(way, k):
        source = relayed(place, way, k)[0]
        from_ref = half(src, t) if k == 0 else stage.at[source]
        return relay_step(place, way, k, from_ref, stage.at[source], zsend, zrecv)

    def in_plane(source, k, first):
        return pltpu.make_async_remote_copy(
            src_ref=half(src, t) if first else stage.at[source],
            dst_ref=half(out.at[own, source], t),
            send_sem=psend.at[source, k],
            recv_sem=precv.at[own, source, t],
            device_id={"fsdp": lax.rem(f + k, nf), "tp": f // seqs},
            device_id_type=MESH,
        )

    def keep(source, first):
        from_ref = half(src, t) if first else stage.at[source]
        return pltpu.make_async_copy(from_ref, half(out.at[own, source], t), here.at[source])

    def share(source, first=False):
        for k in range(1, nf):
            in_plane(source, k, first).start()
        pl.when(home)(lambda: keep(source, first).start())
        pl.when(jnp.logical_not(home))(lambda: in_plane(source, 0, first).start())

    def small_along_ctx(j, source):
        return pltpu.make_async_remote_copy(
            src_ref=small,
            dst_ref=smalls.at[source],
            send_sem=ssend.at[j],
            recv_sem=srecv.at[j],
            device_id={"ctx": lax.rem(c + j, nc)},
            device_id_type=MESH,
        )

    def later_along_ctx(j):
        return pltpu.make_async_remote_copy(
            src_ref=later.at[j, :, pl.ds(pl.multiple_of(t * width, 128), width)],
            dst_ref=mine.at[j],
            send_sem=lsend.at[j],
            recv_sem=lrecv.at[j],
            device_id={"ctx": lax.rem(c + (nc // experts) * j, nc)},
            device_id_type=MESH,
        )

    def keep_later():
        src_ref = later.at[0, :, pl.ds(pl.multiple_of(t * width, 128), width)]
        return pltpu.make_async_copy(src_ref, mine.at[0], lsend.at[0])

    for way in range(2):
        copy, sent = relay(way, 0)
        pl.when(sent)(lambda: copy.start())
    for j in range(1, nc):
        small_along_ctx(j, c).start()
    keep_small = pltpu.make_async_copy(small, smalls.at[c], ssend.at[0])
    keep_small.start()
    share(c, True)
    loads[0].start()
    keep_later().start()

    for k in range(1, nc):
        for way in range(2):
            source, there = relayed(place, way, k)

            @pl.when(there)
            def _():
                pltpu.make_async_remote_copy(
                    src_ref=stage.at[source],
                    dst_ref=stage.at[source],
                    send_sem=zsend.at[way, k],
                    recv_sem=zrecv.at[way, k - 1],
                    device_id={"ctx": lax.rem(c + 1, nc)},
                    device_id_type=MESH,
                ).wait_recv()
                if k < nc - 1:
                    copy, sent = relay(way, k)
                    pl.when(sent)(lambda: copy.start())
                share(source)

    start_all(loads[1:])
    for j in range(1, experts):
        later_along_ctx(j).start()

    for i in range(seqs):
        for core in range(nt):
            mine_here = jnp.logical_and(f == t * seqs + i, t == core)

            @pl.when(jnp.logical_not(mine_here))
            def _():
                for source in range(nc):
                    landing = half(out.at[i, source], core)
                    pltpu.make_async_remote_copy(
                        src_ref=landing,
                        dst_ref=landing,
                        send_sem=psend.at[source, 0],
                        recv_sem=precv.at[i, source, core],
                        device_id={"fsdp": lax.rem(f + 1, nf)},
                        device_id_type=MESH,
                    ).wait_recv()

    for j in range(1, nc):
        small_along_ctx(j, lax.rem(c - j + nc, nc)).wait_recv()
        small_along_ctx(j, c).wait_send()
    keep_small.wait()
    keep_later().wait()
    for k in range(nc - 1):
        for way in range(2):
            copy, sent = relay(way, k)
            pl.when(sent)(lambda: copy.wait_send())
    for source in range(nc):
        for k in range(1, nf):
            in_plane(source, k, False).wait_send()
        pl.when(home)(lambda: keep(source, False).wait())
        pl.when(jnp.logical_not(home))(lambda: in_plane(source, 0, False).wait_send())
    for j in range(1, experts):
        later_along_ctx(j).wait()
    finish_all(loads)


def opening(lay, rows, small, later, call_id, hauls):
    count, width = rows.shape
    nf, nc, nt, seqs = lay.sizes
    hauls = Hauls(lay, hauls)
    experts = lay.experts
    dma = pltpu.SemaphoreType.DMA
    anywhere = pl.BlockSpec(memory_space=pl.ANY)
    shapes = [
        jax.ShapeDtypeStruct((seqs, nc, count, width), rows.dtype),
        jax.ShapeDtypeStruct((nc,) + small.shape, small.dtype),
        jax.ShapeDtypeStruct(later.shape[:2] + (later.shape[2] // nt,), later.dtype),
        jax.ShapeDtypeStruct((nc, count // nt, width), rows.dtype),
    ]
    return pl.pallas_call(
        functools.partial(opening_body, lay.sizes, experts, hauls),
        out_shape=shapes + hauls.shapes,
        in_specs=[anywhere] * 3 + hauls.in_specs,
        out_specs=[anywhere] * 4 + hauls.out_specs,
        scratch_shapes=[
            dma((2, nc)),
            dma((2, nc)),
            dma((nc, nf)),
            dma((seqs, nc, nt)),
            dma((nc,)),
            dma((nc,)),
            dma((experts,)),
            dma((experts,)),
            dma((nc,)),
        ]
        + hauls.scratch,
        compiler_params=params(call_id),
        name=f"opening{call_id}",
    )(rows, small, later, *hauls.operands)


def spread_body(lay_sizes, stride, blocks, hauls, *refs):
    nf, nc, nt, seqs = lay_sizes
    (src,), (out,), (zsend, zrecv, psend, precv, here), loads = hauls.split(refs, 1, 1)
    f, c, t = lax.axis_index("fsdp"), lax.axis_index("ctx"), lax.axis_index("tp")
    own = lax.rem(f, seqs)
    home = t == f // seqs
    greet(nf, nc, nt)

    def along_ctx(j):
        return pltpu.make_async_remote_copy(
            src_ref=src.at[j],
            dst_ref=out.at[own, j],
            send_sem=zsend.at[j],
            recv_sem=zrecv.at[j],
            device_id={"ctx": lax.rem(c + stride * j, nc)},
            device_id_type=MESH,
        )

    def in_plane(j, k):
        return pltpu.make_async_remote_copy(
            src_ref=src.at[0] if j == 0 else out.at[own, j],
            dst_ref=out.at[own, j],
            send_sem=psend.at[j, k],
            recv_sem=precv.at[own, j],
            device_id={"fsdp": lax.rem(f + k, nf)},
            device_id_type=MESH,
        )

    keep = pltpu.make_async_copy(src.at[0], out.at[own, 0], here)

    @pl.when(home)
    def _():
        for j, there in farthest_first(c // stride, blocks):
            pl.when(there)(lambda j=j: along_ctx(j).start())
        for k in range(1, nf):
            in_plane(0, k).start()
        keep.start()

    start_all(loads)

    @pl.when(home)
    def _():
        for j, there in nearest_first(c // stride, blocks):

            @pl.when(there)
            def _():
                along_ctx(j).wait_recv()
                for k in range(1, nf):
                    in_plane(j, k).start()

        keep.wait()

    for i in range(seqs):

        @pl.when(jnp.logical_not(jnp.logical_and(home, own == i)))
        def _():
            for j in range(blocks):
                pltpu.make_async_remote_copy(
                    src_ref=out.at[i, j],
                    dst_ref=out.at[i, j],
                    send_sem=psend.at[j, 0],
                    recv_sem=precv.at[i, j],
                    device_id={"fsdp": lax.rem(f + 1, nf)},
                    device_id_type=MESH,
                ).wait_recv()

    @pl.when(home)
    def _():
        for j in range(1, blocks):
            along_ctx(j).wait_send()
        for j in range(blocks):
            for k in range(1, nf):
                in_plane(j, k).wait_send()

    finish_all(loads)


def spread(lay, rows, stride, call_id, hauls=()):
    blocks = rows.shape[0]
    hauls = Hauls(lay, hauls)
    dma = pltpu.SemaphoreType.DMA
    anywhere = pl.BlockSpec(memory_space=pl.ANY)
    return pl.pallas_call(
        functools.partial(spread_body, lay.sizes, stride, blocks, hauls),
        out_shape=[jax.ShapeDtypeStruct((lay.seqs,) + rows.shape, rows.dtype)] + hauls.shapes,
        in_specs=[anywhere] + hauls.in_specs,
        out_specs=[anywhere] + hauls.out_specs,
        scratch_shapes=[
            dma((blocks,)),
            dma((blocks,)),
            dma((blocks, lay.nf)),
            dma((lay.seqs, blocks)),
            dma,
        ]
        + hauls.scratch,
        compiler_params=params(call_id),
        name=f"spread{call_id}",
    )(rows, *hauls.operands)


def collect_body(lay_sizes, stride, blocks, by_plane, dims, sets, n_a, n_w, hauls, *refs):
    nf, nc, nt, seqs = lay_sizes
    ins, outs, scratch, loads = hauls.split(refs, n_a + n_w, len(sets))
    lefts, rights = ins[:n_a], ins[n_a:]
    part, came, psend, precv, zsend, zrecv = scratch
    f, c, t = lax.axis_index("fsdp"), lax.axis_index("ctx"), lax.axis_index("tp")
    own = lax.rem(f, seqs)
    home = t == f // seqs
    greet(nf, nc, nt)
    start_all(loads)
    wide = part.shape[-1]
    rows = part.shape[-2] // blocks

    def to_chip(n, slot, s):
        chip = t * seqs + slot
        gap = lax.rem(f - chip + nf, nf) - 1
        return pltpu.make_async_remote_copy(
            src_ref=part.at[n, slot, s],
            dst_ref=came.at[n, gap, s],
            send_sem=psend.at[n, slot, s],
            recv_sem=precv.at[n, gap, s],
            device_id={"fsdp": chip},
            device_id_type=MESH,
        )

    def block(j):
        at = lax.rem(c - j + nc, nc) if by_plane else j
        return pl.ds(pl.multiple_of(at * rows, 16), rows)

    def to_owner(n, s, j):
        return pltpu.make_async_remote_copy(
            src_ref=part.at[n, own, s, block(j)],
            dst_ref=outs[n].at[j, :, pl.ds(pl.multiple_of(s * wide, wide), wide)],
            send_sem=zsend.at[n, s, j],
            recv_sem=zrecv.at[n, s, j],
            device_id={"ctx": lax.rem(c - stride * j + nc, nc)},
            device_id_type=MESH,
        )

    for n, terms in enumerate(sets):

        @pl.loop(0, seqs * nc)
        def _(i):
            s = lax.rem(i, nc)
            slot = lax.rem(own + 1 + i // nc, seqs)
            acc = None
            for which, lead, first, size, weight, row in terms:
                right = rights[weight][s] if row is None else rights[weight][s, row]
                term = dot(lefts[which][lead, slot, :, first : first + size], right, dims)
                acc = term if acc is None else acc + term
            part[n, slot, s] = acc.astype(BF16)

            @pl.when(t * seqs + slot != f)
            def _():
                to_chip(n, slot, s).start()

    for n in range(len(sets)):

        @pl.when(home)
        def _():
            @pl.loop(0, nc)
            def _(s):
                for r in range(nf - 1):
                    pltpu.make_async_remote_copy(
                        src_ref=came.at[n, r, s],
                        dst_ref=came.at[n, r, s],
                        send_sem=psend.at[n, 0, s],
                        recv_sem=precv.at[n, r, s],
                        device_id={"fsdp": lax.rem(f + 1, nf)},
                        device_id_type=MESH,
                    ).wait_recv()
                for j in reversed(range(blocks)):
                    where = block(j)
                    summed = part[n, own, s, where].astype(F32)
                    for r in range(nf - 1):
                        summed = summed + came[n, r, s, where].astype(F32)
                    if j == 0:
                        outs[n][0, :, pl.ds(pl.multiple_of(s * wide, wide), wide)] = summed.astype(BF16)
                    else:
                        part[n, own, s, where] = summed.astype(BF16)
                        to_owner(n, s, j).start()

    @pl.when(home)
    def _():
        for n in range(len(sets)):
            for s in range(nc):
                for j in range(1, blocks):
                    to_owner(n, s, j).wait()

    @pl.when(jnp.logical_not(home))
    def _():
        for out in outs:
            out[...] = jnp.zeros_like(out)

    for slot in range(seqs):

        @pl.when(t * seqs + slot != f)
        def _():
            for n in range(len(sets)):
                for s in range(nc):
                    to_chip(n, slot, s).wait_send()

    finish_all(loads)


def collect(lay, lefts, rights, sets, stride, blocks, call_id, dims=NT, hauls=(), by_plane=False):
    seqs, count = lefts[0].shape[1:3]
    nc, wide = rights[0].shape[0], rights[0].shape[-2 if dims == NT else -1]
    rows, width = count // blocks, nc * wide
    held = len(sets) * (seqs + lay.nf) * count * width * 2
    held += sum(a.size for a in lefts) * 9 // 4 + sum(w.size for w in rights) * 2
    if held > VMEM_LIMIT:

        def block_of(terms, j, last):
            at = (lay.c - j) % nc if by_plane else j
            here = [lax.dynamic_slice_in_dim(a, at * rows, rows, 2) for a in lefts]
            if last is not None:
                here = lax.optimization_barrier((here, last))[0]
            partial = 0.0
            for which, lead, first, size, weight, row in terms:
                partial = partial + jnp.einsum(
                    "srh,pdh->srpd" if dims == NT else "srh,phd->srpd",
                    here[which][lead, :, :, first : first + size],
                    rights[weight] if row is None else rights[weight][:, row],
                    preferred_element_type=F32,
                )
            return partial.astype(BF16).reshape(seqs, rows, width)

        sums = [
            collect_permute(lay, functools.partial(block_of, terms), blocks, stride) for terms in sets
        ]
        return [*sums, *haul_alone(lay, hauls, call_id)]
    hauls = Hauls(lay, hauls)
    dma = pltpu.SemaphoreType.DMA
    in_vmem = pl.BlockSpec(memory_space=pltpu.VMEM)
    return pl.pallas_call(
        functools.partial(
            collect_body,
            lay.sizes,
            stride,
            blocks,
            by_plane,
            dims,
            sets,
            len(lefts),
            len(rights),
            hauls,
        ),
        out_shape=[jax.ShapeDtypeStruct((blocks, rows, width), BF16)] * len(sets) + hauls.shapes,
        in_specs=[in_vmem] * (len(lefts) + len(rights)) + hauls.in_specs,
        out_specs=[in_vmem] * len(sets) + hauls.out_specs,
        scratch_shapes=[
            pltpu.VMEM((len(sets), seqs, nc, count, wide), BF16),
            pltpu.VMEM((len(sets), lay.nf - 1, nc, count, wide), BF16),
            dma((len(sets), seqs, nc)),
            dma((len(sets), lay.nf - 1, nc)),
            dma((len(sets), nc, blocks)),
            dma((len(sets), nc, blocks)),
        ]
        + hauls.scratch,
        compiler_params=params(call_id),
        name=f"collect{call_id}",
    )(*lefts, *rights, *hauls.operands)


def haul_alone_body(lay_sizes, hauls, *refs):
    nf, nc, nt, seqs = lay_sizes
    loads = hauls.split(refs, 0, 0)[3]
    greet(nf, nc, nt)
    start_all(loads)
    finish_all(loads)


def haul_alone(lay, hauls, call_id):
    if not hauls:
        return []
    hauls = Hauls(lay, hauls)
    return pl.pallas_call(
        functools.partial(haul_alone_body, lay.sizes, hauls),
        out_shape=hauls.shapes,
        in_specs=hauls.in_specs,
        out_specs=hauls.out_specs,
        scratch_shapes=hauls.scratch,
        compiler_params=params(call_id),
        name=f"haul{call_id}",
    )(*hauls.operands)


def finish_body(lay_sizes, hauls, *refs):
    nf, nc, nt, seqs = lay_sizes
    (terms, grad), (sums, grad_out), scratch, loads = hauls.split(refs, 2, 2)
    landed, middle, total, zsend, zrecv, psend, precv, tsend, trecv = scratch
    f, c, t = lax.axis_index("fsdp"), lax.axis_index("ctx"), lax.axis_index("tp")
    home = t == f // seqs
    barrier = pltpu.get_barrier_semaphore()
    others = [(k, u) for k in range(nf) for u in range(nt) if (k, u) != (0, 0)]
    for j in range(1, nc):
        pl.semaphore_signal(
            barrier, inc=1, device_id={"ctx": lax.rem(c + j, nc)}, device_id_type=MESH
        )
    for k, u in others:
        pl.semaphore_signal(
            barrier,
            inc=1,
            device_id={"fsdp": lax.rem(f + k, nf), "tp": lax.rem(t + u, nt)},
            device_id_type=MESH,
        )
    pl.semaphore_wait(barrier, nc - 1 + len(others))

    def along_ctx(j):
        return pltpu.make_async_remote_copy(
            src_ref=terms.at[lax.rem(c + j, nc)],
            dst_ref=middle.at[j],
            send_sem=zsend.at[j],
            recv_sem=zrecv.at[j],
            device_id={"ctx": lax.rem(c + j, nc)},
            device_id_type=MESH,
        )

    def in_plane(k, u):
        chip = lax.rem(f + k, nf)
        return pltpu.make_async_remote_copy(
            src_ref=total.at[chip],
            dst_ref=landed.at[f],
            send_sem=psend.at[k, u],
            recv_sem=precv.at[f],
            device_id={"fsdp": chip, "tp": lax.rem(t + u, nt)},
            device_id_type=MESH,
        )

    def to_core(u):
        return pltpu.make_async_remote_copy(
            src_ref=grad,
            dst_ref=grad_out,
            send_sem=tsend.at[u],
            recv_sem=trecv.at[0],
            device_id={"tp": lax.rem(t + u, nt)},
            device_id_type=MESH,
        )

    @pl.when(home)
    def _():
        for j in range(1, nc):
            along_ctx(j).start()
        for u in range(1, nt):
            to_core(u).start()

    start_all(loads)

    @pl.when(home)
    def _():
        grad_out[...] = grad[...]
        summed = terms[c]
        for j in range(1, nc):
            along_ctx(j).wait_recv()
            summed = summed + middle[j]
        total[...] = summed
        for k, u in others:
            in_plane(k, u).start()
        landed[f] = total[f]

    for chip in range(nf):

        @pl.when(jnp.logical_not(jnp.logical_and(home, f == chip)))
        def _():
            pltpu.make_async_remote_copy(
                src_ref=landed.at[chip],
                dst_ref=landed.at[chip],
                send_sem=psend.at[0, 0],
                recv_sem=precv.at[chip],
                device_id={"fsdp": lax.rem(f + 1, nf)},
                device_id_type=MESH,
            ).wait_recv()

    sums[...] = jnp.sum(landed[...], axis=0)

    @pl.when(home)
    def _():
        for j in range(1, nc):
            along_ctx(j).wait_send()
        for k, u in others:
            in_plane(k, u).wait_send()
        for u in range(1, nt):
            to_core(u).wait_send()

    @pl.when(jnp.logical_not(home))
    def _():
        to_core(1).wait_recv()

    finish_all(loads)


def finish(lay, terms, grad, call_id, hauls=()):
    lines, part = terms.shape[2:]
    hauls = Hauls(lay, hauls)
    dma = pltpu.SemaphoreType.DMA
    in_vmem = pl.BlockSpec(memory_space=pltpu.VMEM)
    return pl.pallas_call(
        functools.partial(finish_body, lay.sizes, hauls),
        out_shape=[
            jax.ShapeDtypeStruct((lines, part), F32),
            jax.ShapeDtypeStruct(grad.shape, grad.dtype),
        ]
        + hauls.shapes,
        in_specs=[in_vmem] * 2 + hauls.in_specs,
        out_specs=[in_vmem] * 2 + hauls.out_specs,
        scratch_shapes=[
            pltpu.VMEM((lay.nf, lines, part), F32),
            pltpu.VMEM((lay.nc, lay.nf, lines, part), F32),
            pltpu.VMEM((lay.nf, lines, part), F32),
            dma((lay.nc,)),
            dma((lay.nc,)),
            dma((lay.nf, lay.nt)),
            dma((lay.nf,)),
            dma((lay.nt,)),
            dma((1,)),
        ]
        + hauls.scratch,
        compiler_params=params(call_id),
        name=f"finish{call_id}",
    )(terms, grad, *hauls.operands)


def turn(values, cosine, sine):
    return values * cosine + pltpu.roll(values, DH // 2, axis=1) * sine


def chunk_dot(a_ref, weights, row=None, dims=NN):
    planes, wide = weights.shape[0], weights.shape[-2 if dims == NN else -1]
    acc = None
    for s in range(planes):
        weight = weights[s] if row is None else weights[s, row]
        term = dot(a_ref[:, s * wide : (s + 1) * wide], weight, dims)
        acc = term if acc is None else acc + term
    return acc


def pick_columns(ids, expert, planes, cap):
    count = ids.shape[0]
    rows = count // lax.axis_size("ctx")
    member = jnp.where(jnp.logical_or(ids[:, 0:1] == expert, ids[:, 1:2] == expert), 1.0, 0.0)
    before = lax.broadcasted_iota(jnp.int32, (rows, rows), 1)
    before = (before < lax.broadcasted_iota(jnp.int32, (rows, rows), 0)).astype(BF16)
    places = []
    for plane in range(count // rows):
        here = member[plane * rows : (plane + 1) * rows]
        rank = dot(before, jnp.broadcast_to(here, (rows, DH)).astype(BF16))[:, 0:1]
        first = -1.0
        for n, chosen in enumerate(planes):
            first = jnp.where(chosen == plane, float(n * cap), first)
        places.append(jnp.where(jnp.logical_and(here > 0.5, first >= 0.0), rank + first, -1.0))
    place = jnp.concatenate(places, axis=0)
    columns = lax.broadcasted_iota(jnp.int32, (count, len(planes) * cap), 1).astype(F32)
    return jnp.where(place == columns, 1.0, 0.0)


def attend_body(lay_sizes, rep, hauls, *refs):
    nf, nc, nt, seqs = lay_sizes
    ins, outs, scratch, loads = hauls.split(refs, 10, 8)
    x_ref, ids_ref, small_ref, q0, q1, kv0, kv1, cos_ref, sin_ref, pos_ref = ins
    normed_ref, q_ref, k_ref, v_ref, mixed_ref, put_ref, qpos_ref, other_ref = outs
    c = lax.axis_index("ctx")
    expert = c // rep

    @pl.when(pl.program_id(0) == 0)
    def _():
        greet(nf, nc, nt, True)
        start_all(loads)

    wide = small_ref.shape[-1]
    total = 0.0
    for s in range(nc):
        x = x_ref[0, :, s * wide : (s + 1) * wide].astype(F32)
        total = total + jnp.sum(x * x, axis=-1, keepdims=True)
    inverse = lax.rsqrt(total * (1.0 / (nc * wide)) + EPSILON)
    for s in range(nc):
        columns = slice(s * wide, (s + 1) * wide)
        gain = small_ref[s, 0:1].astype(F32)
        normed_ref[0, :, columns] = (x_ref[0, :, columns].astype(F32) * inverse * gain).astype(BF16)
    normed = normed_ref.at[0]

    cap = qpos_ref.shape[-1] * rep // nc
    planes = [lax.rem(c - rep * j + nc, nc) for j in range(nc // rep)]
    ids = ids_ref[0].astype(F32)
    pick = pick_columns(ids[:, 0:2], expert.astype(F32), planes, cap)
    put_ref[0] = pick.astype(BF16)
    qpos_ref[0] = jnp.sum(pick * pos_ref[...], axis=0, keepdims=True)
    seen = pos_ref[...] <= qpos_ref[0]
    pick_m = pick_columns(ids[:, 2:4], expert.astype(F32), planes, cap).astype(BF16)
    other = jnp.where(ids[:, 2:3] == expert.astype(F32), ids[:, 3:4], ids[:, 2:3])
    other = dot(pick_m, jnp.broadcast_to(other, (other.shape[0], DH)).astype(BF16), TN)
    other_ref[0] = other[:, 0:1]

    cosine, sine = cos_ref[...], sin_ref[...]
    half = q0.shape[-1]
    for side, (query, key_value) in enumerate(((q0, kv0), (q1, kv1))):
        v_ref[0, :, side * half : (side + 1) * half] = chunk_dot(normed, key_value, 1).astype(BF16)
        keys = chunk_dot(normed, key_value, 0)
        queries = chunk_dot(normed, query)
        for h in range(half // DH):
            cols = slice(side * half + h * DH, side * half + (h + 1) * DH)
            here = slice(h * DH, (h + 1) * DH)
            k_ref[0, :, cols] = turn(keys[:, here], cosine, sine).astype(BF16)
            turned = turn(queries[:, here], cosine, sine).astype(BF16)
            q_ref[0, :, cols] = dot(put_ref[0], turned, TN).astype(BF16)
    for h in range(2 * half // DH):
        cols = slice(h * DH, (h + 1) * DH)
        scores = dot(k_ref[0, :, cols], q_ref[0, :, cols], NT) * (1.0 / math.sqrt(DH))
        scores = jnp.where(seen, scores, MASKED)
        powers = jnp.exp(scores - jnp.max(scores, axis=0, keepdims=True))
        probs = (powers / jnp.sum(powers, axis=0, keepdims=True)).astype(BF16)
        mixed_ref[0, :, cols] = dot(probs, v_ref[0, :, cols], TN).astype(BF16)

    @pl.when(pl.program_id(0) == seqs - 1)
    def _():
        finish_all(loads)


def attend(lay, x, small, weights, cosine, sine, pos, cap, call_id, hauls):
    seqs, count = x.shape[:2]
    width = lay.nc * small.shape[-1]
    heads = 2 * weights[0].shape[-1]
    picked = lay.experts * cap
    hauls = Hauls(lay, hauls)
    per_seq = lambda i: (i, 0, 0)
    once = pl.Buffered(1)
    weight_specs = [
        pl.BlockSpec(w.shape, lambda i, n=w.ndim: (0,) * n, pipeline_mode=once) for w in weights
    ]
    results = [
        ((count, width), BF16),
        ((picked, heads), BF16),
        ((count, heads), BF16),
        ((count, heads), BF16),
        ((picked, heads), BF16),
        ((count, picked), BF16),
        ((1, picked), F32),
        ((picked, 1), F32),
    ]
    return pl.pallas_call(
        functools.partial(attend_body, lay.sizes, lay.rep, hauls),
        grid=(seqs,),
        in_specs=[
            pl.BlockSpec((1, count, width), per_seq),
            pl.BlockSpec((1, count, DH), lambda i: (i, 0, width // DH)),
            pl.BlockSpec(small.shape, lambda i: (0, 0, 0)),
            *weight_specs,
            pl.BlockSpec((count, DH), lambda i: (0, 0)),
            pl.BlockSpec((count, DH), lambda i: (0, 0)),
            pl.BlockSpec((count, 1), lambda i: (0, 0)),
        ]
        + hauls.in_specs,
        out_specs=[pl.BlockSpec((1,) + dims, per_seq) for dims, _ in results] + hauls.out_specs,
        out_shape=[jax.ShapeDtypeStruct((seqs,) + dims, kind) for dims, kind in results]
        + hauls.shapes,
        scratch_shapes=hauls.scratch,
        compiler_params=params(call_id),
        name="attend",
    )(x, x, small, *weights, cosine, sine, pos, *hauls.operands)


def experts_body(rep, experts, n_ref, g_ref, small_ref, other_ref, *refs):
    weights, (ge_ref, hidden_ref, gate_ref, up_ref) = refs[:6], refs[6:]
    c = lax.axis_index("ctx")
    lanes = lax.broadcasted_iota(jnp.int32, (1, small_ref.shape[1]), 1) - (2 + experts)
    logits = chunk_dot(n_ref.at[0], small_ref, None, NT)
    mine = jnp.sum(jnp.where(lanes == c // rep, logits, 0.0), axis=-1, keepdims=True)
    theirs = jnp.where(lanes.astype(F32) == other_ref[0], logits, 0.0)
    theirs = jnp.sum(theirs, axis=-1, keepdims=True)
    ge_ref[0] = (jax.nn.sigmoid(mine - theirs) * g_ref[0].astype(F32)).astype(BF16)
    for side in range(2):
        gate_weight, up_weight, down_weight = weights[side::2]
        gate_pre = chunk_dot(n_ref.at[0], gate_weight, None, NT)
        up_pre = chunk_dot(n_ref.at[0], up_weight, None, NT)
        grad_hidden = chunk_dot(ge_ref.at[0], down_weight, None, NT)
        sigmoid_gate = jax.nn.sigmoid(gate_pre)
        silu_gate = gate_pre * sigmoid_gate
        hidden_ref[side, 0] = (silu_gate * up_pre).astype(BF16)
        silu_slope = sigmoid_gate + silu_gate * (1.0 - sigmoid_gate)
        gate_ref[side, 0] = (grad_hidden * up_pre * silu_slope).astype(BF16)
        up_ref[side, 0] = (grad_hidden * silu_gate).astype(BF16)


def experts_apply(lay, n2, g, small, other, *weights):
    seqs, count, width = n2.shape
    ff = weights[0].shape[-2]
    per_seq = lambda i: (i, 0, 0)
    once = pl.Buffered(1)
    wide = pl.BlockSpec((2, 1, count, ff), lambda i: (0, i, 0, 0))
    return pl.pallas_call(
        functools.partial(experts_body, lay.rep, lay.experts),
        grid=(seqs,),
        in_specs=[
            pl.BlockSpec((1, count, width), per_seq),
            pl.BlockSpec((1, count, width), per_seq),
            pl.BlockSpec(small.shape, lambda i: (0, 0, 0)),
            pl.BlockSpec((1, count, 1), per_seq),
        ]
        + [pl.BlockSpec(w.shape, lambda i: (0, 0, 0), pipeline_mode=once) for w in weights],
        out_specs=[pl.BlockSpec((1, count, width), per_seq), wide, wide, wide],
        out_shape=[jax.ShapeDtypeStruct(n2.shape, BF16)]
        + [jax.ShapeDtypeStruct((2, seqs, count, ff), BF16)] * 3,
        compiler_params=pltpu.CompilerParams(vmem_limit_bytes=VMEM_LIMIT),
        name="experts",
    )(n2, g, small, other, *weights)


def core_exchange(refs, nt):
    away, came, send_sem, recv_sem = refs

    def copy(s):
        return pltpu.make_async_remote_copy(
            src_ref=away.at[s],
            dst_ref=came.at[s],
            send_sem=send_sem.at[s],
            recv_sem=recv_sem.at[s],
            device_id={"tp": lax.rem(lax.axis_index("tp") + 1, nt)},
            device_id_type=MESH,
        )

    return copy


def greet_core(nt):
    barrier = pltpu.get_barrier_semaphore()
    other = lax.rem(lax.axis_index("tp") + 1, nt)
    pl.semaphore_signal(barrier, inc=1, device_id={"tp": other}, device_id_type=MESH)
    pl.semaphore_wait(barrier, 1)


def mlp_grads_body(nc, nt, n_ref, ge_ref, hidden_ref, gate_ref, up_ref, *refs):
    outs, (away, came) = refs[:5], refs[5:7]
    copy = core_exchange(refs[5:], nt)
    wide = away.shape[-1]
    half = outs[1].shape[1]
    pairs = ((gate_ref, n_ref), (up_ref, n_ref), (hidden_ref, ge_ref))
    greet_core(nt)

    @pl.loop(0, nc)
    def _(s):
        columns = pl.ds(pl.multiple_of(s * wide, wide), wide)
        for i, (left, right) in enumerate(pairs):
            away[s, i] = dot(left[1], right[:, columns], TN).astype(BF16)
        copy(s).start()

    @pl.loop(0, nc)
    def _(s):
        columns = pl.ds(pl.multiple_of(s * wide, wide), wide)
        copy(s).wait_recv()
        for i, (left, right) in enumerate(pairs):
            own = dot(left[0], right[:, columns], TN)
            grad = (own + came[s, i].astype(F32)).astype(BF16)
            if i == 0:
                outs[0][s] = grad
            else:
                outs[2 * i - 1][s] = grad[:half]
                outs[2 * i][s] = grad[half:]

    @pl.loop(0, nc)
    def _(s):
        copy(s).wait_send()


def mlp_grads(lay, n2, ge, hidden, gate, up, call_id):
    width, ff, nc = n2.shape[1], hidden.shape[-1], lay.nc
    piece = (3, ff, width // nc)
    in_vmem = pl.BlockSpec(memory_space=pltpu.VMEM)
    whole = jax.ShapeDtypeStruct((nc, ff, width // nc), BF16)
    half = jax.ShapeDtypeStruct((nc, ff // 2, width // nc), BF16)
    return pl.pallas_call(
        functools.partial(mlp_grads_body, nc, lay.nt),
        in_specs=[in_vmem] * 5,
        out_specs=[in_vmem] * 5,
        out_shape=[whole] + [half] * 4,
        scratch_shapes=[
            pltpu.VMEM((nc,) + piece, BF16),
            pltpu.VMEM((nc,) + piece, BF16),
            pltpu.SemaphoreType.DMA((nc,)),
            pltpu.SemaphoreType.DMA((nc,)),
        ],
        compiler_params=params(call_id),
        name="mlp_grads",
    )(n2, ge, hidden, gate, up)


def attn_grads_body(lay_sizes, hauls, *refs):
    nf, nc, nt, seqs = lay_sizes
    (x_ref, d_ref, g_ref, mixed_ref), outs, scratch, loads = hauls.split(refs, 4, 2 + lay_sizes[1])
    kept, away, came = scratch[:3]
    copy = core_exchange(scratch[1:], nt)
    wide, half = away.shape[-2:]
    greet(nf, nc, nt)
    start_all(loads)

    @pl.loop(0, nc)
    def _(s):
        columns = pl.ds(pl.multiple_of(s * wide, wide), wide)
        first = dot(x_ref[:, columns], d_ref[...], TN)
        last = dot(g_ref[:, columns], mixed_ref[...], TN)
        for i in range(4):
            part, at = (first, i) if i < 3 else (last, 0)
            step = 3 if i < 3 else 1
            kept[s, i] = part[:, at * half : (at + 1) * half]
            away[s, i] = part[:, (step + at) * half : (step + at + 1) * half].astype(BF16)
        copy(s).start()

    @pl.loop(0, nc)
    def _(s):
        copy(s).wait_recv()
        outs[0][s] = (kept[s, 0] + came[s, 0].astype(F32)).astype(BF16)
        outs[1][s] = (kept[s, 3] + came[s, 3].astype(F32)).astype(BF16)

    for s, piece in enumerate(outs[2:]):
        d = lax.rem(lax.axis_index("ctx") + s, nc)
        for i in range(2):
            piece[i] = (kept[d, 1 + i] + came[d, 1 + i].astype(F32)).astype(BF16)

    @pl.loop(0, nc)
    def _(s):
        copy(s).wait_send()

    finish_all(loads)


def attn_grads(lay, x, grads, g, mixed, call_id, hauls):
    width, heads, nc = x.shape[1], mixed.shape[-1], lay.nc
    piece = (width // nc, heads // 2)
    hauls = Hauls(lay, hauls)
    in_vmem = pl.BlockSpec(memory_space=pltpu.VMEM)
    return pl.pallas_call(
        functools.partial(attn_grads_body, lay.sizes, hauls),
        in_specs=[in_vmem] * 4 + hauls.in_specs,
        out_specs=[in_vmem] * (2 + nc) + hauls.out_specs,
        out_shape=[jax.ShapeDtypeStruct((nc,) + piece, BF16)] * 2
        + [jax.ShapeDtypeStruct((2,) + piece, BF16)] * nc
        + hauls.shapes,
        scratch_shapes=[
            pltpu.VMEM((nc, 4) + piece, F32),
            pltpu.VMEM((nc, 4) + piece, BF16),
            pltpu.VMEM((nc, 4) + piece, BF16),
            pltpu.SemaphoreType.DMA((nc,)),
            pltpu.SemaphoreType.DMA((nc,)),
        ]
        + hauls.scratch,
        compiler_params=params(call_id),
        name="attn_grads",
    )(x, grads, g, mixed, *hauls.operands)


def attend_back_body(lay_sizes, hauls, *refs):
    nf, nc, nt, seqs = lay_sizes
    ins, (out_ref,), scratch, loads = hauls.split(refs, 11, 1)
    q_ref, k_ref, v_ref, g_ref, wo0, wo1, qpos_ref, kpos_ref, cosine, sine, put = ins

    @pl.when(pl.program_id(0) == 0)
    def _():
        greet(nf, nc, nt)
        start_all(loads)

    scale = 1.0 / math.sqrt(DH)
    seen = kpos_ref[...] <= qpos_ref[0]
    half = wo0.shape[-1]
    for side, weight in enumerate((wo0, wo1)):
        grad_mixed = chunk_dot(g_ref.at[0], weight).astype(BF16)
        for h in range(half // DH):
            cols = slice(side * half + h * DH, side * half + (h + 1) * DH)
            q, k, v = q_ref[0, :, cols], k_ref[0, :, cols], v_ref[0, :, cols]
            g = grad_mixed[:, h * DH : (h + 1) * DH]
            scores = jnp.where(seen, dot(k, q, NT) * scale, MASKED)
            powers = jnp.exp(scores - jnp.max(scores, axis=0, keepdims=True))
            probs = powers / jnp.sum(powers, axis=0, keepdims=True)
            grad_probs = dot(v, g, NT)
            centre = jnp.sum(probs * grad_probs, axis=0, keepdims=True)
            grad_scores = (probs * (grad_probs - centre)).astype(BF16)

            def at(part):
                first = (3 * side + part) * half + h * DH
                return slice(first, first + DH)

            out_ref[0, :, at(2)] = dot(probs.astype(BF16), g).astype(BF16)
            dk = dot(grad_scores, q) * scale
            out_ref[0, :, at(1)] = turn(dk, cosine[...], -sine[...]).astype(BF16)
            dq = dot(grad_scores, k, TN) * scale
            high = dq.astype(BF16)
            low = (dq - high.astype(F32)).astype(BF16)
            dq = dot(put[0], high) + dot(put[0], low)
            out_ref[0, :, at(0)] = turn(dq, cosine[...], -sine[...]).astype(BF16)

    @pl.when(pl.program_id(0) == seqs - 1)
    def _():
        finish_all(loads)


def attend_back(lay, q, k, v, g, weights, qpos, kpos, cosine, sine, put, call_id, hauls):
    seqs, count, heads = q.shape
    width = g.shape[-1]
    length = k.shape[1]
    hauls = Hauls(lay, hauls)
    per_seq = lambda s: (s, 0, 0)
    once = lambda s: (0, 0)
    return pl.pallas_call(
        functools.partial(attend_back_body, lay.sizes, hauls),
        grid=(seqs,),
        in_specs=[
            pl.BlockSpec((1, count, heads), per_seq),
            pl.BlockSpec((1, length, heads), per_seq),
            pl.BlockSpec((1, length, heads), per_seq),
            pl.BlockSpec((1, count, width), per_seq),
            pl.BlockSpec(weights[0].shape, lambda s: (0, 0, 0)),
            pl.BlockSpec(weights[1].shape, lambda s: (0, 0, 0)),
            pl.BlockSpec((1, 1, count), per_seq),
            pl.BlockSpec((length, 1), once),
            pl.BlockSpec((length, DH), once),
            pl.BlockSpec((length, DH), once),
            pl.BlockSpec((1, length, count), per_seq),
        ]
        + hauls.in_specs,
        out_specs=[pl.BlockSpec((1, length, 3 * heads), per_seq)] + hauls.out_specs,
        out_shape=[jax.ShapeDtypeStruct((seqs, length, 3 * heads), BF16)] + hauls.shapes,
        scratch_shapes=hauls.scratch,
        compiler_params=params(call_id),
        name="attend_back",
    )(q, k, v, g, *weights, qpos, kpos, cosine, sine, put, *hauls.operands)


def unpack_body(gate, up_a, up_b, down_a, down_b, gate_up, down):
    half = up_a.shape[1]

    def total(ref):
        return jnp.sum(ref[...].astype(F32), axis=0)

    gate_up[0, 0] = total(gate)
    gate_up[0, 1, 0:half] = total(up_a)
    gate_up[0, 1, half:] = total(up_b)
    down[0, 0:half] = total(down_a)
    down[0, half:] = total(down_b)


def unpack(lay, *parts):
    ff, wide = parts[0].shape[1:]
    experts, rep = lay.experts, lay.rep
    return pl.pallas_call(
        unpack_body,
        grid=(experts,),
        in_specs=[pl.BlockSpec((rep,) + p.shape[1:], lambda e: (e, 0, 0)) for p in parts],
        out_specs=[
            pl.BlockSpec((1, 2, ff, wide), lambda e: (e, 0, 0, 0)),
            pl.BlockSpec((1, ff, wide), lambda e: (e, 0, 0)),
        ],
        out_shape=[
            jax.ShapeDtypeStruct((experts, 2, ff, wide), F32),
            jax.ShapeDtypeStruct((experts, ff, wide), F32),
        ],
        compiler_params=pltpu.CompilerParams(vmem_limit_bytes=VMEM_LIMIT),
        name="unpack",
    )(*parts)


def row_of(small_ref, line):
    planes = [small_ref[s, line : line + 1] for s in range(small_ref.shape[0])]
    return jnp.concatenate(planes, axis=1).astype(F32)


def choices(ids, expert, experts, cap):
    rows = ids.shape[0]
    before = lax.broadcasted_iota(jnp.int32, (rows, rows), 1)
    before = (before < lax.broadcasted_iota(jnp.int32, (rows, rows), 0)).astype(BF16)
    lanes = lax.broadcasted_iota(jnp.int32, (rows, DH), 1).astype(F32)
    member = jnp.where(jnp.logical_or(ids[:, 0:1] == lanes, ids[:, 1:2] == lanes), 1.0, 0.0)
    ranks = dot(before, member.astype(BF16))
    columns = lax.broadcasted_iota(jnp.int32, (rows, experts * cap), 1).astype(F32)
    maps = []
    for slot in range(2):
        chosen = ids[:, slot : slot + 1]
        rank = jnp.sum(jnp.where(lanes == chosen, ranks, 0.0), axis=-1, keepdims=True)
        ahead = chosen - expert.astype(F32)
        ahead = jnp.where(ahead < 0.0, ahead + experts, ahead)
        maps.append(jnp.where(columns == ahead * cap + rank, 1.0, 0.0).astype(BF16))
    return maps


def slot_gates(normed, small_ref, ids, first):
    planes, lines, wide = small_ref.shape
    logits = 0.0
    for s in range(planes):
        logits = logits + dot(normed[:, s * wide : (s + 1) * wide], small_ref[s], NT)
    lanes = lax.broadcasted_iota(jnp.int32, logits.shape, 1).astype(F32)
    picked = [
        jnp.sum(jnp.where(lanes == ids[:, k : k + 1] + first, logits, 0.0), axis=-1, keepdims=True)
        for k in range(2)
    ]
    return jax.nn.sigmoid(picked[0] - picked[1]), jax.nn.sigmoid(picked[1] - picked[0])


def norm_of(values, gain):
    inverse = lax.rsqrt(jnp.mean(values * values, axis=-1, keepdims=True) + EPSILON)
    scaled = values * inverse
    return inverse, scaled, (scaled * gain).astype(BF16)


def norm_back(grad, gain, inverse, scaled):
    turned = grad * gain
    return inverse * (turned - scaled * jnp.mean(turned * scaled, axis=-1, keepdims=True))


def logits_back(gates, choice, ids, first):
    mean = gates[0] * choice[0] + gates[1] * choice[1]
    lanes = lax.broadcasted_iota(jnp.int32, (ids.shape[0], DH), 1).astype(F32)
    out = 0.0
    for k in range(2):
        inner = gates[k] * (choice[k] - mean)
        out = out + jnp.where(lanes == ids[:, k : k + 1] + first, inner, 0.0)
    return out


def exact_tn(left, right):
    total = 0.0
    for _ in range(3):
        part = left.astype(BF16)
        total = total + dot(part, right, TN)
        left = left - part.astype(F32)
    return total


def owner_forward_body(rep, experts, x_ref, ids_ref, small_ref, rows_ref, residual_ref, out_ref):
    expert = lax.axis_index("ctx") // rep
    cap = rows_ref.shape[0] // experts
    ids = ids_ref[...]
    x = x_ref[...].astype(F32)
    normed_one = norm_of(x, row_of(small_ref, 0))[2]
    gates = slot_gates(normed_one, small_ref, ids[:, 0:2], 2)
    maps = choices(ids[:, 0:2], expert, experts, cap)
    residual = x + (gates[0] * dot(maps[0], rows_ref[...]) + gates[1] * dot(maps[1], rows_ref[...]))
    residual_ref[...] = residual
    normed_two = norm_of(residual, row_of(small_ref, 1))[2]
    maps = choices(ids[:, 2:4], expert, experts, cap)
    out_ref[...] = dot(maps[0] + maps[1], normed_two, TN).astype(BF16)


def owner_middle_body(rep, experts, *refs):
    x_ref, ids_ref, small_ref, up_ref, residual_ref, branch_ref, expert_ref, grad_ref = refs[:8]
    layer_ref, grad_res_ref, out_ref, logits_ref, terms_ref = refs[8:]
    expert = lax.axis_index("ctx") // rep
    cap = branch_ref.shape[0] // experts
    ids = ids_ref[...]
    upstream, residual = up_ref[...].astype(F32), residual_ref[...]
    gain_two = row_of(small_ref, 1)
    inverse_two, scaled_two, normed_two = norm_of(residual, gain_two)
    gates = slot_gates(normed_two, small_ref, ids[:, 2:4], 2 + experts)
    maps = choices(ids[:, 2:4], expert, experts, cap)
    choice, total = [], 0.0
    for k in range(2):
        expert_out = dot(maps[k], expert_ref[...])
        choice.append(jnp.sum(upstream * expert_out, axis=-1, keepdims=True))
        total = total + gates[k] * expert_out
    layer_ref[...] = (residual + total).astype(BF16)
    logits_two = logits_back(gates, choice, ids[:, 2:4], 2 + experts)
    grad = dot(maps[0] + maps[1], grad_ref[...])
    for e in range(experts):
        line = 2 + experts + e
        grad = grad + logits_two[:, line : line + 1] * row_of(small_ref, line)
    grad_res = upstream + norm_back(grad, gain_two, inverse_two, scaled_two)
    grad_res_ref[...] = grad_res
    gain_grad = jnp.sum(grad * scaled_two, axis=0, keepdims=True)
    normed_one = norm_of(x_ref[...].astype(F32), row_of(small_ref, 0))[2]
    gates = slot_gates(normed_one, small_ref, ids[:, 0:2], 2)
    maps = choices(ids[:, 0:2], expert, experts, cap)
    choice, out = [], 0.0
    for k in range(2):
        branch = dot(maps[k], branch_ref[...])
        choice.append(jnp.sum(grad_res * branch, axis=-1, keepdims=True))
        out = out + dot(maps[k], (gates[k] * grad_res).astype(BF16), TN)
    out_ref[...] = out.astype(BF16)
    logits_one = logits_back(gates, choice, ids[:, 0:2], 2)
    logits_ref[...] = logits_one
    lines = terms_ref.shape[0]
    terms = exact_tn(logits_one, normed_one) + exact_tn(logits_two, normed_two)
    place = lax.broadcasted_iota(jnp.int32, terms_ref.shape, 0)
    terms_ref[...] = jnp.where(place == 1, gain_grad, terms[:lines])


def owner_back_body(experts, x_ref, small_ref, rows_ref, logits_ref, grad_res_ref, layer_ref, terms_ref, both_ref, out_ref):
    gain = row_of(small_ref, 0)
    inverse, scaled, _ = norm_of(x_ref[...].astype(F32), gain)
    grad = 0.0
    for j in range(rows_ref.shape[0]):
        grad = grad + rows_ref[j].astype(F32)
    for e in range(experts):
        grad = grad + logits_ref[:, 2 + e : 3 + e] * row_of(small_ref, 2 + e)
    both_ref[0] = layer_ref[...]
    both_ref[1] = (grad_res_ref[...] + norm_back(grad, gain, inverse, scaled)).astype(BF16)
    gain_grad = jnp.sum(grad * scaled, axis=0, keepdims=True)
    place = lax.broadcasted_iota(jnp.int32, terms_ref.shape, 0)
    terms = jnp.where(place == 0, gain_grad, terms_ref[...])
    planes, chips, _, part = out_ref.shape
    for plane in range(planes):
        for chip in range(chips):
            first = (chip * planes + plane) * part
            out_ref[plane, chip] = terms[:, first : first + part]


def own_kernel(body, name, results, *operands):
    in_vmem = pl.BlockSpec(memory_space=pltpu.VMEM)
    return pl.pallas_call(
        body,
        in_specs=[in_vmem] * len(operands),
        out_specs=[in_vmem] * len(results),
        out_shape=[jax.ShapeDtypeStruct(dims, kind) for dims, kind in results],
        compiler_params=pltpu.CompilerParams(vmem_limit_bytes=VMEM_LIMIT),
        name=name,
    )(*operands)


def ranks_of(member):
    count = member.shape[-1]
    before = (jnp.arange(count)[:, None] < jnp.arange(count)[None, :]).astype(BF16)
    return jnp.einsum("...m,mn->...n", member.astype(BF16), before, preferred_element_type=F32)


def pick_maps(ids, expert, cap):
    member = jnp.any(ids == expert[..., None, None], axis=-1)
    rank = ranks_of(member).astype(jnp.int32)
    place = jnp.arange(cap, dtype=jnp.int32)[:, None]
    return jnp.logical_and(member[..., None, :], rank[..., None, :] == place)


def per_device(
    tokens,
    cotangent,
    attn_ids,
    mlp_ids,
    span_ids,
    attn_gain,
    attn_router,
    kv_weight,
    query_weight,
    output_weight,
    mlp_gain,
    mlp_router,
    gate_up_weight,
    down_weight,
):
    experts = query_weight.shape[0]
    lay = Layout(experts)
    nf, nc, rep, seqs = lay.nf, lay.nc, lay.rep, lay.seqs
    rows, width = tokens.shape
    cap = 3 * rows // 4
    expert = lay.c // rep

    def to_planes(array, index_of, both=False):
        index = index_of(0)
        shape = array.shape[len(index) :]
        return Haul(array, lambda ref, d: ref.at[index_of(d)] if index else ref, shape, both)

    expert_of = (expert + jnp.arange(experts)) % experts
    pick_own_m = pick_maps(jnp.broadcast_to(mlp_ids, (experts, rows, 2)), expert_of, cap)

    def dispatch(pick, values):
        return jnp.einsum(
            "jrn,nd->jrd", pick.astype(BF16), values, preferred_element_type=F32
        ).astype(BF16)

    ids = jnp.concatenate([attn_ids, mlp_ids], axis=1).astype(BF16)
    payload = jnp.concatenate([tokens, jnp.pad(ids, ((0, 0), (0, 124)))], axis=1)
    small = jnp.concatenate([attn_gain[None], mlp_gain[None], attn_router.T, mlp_router.T])
    small = jnp.pad(small, ((0, -small.shape[0] % 16), (0, 0)))
    g_own = dispatch(pick_own_m, cotangent)
    by_plane = lambda *more: lambda d: (d // rep,) + more
    x_all, small_all, g_mine, _, q_own, q_sib, kv_own, kv_sib = opening(
        lay,
        payload,
        small,
        g_own,
        1,
        [to_planes(query_weight, by_plane(), True), Relay(kv_weight)],
    )
    gate_up_turned = gate_up_weight.swapaxes(-1, -2)
    down_turned = down_weight.swapaxes(-1, -2)

    own_ids = ids.astype(F32)

    half_len = rows // 2
    offsets = jnp.arange(rows, dtype=jnp.int32)
    pos = jnp.where(
        offsets[None, :] < half_len,
        span_ids[:, 0:1] * half_len + offsets[None, :],
        span_ids[:, 1:2] * half_len + offsets[None, :] - half_len,
    )
    pos = pos.astype(F32).reshape(-1, 1)
    freqs = ROPE_BASE ** (-jnp.arange(DH // 2, dtype=F32) / (DH // 2))

    cosine, sine = jnp.cos(pos * freqs), jnp.sin(pos * freqs)
    cosine = jnp.concatenate([cosine, cosine], axis=-1)
    sine = jnp.concatenate([-sine, sine], axis=-1)

    normed_all, q, k, v, mixed, put, pos_q, other, o_own, o_sib, gate_own, gate_sib, g_blocks = attend(
        lay,
        x_all.reshape(seqs, nc * rows, -1),
        small_all,
        [q_own, q_sib, kv_own, kv_sib],
        cosine,
        sine,
        pos,
        cap,
        9,
        [
            to_planes(output_weight, by_plane(), True),
            to_planes(gate_up_turned, by_plane(0), True),
            Share(lay, g_mine),
        ],
    )
    g_blocks = g_blocks.reshape(seqs, experts * cap, width)
    heads = q.shape[-1]
    half = heads // 2
    branch_rows, up_own, up_sib = collect(
        lay,
        [mixed[None]],
        [o_own, o_sib],
        [((0, 0, 0, half, 0, None), (0, 0, half, half, 1, None))],
        rep,
        experts,
        2,
        hauls=[to_planes(gate_up_turned, by_plane(1), True)],
    )
    branch_rows = branch_rows.reshape(-1, width)
    residual, n2_own = own_kernel(
        functools.partial(owner_forward_body, rep, experts),
        "owner_forward",
        [((rows, width), F32), ((experts * cap, width), BF16)],
        tokens,
        own_ids,
        small_all,
        branch_rows,
    )

    n2, down_own, down_sib = spread(
        lay,
        n2_own.reshape(experts, cap, width),
        rep,
        3,
        [to_planes(down_turned, by_plane(), True)],
    )
    n2 = n2.reshape(seqs, experts * cap, width)
    grad_expert, hidden, grad_gate, grad_up = experts_apply(
        lay,
        n2,
        g_blocks,
        small_all,
        other,
        gate_own,
        gate_sib,
        up_own,
        up_sib,
        down_own,
        down_sib,
    )
    ff = hidden.shape[-1]
    gate_grads, up_a, up_b, down_a, down_b = mlp_grads(
        lay,
        n2.reshape(-1, width),
        grad_expert.reshape(-1, width),
        *(a.reshape(2, -1, ff) for a in (hidden, grad_gate, grad_up)),
        4,
    )
    by_piece = lambda d: (d,)
    expert_rows, grad_rows, gate_back = collect(
        lay,
        [hidden, grad_gate, grad_up],
        [gate_own, up_own, down_own, gate_sib, up_sib, down_sib],
        [
            tuple((0, side, 0, ff, 3 * side + 2, None) for side in range(2)),
            tuple((1 + i, side, 0, ff, 3 * side + i, None) for side in range(2) for i in range(2)),
        ],
        rep,
        experts,
        5,
        NN,
        [to_planes(gate_grads, by_piece)],
    )
    lines = -(-(2 + 2 * experts) // 16) * 16
    layer_out, grad_residual, gb_own, logits_one, terms = own_kernel(
        functools.partial(owner_middle_body, rep, experts),
        "owner_middle",
        [
            ((rows, width), BF16),
            ((rows, width), F32),
            ((experts * cap, width), BF16),
            ((rows, DH), F32),
            ((lines, width), F32),
        ],
        tokens,
        own_ids,
        small_all,
        cotangent,
        residual,
        branch_rows,
        expert_rows.reshape(-1, width),
        grad_rows.reshape(-1, width),
    )

    gb, up_a = spread(lay, gb_own.reshape(experts, cap, width), rep, 6, [to_planes(up_a, by_piece)])
    gb = gb.reshape(seqs, experts * cap, width)
    dqkv, up_b = attend_back(
        lay,
        q,
        k,
        v,
        gb,
        [o_own, o_sib],
        pos_q,
        pos,
        cosine,
        sine,
        put,
        11,
        [to_planes(up_b, by_piece)],
    )
    q_grads, o_grads, *kv_pieces, down_a = attn_grads(
        lay,
        normed_all.reshape(-1, width),
        dqkv.reshape(-1, 3 * heads),
        gb.reshape(-1, width),
        mixed.reshape(-1, heads),
        10,
        [to_planes(down_a, by_piece)],
    )
    kv_back = [kv_pieces[0]] + [ctx_shift(lay, kv_pieces[s], s) for s in range(1, nc)]
    grad_one_rows, down_b, o_back, q_back = collect(
        lay,
        [dqkv[None]],
        [q_own, kv_own, q_sib, kv_sib],
        [
            tuple(
                (0, 0, (3 * s + i) * half, half, 2 * s + (i > 0), None if i == 0 else i - 1)
                for i in range(3)
                for s in range(2)
            )
        ],
        1,
        nc,
        7,
        hauls=[to_planes(grads, by_piece) for grads in (down_b, o_grads, q_grads)],
        by_plane=True,
    )

    both, terms = own_kernel(
        functools.partial(owner_back_body, experts),
        "owner_back",
        [((2, rows, width), BF16), ((nc, nf, lines, width // (nf * nc)), F32)],
        tokens,
        small_all,
        grad_one_rows,
        logits_one,
        grad_residual,
        layer_out,
        terms,
    )
    terms, both_out = finish(lay, terms, both, 8)
    layer_out, grad_tokens = both_out[0], both_out[1]

    def by_expert(came):
        out = came.astype(F32)
        if rep > 1:
            out = jnp.sum(out.reshape((experts, rep) + out.shape[1:]), axis=1)
        return out

    grad_query_weight, grad_output_weight = by_expert(q_back), by_expert(o_back)
    grad_kv_weight = functools.reduce(jnp.add, [piece.astype(F32) for piece in kv_back])
    grad_gate_up, grad_down = unpack(lay, gate_back, up_a, up_b, down_a, down_b)
    grad_gate_up, grad_down = grad_gate_up.swapaxes(-1, -2), grad_down.swapaxes(-1, -2)
    return (
        layer_out,
        grad_tokens,
        terms[0],
        terms[2 : 2 + experts].T,
        grad_kv_weight,
        grad_query_weight,
        grad_output_weight,
        terms[1],
        terms[2 + experts : 2 + 2 * experts].T,
        grad_gate_up,
        grad_down,
    )


def solution(mesh):
    placed = (
        P(("fsdp", "ctx"), None),
        P(("fsdp", "ctx"), None),
        P(("fsdp", "ctx"), None),
        P(("fsdp", "ctx"), None),
        P(),
        P("ctx"),
        P("ctx", None),
        P(None, "ctx", ("fsdp", "tp")),
        P(None, "ctx", ("fsdp", "tp")),
        P(None, "ctx", ("fsdp", "tp")),
        P("ctx"),
        P("ctx", None),
        P(None, None, "ctx", ("fsdp", "tp")),
        P(None, "ctx", ("fsdp", "tp")),
    )
    return jax.shard_map(
        per_device,
        mesh=mesh,
        in_specs=placed,
        out_specs=(
            P(("fsdp", "ctx"), None),
            P(("fsdp", "ctx"), None),
            P(("fsdp", "ctx")),
            P(("fsdp", "ctx"), None),
            P(None, "ctx", ("fsdp", "tp")),
            P(None, "ctx", ("fsdp", "tp")),
            P(None, "ctx", ("fsdp", "tp")),
            P(("fsdp", "ctx")),
            P(("fsdp", "ctx"), None),
            P(None, None, "ctx", ("fsdp", "tp")),
            P(None, "ctx", ("fsdp", "tp")),
        ),
        check_vma=False,
    )
```

```python
import functools
import math

import jax
import jax.numpy as jnp
from jax import lax
from jax.experimental import pallas as pl
from jax.experimental.pallas import tpu as pltpu
from jax.sharding import PartitionSpec as P

DH = 128
EPSILON = 1e-06
ROPE_BASE = 10000.0
MASKED = -1e30
HIGH = lax.Precision.HIGHEST
MESH = pl.DeviceIdType.MESH
AXES = ("fsdp", "ctx", "tp")
F32 = jnp.float32
BF16 = jnp.bfloat16
VMEM_LIMIT = 60 * 1024 * 1024
NT = (((1,), (1,)), ((), ()))
NN = (((1,), (0,)), ((), ()))
TN = (((0,), (0,)), ((), ()))


def dot(a, b, dims=NN):
    return lax.dot_general(a, b, dims, preferred_element_type=F32)


class Layout:
    def __init__(self, experts):
        self.nf = lax.axis_size("fsdp")
        self.nc = lax.axis_size("ctx")
        self.nt = lax.axis_size("tp")
        self.experts = experts
        self.rep = self.nc // experts
        self.seqs = self.nf // self.nt
        self.f = lax.axis_index("fsdp")
        self.c = lax.axis_index("ctx")
        self.t = lax.axis_index("tp")
        self.home = self.t == self.f // self.seqs
        self.sizes = (self.nf, self.nc, self.nt, self.seqs)

    def flat(self, f, c, t):
        return (f * self.nc + c) * self.nt + t


def home_pairs(lay, move):
    pairs = []
    for f in range(lay.nf):
        t = f // lay.seqs
        for c in range(lay.nc):
            f2, c2 = move(f, c)
            pairs.append((lay.flat(f, c, t), lay.flat(f2, c2, t)))
    return pairs


def collect_permute(lay, block_of, blocks, stride):
    got, last = [], None
    for j in range(blocks):
        partial = block_of(j, last)
        zeros = jnp.zeros((lay.nf,) + partial.shape[1:], partial.dtype)
        full = lax.dynamic_update_slice_in_dim(zeros, partial, lay.t * lay.seqs, 0)
        last = lax.psum_scatter(full, "fsdp", scatter_dimension=0, tiled=True)[0]
        if j > 0:
            pairs = home_pairs(lay, lambda f, c: (f, (c - stride * j) % lay.nc))
            last = lax.ppermute(last, AXES, pairs)
        got.append(last)
    return jnp.stack(got)


class Haul:
    def __init__(self, array, piece=None, shape=None, both=False):
        self.array, self.piece, self.both = array, piece, both
        self.shape = array.shape if shape is None else shape

    def out_shapes(self, nc):
        dims = self.shape if self.piece is None else (nc,) + self.shape
        return [jax.ShapeDtypeStruct(dims, self.array.dtype)] * (2 if self.both else 1)

    def scratch(self, nc):
        return [pltpu.SemaphoreType.DMA((nc,))] * (4 if self.both else 2)

    def bind(self, place, src, outs, sems):
        load = Load()
        load.piece, load.both, load.place = self.piece, self.both, place
        load.src, load.outs, load.sems = src, outs, sems
        return load


def by_gap(at, size, gaps):
    order = []
    for gap in dict.fromkeys(gap for gap in gaps if gap > 0):
        order += [(gap, at - gap >= 0), (size - gap, at + gap < size)]
    return order


def start_order(size):
    return [size - 1, *range(1, size - 1)]


def wait_order(size):
    return [1, size - 1, *range(2, size - 1)] if size > 1 else []


def ahead_by_gap(at, size):
    return [(size - j, there) for j, there in by_gap(at, size, start_order(size))]


class Load:
    def along_ctx(self, j):
        nc, c, nt, t = self.place
        return pltpu.make_async_remote_copy(
            src_ref=self.piece(self.src, lax.rem(c + j, nc)),
            dst_ref=self.outs[0].at[c],
            send_sem=self.sems[0].at[j],
            recv_sem=self.sems[1].at[j],
            device_id={"ctx": lax.rem(c + j, nc)},
            device_id_type=MESH,
        )

    def landed(self, j):
        nc, c, nt, t = self.place
        here = self.outs[0].at[lax.rem(c - j + nc, nc)]
        return pltpu.make_async_remote_copy(
            src_ref=here,
            dst_ref=here,
            send_sem=self.sems[0].at[j],
            recv_sem=self.sems[1].at[j],
            device_id={"ctx": lax.rem(c + j, nc)},
            device_id_type=MESH,
        )

    def to_core(self, j):
        nc, c, nt, t = self.place
        if self.piece is None:
            src, dst, at = self.src, self.outs[0], 0
        else:
            source = lax.rem(c - j + nc, nc)
            src = self.piece(self.src, c) if j == 0 else self.outs[0].at[source]
            dst, at = self.outs[1].at[source], 2
        return pltpu.make_async_remote_copy(
            src_ref=src,
            dst_ref=dst,
            send_sem=self.sems[at].at[j],
            recv_sem=self.sems[at + 1].at[j],
            device_id={"tp": lax.rem(t + 1, nt)},
            device_id_type=MESH,
        )

    def keep(self):
        nc, c, nt, t = self.place
        return pltpu.make_async_copy(
            self.piece(self.src, c), self.outs[0].at[c], self.sems[0].at[0]
        )

    def start(self):
        if self.piece is None:
            self.to_core(0).start()
            return
        for j, there in ahead_by_gap(self.place[1], self.place[0]):
            pl.when(there)(lambda j=j: self.along_ctx(j).start())
        self.keep().start()
        if self.both:
            self.to_core(0).start()

    def pass_on(self):
        if self.piece is None:
            return
        for j, there in by_gap(self.place[1], self.place[0], wait_order(self.place[0])):

            @pl.when(there)
            def _():
                self.landed(j).wait_recv()
                if self.both:
                    self.to_core(j).start()

    def finish(self):
        if self.piece is None:
            self.to_core(0).wait()
            return
        self.keep().wait()
        for j in range(self.place[0]):
            if j > 0:
                self.along_ctx(j).wait_send()
            if self.both:
                self.to_core(j).wait()


class Relay:
    both = True

    def __init__(self, array):
        self.array = array

    def out_shapes(self, nc):
        return [jax.ShapeDtypeStruct((nc,) + self.array.shape, self.array.dtype)] * 2

    def scratch(self, nc):
        return [pltpu.SemaphoreType.DMA((2, nc))] * 2 + [pltpu.SemaphoreType.DMA((nc,))] * 2

    def bind(self, place, src, outs, sems):
        load = RelayLoad()
        load.place, load.src, load.outs, load.sems = place, src, outs, sems
        return load


def relay_step(place, way, k, src, dst, send_sem, recv_sem):
    nc, c = place[:2]
    step = 1 - 2 * way
    copy = pltpu.make_async_remote_copy(
        src_ref=src,
        dst_ref=dst,
        send_sem=send_sem.at[way, k],
        recv_sem=recv_sem.at[way, k],
        device_id={"ctx": lax.rem(c + step + nc, nc)},
        device_id_type=MESH,
    )
    sent = jnp.logical_and(c - step * k >= 0, c - step * k < nc)
    sent = jnp.logical_and(sent, jnp.logical_and(c + step >= 0, c + step < nc))
    return copy, sent


def relayed(place, way, k):
    nc, c = place[:2]
    source = c - (1 - 2 * way) * k
    return lax.rem(source + nc, nc), jnp.logical_and(source >= 0, source < nc)


class RelayLoad:
    def copy(self, way, k):
        source = relayed(self.place, way, k)[0]
        src = self.src if k == 0 else self.outs[0].at[source]
        return relay_step(self.place, way, k, src, self.outs[0].at[source], *self.sems[:2])

    def arrival(self, way, k):
        source, there = relayed(self.place, way, k)
        here = self.outs[0].at[source]
        return pltpu.make_async_remote_copy(
            src_ref=here,
            dst_ref=here,
            send_sem=self.sems[0].at[way, k],
            recv_sem=self.sems[1].at[way, k - 1],
            device_id={"ctx": lax.rem(self.place[1] + 1, self.place[0])},
            device_id_type=MESH,
        ), there

    def to_core(self, source):
        nc, c, nt, t = self.place
        return pltpu.make_async_remote_copy(
            src_ref=self.outs[0].at[source],
            dst_ref=self.outs[1].at[source],
            send_sem=self.sems[2].at[source],
            recv_sem=self.sems[3].at[source],
            device_id={"tp": lax.rem(t + 1, nt)},
            device_id_type=MESH,
        )

    def own_to_core(self):
        nc, c, nt, t = self.place
        return pltpu.make_async_remote_copy(
            src_ref=self.src,
            dst_ref=self.outs[1].at[c],
            send_sem=self.sems[2].at[c],
            recv_sem=self.sems[3].at[c],
            device_id={"tp": lax.rem(t + 1, nt)},
            device_id_type=MESH,
        )

    def keep(self):
        nc, c = self.place[:2]
        return pltpu.make_async_copy(self.src, self.outs[0].at[c], self.sems[0].at[0, nc - 1])

    def start(self):
        for way in range(2):
            copy, sent = self.copy(way, 0)
            pl.when(sent)(copy.start)
        self.keep().start()
        self.own_to_core().start()

    def pass_on(self):
        nc = self.place[0]
        for k in range(1, nc):
            for way in range(2):
                arrival, there = self.arrival(way, k)
                source = relayed(self.place, way, k)[0]
                copy, sent = self.copy(way, k)

                @pl.when(there)
                def _():
                    arrival.wait_recv()
                    self.to_core(source).start()

                if k < nc - 1:
                    pl.when(sent)(copy.start)

    def finish(self):
        nc, c = self.place[:2]
        self.keep().wait()
        for k in range(nc - 1):
            for way in range(2):
                copy, sent = self.copy(way, k)
                pl.when(sent)(copy.wait_send)
        for source in range(nc):

            @pl.when(c != source)
            def _():
                self.to_core(source).wait()

        self.own_to_core().wait()


class Share:
    both = False

    def __init__(self, lay, array):
        self.lay_sizes, self.array = lay.sizes, array

    def out_shapes(self, nc):
        nt, seqs = self.lay_sizes[2:]
        n, rows, width = self.array.shape
        return [jax.ShapeDtypeStruct((seqs, n, rows, nt * width), self.array.dtype)]

    def scratch(self, nc):
        nf, _, nt, seqs = self.lay_sizes
        return [pltpu.SemaphoreType.DMA((nf,)), pltpu.SemaphoreType.DMA((seqs, nt))]

    def bind(self, place, src, outs, sems):
        load = SharedLoad()
        load.lay_sizes, load.src, load.out, load.sems = self.lay_sizes, src, outs[0], sems
        return load


class SharedLoad:
    def target(self, slot, core):
        width = self.src.shape[-1]
        return self.out.at[slot, :, :, pl.ds(pl.multiple_of(core * width, 128), width)]

    def to_chip(self, k):
        nf, _, nt, seqs = self.lay_sizes
        f, t = lax.axis_index("fsdp"), lax.axis_index("tp")
        own = lax.rem(f, seqs)
        return pltpu.make_async_remote_copy(
            src_ref=self.src,
            dst_ref=self.target(own, t),
            send_sem=self.sems[0].at[k],
            recv_sem=self.sems[1].at[own, t],
            device_id={"fsdp": lax.rem(f + k, nf), "tp": f // seqs},
            device_id_type=MESH,
        )

    def keep(self):
        f, t = lax.axis_index("fsdp"), lax.axis_index("tp")
        own = lax.rem(f, self.lay_sizes[3])
        return pltpu.make_async_copy(self.src, self.target(own, t), self.sems[0].at[0])

    def at_home(self):
        return lax.axis_index("tp") == lax.axis_index("fsdp") // self.lay_sizes[3]

    def start(self):
        for k in range(1, self.lay_sizes[0]):
            self.to_chip(k).start()
        pl.when(self.at_home())(lambda: self.keep().start())
        pl.when(jnp.logical_not(self.at_home()))(lambda: self.to_chip(0).start())

    def pass_on(self):
        pass

    def finish(self):
        nf, _, nt, seqs = self.lay_sizes
        f, t = lax.axis_index("fsdp"), lax.axis_index("tp")
        for i in range(seqs):
            for core in range(nt):
                mine = jnp.logical_and(f == t * seqs + i, t == core)

                @pl.when(jnp.logical_not(mine))
                def _():
                    pltpu.make_async_remote_copy(
                        src_ref=self.target(i, core),
                        dst_ref=self.target(i, core),
                        send_sem=self.sems[0].at[0],
                        recv_sem=self.sems[1].at[i, core],
                        device_id={"fsdp": lax.rem(f + 1, nf)},
                        device_id_type=MESH,
                    ).wait_recv()

        for k in range(1, nf):
            self.to_chip(k).wait_send()
        pl.when(self.at_home())(lambda: self.keep().wait())
        pl.when(jnp.logical_not(self.at_home()))(lambda: self.to_chip(0).wait_send())


class Hauls:
    def __init__(self, lay, hauls):
        self.nc, self.hauls = lay.nc, list(hauls)
        self.operands = [h.array for h in self.hauls]
        self.shapes = [shape for h in self.hauls for shape in h.out_shapes(lay.nc)]
        self.scratch = [sem for h in self.hauls for sem in h.scratch(lay.nc)]
        anywhere = pl.BlockSpec(memory_space=pl.ANY)
        self.in_specs = [anywhere] * len(self.operands)
        self.out_specs = [anywhere] * len(self.shapes)

    def split(self, refs, n_in, n_out):
        more_in, more_out, sems = len(self.operands), len(self.shapes), len(self.scratch)
        ins, refs = refs[:n_in], refs[n_in:]
        srcs, refs = refs[:more_in], refs[more_in:]
        outs, refs = refs[:n_out], refs[n_out:]
        dsts, refs = refs[:more_out], refs[more_out:]
        scratch = refs[: len(refs) - sems]
        refs = refs[len(refs) - sems :]
        c, t = lax.axis_index("ctx"), lax.axis_index("tp")
        place = (self.nc, c, lax.axis_size("tp"), t)
        loads = []
        for haul, src in zip(self.hauls, srcs):
            count, held = len(haul.out_shapes(self.nc)), len(haul.scratch(self.nc))
            loads.append(haul.bind(place, src, dsts[:count], refs[:held]))
            dsts, refs = dsts[count:], refs[held:]
        return ins, outs, scratch, loads


def start_all(loads):
    for load in loads:
        load.start()


def finish_all(loads):
    for load in loads:
        load.pass_on()
    for load in loads:
        load.finish()


def greet(nf, nc, nt, whole_plane=False):
    f, c, t = lax.axis_index("fsdp"), lax.axis_index("ctx"), lax.axis_index("tp")
    barrier = pltpu.get_barrier_semaphore()
    peers = [{"ctx": lax.rem(c + gap, nc)} for gap in range(1, nc)]
    for k in range(nf):
        for u in range(nt):
            if (k, u) != (0, 0) and (k == 0 or u == 0 or whole_plane):
                peers.append({"fsdp": lax.rem(f + k, nf), "tp": lax.rem(t + u, nt)})
    for peer in peers:
        pl.semaphore_signal(barrier, inc=1, device_id=peer, device_id_type=MESH)
    pl.semaphore_wait(barrier, len(peers))


def params(call_id):
    return pltpu.CompilerParams(
        collective_id=call_id, has_side_effects=True, vmem_limit_bytes=VMEM_LIMIT
    )


def opening_body(lay_sizes, experts, hauls, *refs):
    nf, nc, nt, seqs = lay_sizes
    (src, small, later), (out, smalls, mine, stage), sems, loads = hauls.split(refs, 3, 4)
    zsend, zrecv, psend, precv, ssend, srecv, lsend, lrecv, here = sems
    f, c, t = lax.axis_index("fsdp"), lax.axis_index("ctx"), lax.axis_index("tp")
    place = (nc, c, nt, t)
    own = lax.rem(f, seqs)
    home = t == f // seqs
    rows, width = stage.shape[1], mine.shape[2]
    greet(nf, nc, nt, True)

    def half(ref, core):
        return ref.at[pl.ds(pl.multiple_of(core * rows, 16), rows)]

    def relay(way, k):
        source = relayed(place, way, k)[0]
        from_ref = half(src, t) if k == 0 else stage.at[source]
        return relay_step(place, way, k, from_ref, stage.at[source], zsend, zrecv)

    def in_plane(source, k, first):
        return pltpu.make_async_remote_copy(
            src_ref=half(src, t) if first else stage.at[source],
            dst_ref=half(out.at[own, source], t),
            send_sem=psend.at[source, k],
            recv_sem=precv.at[own, source, t],
            device_id={"fsdp": lax.rem(f + k, nf), "tp": f // seqs},
            device_id_type=MESH,
        )

    def keep(source, first):
        from_ref = half(src, t) if first else stage.at[source]
        return pltpu.make_async_copy(from_ref, half(out.at[own, source], t), here.at[source])

    def share(source, first=False):
        for k in range(1, nf):
            in_plane(source, k, first).start()
        pl.when(home)(lambda: keep(source, first).start())
        pl.when(jnp.logical_not(home))(lambda: in_plane(source, 0, first).start())

    def small_along_ctx(j, source):
        return pltpu.make_async_remote_copy(
            src_ref=small,
            dst_ref=smalls.at[source],
            send_sem=ssend.at[j],
            recv_sem=srecv.at[j],
            device_id={"ctx": lax.rem(c + j, nc)},
            device_id_type=MESH,
        )

    def later_along_ctx(j):
        return pltpu.make_async_remote_copy(
            src_ref=later.at[j, :, pl.ds(pl.multiple_of(t * width, 128), width)],
            dst_ref=mine.at[j],
            send_sem=lsend.at[j],
            recv_sem=lrecv.at[j],
            device_id={"ctx": lax.rem(c + (nc // experts) * j, nc)},
            device_id_type=MESH,
        )

    def keep_later():
        src_ref = later.at[0, :, pl.ds(pl.multiple_of(t * width, 128), width)]
        return pltpu.make_async_copy(src_ref, mine.at[0], lsend.at[0])

    for way in range(2):
        copy, sent = relay(way, 0)
        pl.when(sent)(lambda: copy.start())
    for j in range(1, nc):
        small_along_ctx(j, c).start()
    keep_small = pltpu.make_async_copy(small, smalls.at[c], ssend.at[0])
    keep_small.start()
    share(c, True)
    loads[0].start()
    keep_later().start()

    for k in range(1, nc):
        for way in range(2):
            source, there = relayed(place, way, k)

            @pl.when(there)
            def _():
                pltpu.make_async_remote_copy(
                    src_ref=stage.at[source],
                    dst_ref=stage.at[source],
                    send_sem=zsend.at[way, k],
                    recv_sem=zrecv.at[way, k - 1],
                    device_id={"ctx": lax.rem(c + 1, nc)},
                    device_id_type=MESH,
                ).wait_recv()
                if k < nc - 1:
                    copy, sent = relay(way, k)
                    pl.when(sent)(lambda: copy.start())
                share(source)

    start_all(loads[1:])
    for j in range(1, experts):
        later_along_ctx(j).start()

    for i in range(seqs):
        for core in range(nt):
            mine_here = jnp.logical_and(f == t * seqs + i, t == core)

            @pl.when(jnp.logical_not(mine_here))
            def _():
                for source in range(nc):
                    landing = half(out.at[i, source], core)
                    pltpu.make_async_remote_copy(
                        src_ref=landing,
                        dst_ref=landing,
                        send_sem=psend.at[source, 0],
                        recv_sem=precv.at[i, source, core],
                        device_id={"fsdp": lax.rem(f + 1, nf)},
                        device_id_type=MESH,
                    ).wait_recv()

    for j in range(1, nc):
        small_along_ctx(j, lax.rem(c - j + nc, nc)).wait_recv()
        small_along_ctx(j, c).wait_send()
    keep_small.wait()
    keep_later().wait()
    for k in range(nc - 1):
        for way in range(2):
            copy, sent = relay(way, k)
            pl.when(sent)(lambda: copy.wait_send())
    for source in range(nc):
        for k in range(1, nf):
            in_plane(source, k, False).wait_send()
        pl.when(home)(lambda: keep(source, False).wait())
        pl.when(jnp.logical_not(home))(lambda: in_plane(source, 0, False).wait_send())
    for j in range(1, experts):
        later_along_ctx(j).wait()
    finish_all(loads)


def opening(lay, rows, small, later, call_id, hauls):
    count, width = rows.shape
    nf, nc, nt, seqs = lay.sizes
    hauls = Hauls(lay, hauls)
    experts = lay.experts
    dma = pltpu.SemaphoreType.DMA
    anywhere = pl.BlockSpec(memory_space=pl.ANY)
    shapes = [
        jax.ShapeDtypeStruct((seqs, nc, count, width), rows.dtype),
        jax.ShapeDtypeStruct((nc,) + small.shape, small.dtype),
        jax.ShapeDtypeStruct(later.shape[:2] + (later.shape[2] // nt,), later.dtype),
        jax.ShapeDtypeStruct((nc, count // nt, width), rows.dtype),
    ]
    return pl.pallas_call(
        functools.partial(opening_body, lay.sizes, experts, hauls),
        out_shape=shapes + hauls.shapes,
        in_specs=[anywhere] * 3 + hauls.in_specs,
        out_specs=[anywhere] * 4 + hauls.out_specs,
        scratch_shapes=[
            dma((2, nc)),
            dma((2, nc)),
            dma((nc, nf)),
            dma((seqs, nc, nt)),
            dma((nc,)),
            dma((nc,)),
            dma((experts,)),
            dma((experts,)),
            dma((nc,)),
        ]
        + hauls.scratch,
        compiler_params=params(call_id),
        name=f"opening{call_id}",
    )(rows, small, later, *hauls.operands)


def spread_body(lay_sizes, stride, blocks, hauls, *refs):
    nf, nc, nt, seqs = lay_sizes
    (src,), (out,), (zsend, zrecv, psend, precv, here), loads = hauls.split(refs, 1, 1)
    f, c, t = lax.axis_index("fsdp"), lax.axis_index("ctx"), lax.axis_index("tp")
    own = lax.rem(f, seqs)
    home = t == f // seqs
    greet(nf, nc, nt)

    def along_ctx(j):
        return pltpu.make_async_remote_copy(
            src_ref=src.at[j],
            dst_ref=out.at[own, j],
            send_sem=zsend.at[j],
            recv_sem=zrecv.at[j],
            device_id={"ctx": lax.rem(c + stride * j, nc)},
            device_id_type=MESH,
        )

    def in_plane(j, k):
        return pltpu.make_async_remote_copy(
            src_ref=src.at[0] if j == 0 else out.at[own, j],
            dst_ref=out.at[own, j],
            send_sem=psend.at[j, k],
            recv_sem=precv.at[own, j],
            device_id={"fsdp": lax.rem(f + k, nf)},
            device_id_type=MESH,
        )

    keep = pltpu.make_async_copy(src.at[0], out.at[own, 0], here)

    @pl.when(home)
    def _():
        for j, there in ahead_by_gap(c // stride, blocks):
            pl.when(there)(lambda j=j: along_ctx(j).start())
        for k in range(1, nf):
            in_plane(0, k).start()
        keep.start()

    @pl.when(jnp.logical_not(home))
    def _():
        start_all(loads)

    @pl.when(home)
    def _():
        for j, there in by_gap(c // stride, blocks, wait_order(blocks)):

            @pl.when(there)
            def _():
                along_ctx(j).wait_recv()
                for k in range(1, nf):
                    in_plane(j, k).start()

        start_all(loads)
        keep.wait()

    for i in range(seqs):

        @pl.when(jnp.logical_not(jnp.logical_and(home, own == i)))
        def _():
            for j in range(blocks):
                pltpu.make_async_remote_copy(
                    src_ref=out.at[i, j],
                    dst_ref=out.at[i, j],
                    send_sem=psend.at[j, 0],
                    recv_sem=precv.at[i, j],
                    device_id={"fsdp": lax.rem(f + 1, nf)},
                    device_id_type=MESH,
                ).wait_recv()

    @pl.when(home)
    def _():
        for j in range(1, blocks):
            along_ctx(j).wait_send()
        for j in range(blocks):
            for k in range(1, nf):
                in_plane(j, k).wait_send()

    finish_all(loads)


def spread(lay, rows, stride, call_id, hauls=()):
    blocks = rows.shape[0]
    hauls = Hauls(lay, hauls)
    dma = pltpu.SemaphoreType.DMA
    anywhere = pl.BlockSpec(memory_space=pl.ANY)
    return pl.pallas_call(
        functools.partial(spread_body, lay.sizes, stride, blocks, hauls),
        out_shape=[jax.ShapeDtypeStruct((lay.seqs,) + rows.shape, rows.dtype)] + hauls.shapes,
        in_specs=[anywhere] + hauls.in_specs,
        out_specs=[anywhere] + hauls.out_specs,
        scratch_shapes=[
            dma((blocks,)),
            dma((blocks,)),
            dma((blocks, lay.nf)),
            dma((lay.seqs, blocks)),
            dma,
        ]
        + hauls.scratch,
        compiler_params=params(call_id),
        name=f"spread{call_id}",
    )(rows, *hauls.operands)


def collect_body(lay_sizes, stride, blocks, by_plane, dims, sets, n_a, n_w, hauls, *refs):
    nf, nc, nt, seqs = lay_sizes
    ins, outs, scratch, loads = hauls.split(refs, n_a + n_w, len(sets))
    lefts, rights = ins[:n_a], ins[n_a:]
    part, came, psend, precv, zsend, zrecv = scratch
    f, c, t = lax.axis_index("fsdp"), lax.axis_index("ctx"), lax.axis_index("tp")
    own = lax.rem(f, seqs)
    home = t == f // seqs
    greet(nf, nc, nt)
    start_all(loads)
    wide = part.shape[-1]
    rows = part.shape[-2] // blocks

    def to_chip(n, slot, s):
        chip = t * seqs + slot
        gap = lax.rem(f - chip + nf, nf) - 1
        return pltpu.make_async_remote_copy(
            src_ref=part.at[n, slot, s],
            dst_ref=came.at[n, gap, s],
            send_sem=psend.at[n, slot, s],
            recv_sem=precv.at[n, gap, s],
            device_id={"fsdp": chip},
            device_id_type=MESH,
        )

    def block(j):
        at = lax.rem(c - j + nc, nc) if by_plane else j
        return pl.ds(pl.multiple_of(at * rows, 16), rows)

    def to_owner(n, s, j):
        return pltpu.make_async_remote_copy(
            src_ref=part.at[n, own, s, block(j)],
            dst_ref=outs[n].at[j, :, pl.ds(pl.multiple_of(s * wide, wide), wide)],
            send_sem=zsend.at[n, s, j],
            recv_sem=zrecv.at[n, s, j],
            device_id={"ctx": lax.rem(c - stride * j + nc, nc)},
            device_id_type=MESH,
        )

    for n, terms in enumerate(sets):

        @pl.loop(0, seqs * nc)
        def _(i):
            s = lax.rem(i, nc)
            slot = lax.rem(own + 1 + i // nc, seqs)
            acc = None
            for which, lead, first, size, weight, row in terms:
                right = rights[weight][s] if row is None else rights[weight][s, row]
                term = dot(lefts[which][lead, slot, :, first : first + size], right, dims)
                acc = term if acc is None else acc + term
            part[n, slot, s] = acc.astype(BF16)

            @pl.when(t * seqs + slot != f)
            def _():
                to_chip(n, slot, s).start()

    for n in range(len(sets)):

        @pl.when(home)
        def _():
            @pl.loop(0, nc)
            def _(s):
                for r in range(nf - 1):
                    pltpu.make_async_remote_copy(
                        src_ref=came.at[n, r, s],
                        dst_ref=came.at[n, r, s],
                        send_sem=psend.at[n, 0, s],
                        recv_sem=precv.at[n, r, s],
                        device_id={"fsdp": lax.rem(f + 1, nf)},
                        device_id_type=MESH,
                    ).wait_recv()
                for j in reversed(range(blocks)):
                    where = block(j)
                    summed = part[n, own, s, where].astype(F32)
                    for r in range(nf - 1):
                        summed = summed + came[n, r, s, where].astype(F32)
                    if j == 0:
                        outs[n][0, :, pl.ds(pl.multiple_of(s * wide, wide), wide)] = summed.astype(BF16)
                    else:
                        part[n, own, s, where] = summed.astype(BF16)
                for j, there in by_gap(c // stride, blocks, start_order(blocks)):
                    pl.when(there)(lambda j=j: to_owner(n, s, j).start())

    @pl.when(home)
    def _():
        for n in range(len(sets)):
            for s in range(nc):
                for j in range(1, blocks):
                    to_owner(n, s, j).wait()

    @pl.when(jnp.logical_not(home))
    def _():
        for out in outs:
            out[...] = jnp.zeros_like(out)

    for slot in range(seqs):

        @pl.when(t * seqs + slot != f)
        def _():
            for n in range(len(sets)):
                for s in range(nc):
                    to_chip(n, slot, s).wait_send()

    finish_all(loads)


def collect(lay, lefts, rights, sets, stride, blocks, call_id, dims=NT, hauls=(), by_plane=False):
    seqs, count = lefts[0].shape[1:3]
    nc, wide = rights[0].shape[0], rights[0].shape[-2 if dims == NT else -1]
    rows, width = count // blocks, nc * wide
    held = len(sets) * (seqs + lay.nf) * count * width * 2
    held += sum(a.size for a in lefts) * 9 // 4 + sum(w.size for w in rights) * 2
    if held > VMEM_LIMIT:

        def block_of(terms, j, last):
            at = (lay.c - j) % nc if by_plane else j
            here = [lax.dynamic_slice_in_dim(a, at * rows, rows, 2) for a in lefts]
            if last is not None:
                here = lax.optimization_barrier((here, last))[0]
            partial = 0.0
            for which, lead, first, size, weight, row in terms:
                partial = partial + jnp.einsum(
                    "srh,pdh->srpd" if dims == NT else "srh,phd->srpd",
                    here[which][lead, :, :, first : first + size],
                    rights[weight] if row is None else rights[weight][:, row],
                    preferred_element_type=F32,
                )
            return partial.astype(BF16).reshape(seqs, rows, width)

        sums = [
            collect_permute(lay, functools.partial(block_of, terms), blocks, stride) for terms in sets
        ]
        return [*sums, *haul_alone(lay, hauls, call_id)]
    hauls = Hauls(lay, hauls)
    dma = pltpu.SemaphoreType.DMA
    in_vmem = pl.BlockSpec(memory_space=pltpu.VMEM)
    return pl.pallas_call(
        functools.partial(
            collect_body,
            lay.sizes,
            stride,
            blocks,
            by_plane,
            dims,
            sets,
            len(lefts),
            len(rights),
            hauls,
        ),
        out_shape=[jax.ShapeDtypeStruct((blocks, rows, width), BF16)] * len(sets) + hauls.shapes,
        in_specs=[in_vmem] * (len(lefts) + len(rights)) + hauls.in_specs,
        out_specs=[in_vmem] * len(sets) + hauls.out_specs,
        scratch_shapes=[
            pltpu.VMEM((len(sets), seqs, nc, count, wide), BF16),
            pltpu.VMEM((len(sets), lay.nf - 1, nc, count, wide), BF16),
            dma((len(sets), seqs, nc)),
            dma((len(sets), lay.nf - 1, nc)),
            dma((len(sets), nc, blocks)),
            dma((len(sets), nc, blocks)),
        ]
        + hauls.scratch,
        compiler_params=params(call_id),
        name=f"collect{call_id}",
    )(*lefts, *rights, *hauls.operands)


def haul_alone_body(lay_sizes, hauls, *refs):
    nf, nc, nt, seqs = lay_sizes
    loads = hauls.split(refs, 0, 0)[3]
    greet(nf, nc, nt)
    start_all(loads)
    finish_all(loads)


def haul_alone(lay, hauls, call_id):
    if not hauls:
        return []
    hauls = Hauls(lay, hauls)
    return pl.pallas_call(
        functools.partial(haul_alone_body, lay.sizes, hauls),
        out_shape=hauls.shapes,
        in_specs=hauls.in_specs,
        out_specs=hauls.out_specs,
        scratch_shapes=hauls.scratch,
        compiler_params=params(call_id),
        name=f"haul{call_id}",
    )(*hauls.operands)


def finish_body(lay_sizes, hauls, *refs):
    nf, nc, nt, seqs = lay_sizes
    (terms, grad), (sums, grad_out), scratch, loads = hauls.split(refs, 2, 2)
    landed, middle, total, zsend, zrecv, psend, precv, tsend, trecv = scratch
    f, c, t = lax.axis_index("fsdp"), lax.axis_index("ctx"), lax.axis_index("tp")
    home = t == f // seqs
    barrier = pltpu.get_barrier_semaphore()
    others = [(k, u) for k in range(nf) for u in range(nt) if (k, u) != (0, 0)]
    for j in range(1, nc):
        pl.semaphore_signal(
            barrier, inc=1, device_id={"ctx": lax.rem(c + j, nc)}, device_id_type=MESH
        )
    for k, u in others:
        pl.semaphore_signal(
            barrier,
            inc=1,
            device_id={"fsdp": lax.rem(f + k, nf), "tp": lax.rem(t + u, nt)},
            device_id_type=MESH,
        )
    pl.semaphore_wait(barrier, nc - 1 + len(others))

    def along_ctx(j):
        return pltpu.make_async_remote_copy(
            src_ref=terms.at[lax.rem(c + j, nc)],
            dst_ref=middle.at[j],
            send_sem=zsend.at[j],
            recv_sem=zrecv.at[j],
            device_id={"ctx": lax.rem(c + j, nc)},
            device_id_type=MESH,
        )

    def in_plane(k, u):
        chip = lax.rem(f + k, nf)
        return pltpu.make_async_remote_copy(
            src_ref=total.at[chip],
            dst_ref=landed.at[f],
            send_sem=psend.at[k, u],
            recv_sem=precv.at[f],
            device_id={"fsdp": chip, "tp": lax.rem(t + u, nt)},
            device_id_type=MESH,
        )

    def to_core(u):
        return pltpu.make_async_remote_copy(
            src_ref=grad,
            dst_ref=grad_out,
            send_sem=tsend.at[u],
            recv_sem=trecv.at[0],
            device_id={"tp": lax.rem(t + u, nt)},
            device_id_type=MESH,
        )

    @pl.when(home)
    def _():
        for j in range(1, nc):
            along_ctx(j).start()
        for u in range(1, nt):
            to_core(u).start()

    start_all(loads)

    @pl.when(home)
    def _():
        grad_out[...] = grad[...]
        summed = terms[c]
        for j in range(1, nc):
            along_ctx(j).wait_recv()
            summed = summed + middle[j]
        total[...] = summed
        for k, u in others:
            in_plane(k, u).start()
        landed[f] = total[f]

    for chip in range(nf):

        @pl.when(jnp.logical_not(jnp.logical_and(home, f == chip)))
        def _():
            pltpu.make_async_remote_copy(
                src_ref=landed.at[chip],
                dst_ref=landed.at[chip],
                send_sem=psend.at[0, 0],
                recv_sem=precv.at[chip],
                device_id={"fsdp": lax.rem(f + 1, nf)},
                device_id_type=MESH,
            ).wait_recv()

    sums[...] = jnp.sum(landed[...], axis=0)

    @pl.when(home)
    def _():
        for j in range(1, nc):
            along_ctx(j).wait_send()
        for k, u in others:
            in_plane(k, u).wait_send()
        for u in range(1, nt):
            to_core(u).wait_send()

    @pl.when(jnp.logical_not(home))
    def _():
        to_core(1).wait_recv()

    finish_all(loads)


def finish(lay, terms, grad, call_id, hauls=()):
    lines, part = terms.shape[2:]
    hauls = Hauls(lay, hauls)
    dma = pltpu.SemaphoreType.DMA
    in_vmem = pl.BlockSpec(memory_space=pltpu.VMEM)
    return pl.pallas_call(
        functools.partial(finish_body, lay.sizes, hauls),
        out_shape=[
            jax.ShapeDtypeStruct((lines, part), F32),
            jax.ShapeDtypeStruct(grad.shape, grad.dtype),
        ]
        + hauls.shapes,
        in_specs=[in_vmem] * 2 + hauls.in_specs,
        out_specs=[in_vmem] * 2 + hauls.out_specs,
        scratch_shapes=[
            pltpu.VMEM((lay.nf, lines, part), F32),
            pltpu.VMEM((lay.nc, lay.nf, lines, part), F32),
            pltpu.VMEM((lay.nf, lines, part), F32),
            dma((lay.nc,)),
            dma((lay.nc,)),
            dma((lay.nf, lay.nt)),
            dma((lay.nf,)),
            dma((lay.nt,)),
            dma((1,)),
        ]
        + hauls.scratch,
        compiler_params=params(call_id),
        name=f"finish{call_id}",
    )(terms, grad, *hauls.operands)


def turn(values, cosine, sine):
    return values * cosine + pltpu.roll(values, DH // 2, axis=1) * sine


def chunk_dot(a_ref, weights, row=None, dims=NN):
    planes, wide = weights.shape[0], weights.shape[-2 if dims == NN else -1]
    acc = None
    for s in range(planes):
        weight = weights[s] if row is None else weights[s, row]
        term = dot(a_ref[:, s * wide : (s + 1) * wide], weight, dims)
        acc = term if acc is None else acc + term
    return acc


def pick_columns(ids, expert, planes, cap):
    count = ids.shape[0]
    rows = count // lax.axis_size("ctx")
    member = jnp.where(jnp.logical_or(ids[:, 0:1] == expert, ids[:, 1:2] == expert), 1.0, 0.0)
    before = lax.broadcasted_iota(jnp.int32, (rows, rows), 1)
    before = (before < lax.broadcasted_iota(jnp.int32, (rows, rows), 0)).astype(BF16)
    places = []
    for plane in range(count // rows):
        here = member[plane * rows : (plane + 1) * rows]
        rank = dot(before, jnp.broadcast_to(here, (rows, DH)).astype(BF16))[:, 0:1]
        first = -1.0
        for n, chosen in enumerate(planes):
            first = jnp.where(chosen == plane, float(n * cap), first)
        places.append(jnp.where(jnp.logical_and(here > 0.5, first >= 0.0), rank + first, -1.0))
    place = jnp.concatenate(places, axis=0)
    columns = lax.broadcasted_iota(jnp.int32, (count, len(planes) * cap), 1).astype(F32)
    return jnp.where(place == columns, 1.0, 0.0)


def attend_body(lay_sizes, rep, hauls, *refs):
    nf, nc, nt, seqs = lay_sizes
    ins, outs, scratch, loads = hauls.split(refs, 10, 8)
    x_ref, ids_ref, small_ref, q0, q1, kv0, kv1, cos_ref, sin_ref, pos_ref = ins
    normed_ref, q_ref, k_ref, v_ref, mixed_ref, put_ref, qpos_ref, other_ref = outs
    c = lax.axis_index("ctx")
    expert = c // rep

    @pl.when(pl.program_id(0) == 0)
    def _():
        greet(nf, nc, nt, True)
        start_all(loads)

    wide = small_ref.shape[-1]
    total = 0.0
    for s in range(nc):
        x = x_ref[0, :, s * wide : (s + 1) * wide].astype(F32)
        total = total + jnp.sum(x * x, axis=-1, keepdims=True)
    inverse = lax.rsqrt(total * (1.0 / (nc * wide)) + EPSILON)
    for s in range(nc):
        columns = slice(s * wide, (s + 1) * wide)
        gain = small_ref[s, 0:1].astype(F32)
        normed_ref[0, :, columns] = (x_ref[0, :, columns].astype(F32) * inverse * gain).astype(BF16)
    normed = normed_ref.at[0]

    cap = qpos_ref.shape[-1] * rep // nc
    planes = [lax.rem(c - rep * j + nc, nc) for j in range(nc // rep)]
    ids = ids_ref[0].astype(F32)
    pick = pick_columns(ids[:, 0:2], expert.astype(F32), planes, cap)
    put_ref[0] = pick.astype(BF16)
    qpos_ref[0] = jnp.sum(pick * pos_ref[...], axis=0, keepdims=True)
    seen = pos_ref[...] <= qpos_ref[0]
    pick_m = pick_columns(ids[:, 2:4], expert.astype(F32), planes, cap).astype(BF16)
    other = jnp.where(ids[:, 2:3] == expert.astype(F32), ids[:, 3:4], ids[:, 2:3])
    other = dot(pick_m, jnp.broadcast_to(other, (other.shape[0], DH)).astype(BF16), TN)
    other_ref[0] = other[:, 0:1]

    cosine, sine = cos_ref[...], sin_ref[...]
    half = q0.shape[-1]
    for side, (query, key_value) in enumerate(((q0, kv0), (q1, kv1))):
        v_ref[0, :, side * half : (side + 1) * half] = chunk_dot(normed, key_value, 1).astype(BF16)
        keys = chunk_dot(normed, key_value, 0)
        queries = chunk_dot(normed, query)
        for h in range(half // DH):
            cols = slice(side * half + h * DH, side * half + (h + 1) * DH)
            here = slice(h * DH, (h + 1) * DH)
            k_ref[0, :, cols] = turn(keys[:, here], cosine, sine).astype(BF16)
            turned = turn(queries[:, here], cosine, sine).astype(BF16)
            q_ref[0, :, cols] = dot(put_ref[0], turned, TN).astype(BF16)
    for h in range(2 * half // DH):
        cols = slice(h * DH, (h + 1) * DH)
        scores = dot(k_ref[0, :, cols], q_ref[0, :, cols], NT) * (1.0 / math.sqrt(DH))
        scores = jnp.where(seen, scores, MASKED)
        powers = jnp.exp(scores - jnp.max(scores, axis=0, keepdims=True))
        probs = (powers / jnp.sum(powers, axis=0, keepdims=True)).astype(BF16)
        mixed_ref[0, :, cols] = dot(probs, v_ref[0, :, cols], TN).astype(BF16)

    @pl.when(pl.program_id(0) == seqs - 1)
    def _():
        finish_all(loads)


def attend(lay, x, small, weights, cosine, sine, pos, cap, call_id, hauls):
    seqs, count = x.shape[:2]
    width = lay.nc * small.shape[-1]
    heads = 2 * weights[0].shape[-1]
    picked = lay.experts * cap
    hauls = Hauls(lay, hauls)
    per_seq = lambda i: (i, 0, 0)
    once = pl.Buffered(1)
    weight_specs = [
        pl.BlockSpec(w.shape, lambda i, n=w.ndim: (0,) * n, pipeline_mode=once) for w in weights
    ]
    results = [
        ((count, width), BF16),
        ((picked, heads), BF16),
        ((count, heads), BF16),
        ((count, heads), BF16),
        ((picked, heads), BF16),
        ((count, picked), BF16),
        ((1, picked), F32),
        ((picked, 1), F32),
    ]
    return pl.pallas_call(
        functools.partial(attend_body, lay.sizes, lay.rep, hauls),
        grid=(seqs,),
        in_specs=[
            pl.BlockSpec((1, count, width), per_seq),
            pl.BlockSpec((1, count, DH), lambda i: (i, 0, width // DH)),
            pl.BlockSpec(small.shape, lambda i: (0, 0, 0)),
            *weight_specs,
            pl.BlockSpec((count, DH), lambda i: (0, 0)),
            pl.BlockSpec((count, DH), lambda i: (0, 0)),
            pl.BlockSpec((count, 1), lambda i: (0, 0)),
        ]
        + hauls.in_specs,
        out_specs=[pl.BlockSpec((1,) + dims, per_seq) for dims, _ in results] + hauls.out_specs,
        out_shape=[jax.ShapeDtypeStruct((seqs,) + dims, kind) for dims, kind in results]
        + hauls.shapes,
        scratch_shapes=hauls.scratch,
        compiler_params=params(call_id),
        name="attend",
    )(x, x, small, *weights, cosine, sine, pos, *hauls.operands)


def experts_body(rep, experts, n_ref, g_ref, small_ref, other_ref, *refs):
    weights, (ge_ref, hidden_ref, gate_ref, up_ref) = refs[:6], refs[6:]
    c = lax.axis_index("ctx")
    lanes = lax.broadcasted_iota(jnp.int32, (1, small_ref.shape[1]), 1) - (2 + experts)
    logits = chunk_dot(n_ref.at[0], small_ref, None, NT)
    mine = jnp.sum(jnp.where(lanes == c // rep, logits, 0.0), axis=-1, keepdims=True)
    theirs = jnp.where(lanes.astype(F32) == other_ref[0], logits, 0.0)
    theirs = jnp.sum(theirs, axis=-1, keepdims=True)
    ge_ref[0] = (jax.nn.sigmoid(mine - theirs) * g_ref[0].astype(F32)).astype(BF16)
    for side in range(2):
        gate_weight, up_weight, down_weight = weights[side::2]
        gate_pre = chunk_dot(n_ref.at[0], gate_weight, None, NT)
        up_pre = chunk_dot(n_ref.at[0], up_weight, None, NT)
        grad_hidden = chunk_dot(ge_ref.at[0], down_weight, None, NT)
        sigmoid_gate = jax.nn.sigmoid(gate_pre)
        silu_gate = gate_pre * sigmoid_gate
        hidden_ref[side, 0] = (silu_gate * up_pre).astype(BF16)
        silu_slope = sigmoid_gate + silu_gate * (1.0 - sigmoid_gate)
        gate_ref[side, 0] = (grad_hidden * up_pre * silu_slope).astype(BF16)
        up_ref[side, 0] = (grad_hidden * silu_gate).astype(BF16)


def experts_apply(lay, n2, g, small, other, *weights):
    seqs, count, width = n2.shape
    ff = weights[0].shape[-2]
    per_seq = lambda i: (i, 0, 0)
    once = pl.Buffered(1)
    wide = pl.BlockSpec((2, 1, count, ff), lambda i: (0, i, 0, 0))
    return pl.pallas_call(
        functools.partial(experts_body, lay.rep, lay.experts),
        grid=(seqs,),
        in_specs=[
            pl.BlockSpec((1, count, width), per_seq),
            pl.BlockSpec((1, count, width), per_seq),
            pl.BlockSpec(small.shape, lambda i: (0, 0, 0)),
            pl.BlockSpec((1, count, 1), per_seq),
        ]
        + [pl.BlockSpec(w.shape, lambda i: (0, 0, 0), pipeline_mode=once) for w in weights],
        out_specs=[pl.BlockSpec((1, count, width), per_seq), wide, wide, wide],
        out_shape=[jax.ShapeDtypeStruct(n2.shape, BF16)]
        + [jax.ShapeDtypeStruct((2, seqs, count, ff), BF16)] * 3,
        compiler_params=pltpu.CompilerParams(vmem_limit_bytes=VMEM_LIMIT),
        name="experts",
    )(n2, g, small, other, *weights)


def core_exchange(refs, nt):
    away, came, send_sem, recv_sem = refs

    def copy(s):
        return pltpu.make_async_remote_copy(
            src_ref=away.at[s],
            dst_ref=came.at[s],
            send_sem=send_sem.at[s],
            recv_sem=recv_sem.at[s],
            device_id={"tp": lax.rem(lax.axis_index("tp") + 1, nt)},
            device_id_type=MESH,
        )

    return copy


def greet_core(nt):
    barrier = pltpu.get_barrier_semaphore()
    other = lax.rem(lax.axis_index("tp") + 1, nt)
    pl.semaphore_signal(barrier, inc=1, device_id={"tp": other}, device_id_type=MESH)
    pl.semaphore_wait(barrier, 1)


def mlp_grads_body(nc, nt, n_ref, ge_ref, hidden_ref, gate_ref, up_ref, *refs):
    outs, (away, came) = refs[:5], refs[5:7]
    copy = core_exchange(refs[5:], nt)
    wide = away.shape[-1]
    half = outs[1].shape[1]
    pairs = ((gate_ref, n_ref), (up_ref, n_ref), (hidden_ref, ge_ref))
    greet_core(nt)

    @pl.loop(0, nc)
    def _(s):
        columns = pl.ds(pl.multiple_of(s * wide, wide), wide)
        for i, (left, right) in enumerate(pairs):
            away[s, i] = dot(left[1], right[:, columns], TN).astype(BF16)
        copy(s).start()

    @pl.loop(0, nc)
    def _(s):
        columns = pl.ds(pl.multiple_of(s * wide, wide), wide)
        copy(s).wait_recv()
        for i, (left, right) in enumerate(pairs):
            own = dot(left[0], right[:, columns], TN)
            grad = (own + came[s, i].astype(F32)).astype(BF16)
            if i == 0:
                outs[0][s] = grad
            else:
                outs[2 * i - 1][s] = grad[:half]
                outs[2 * i][s] = grad[half:]

    @pl.loop(0, nc)
    def _(s):
        copy(s).wait_send()


def mlp_grads(lay, n2, ge, hidden, gate, up, call_id):
    width, ff, nc = n2.shape[1], hidden.shape[-1], lay.nc
    piece = (3, ff, width // nc)
    in_vmem = pl.BlockSpec(memory_space=pltpu.VMEM)
    whole = jax.ShapeDtypeStruct((nc, ff, width // nc), BF16)
    half = jax.ShapeDtypeStruct((nc, ff // 2, width // nc), BF16)
    return pl.pallas_call(
        functools.partial(mlp_grads_body, nc, lay.nt),
        in_specs=[in_vmem] * 5,
        out_specs=[in_vmem] * 5,
        out_shape=[whole] + [half] * 4,
        scratch_shapes=[
            pltpu.VMEM((nc,) + piece, BF16),
            pltpu.VMEM((nc,) + piece, BF16),
            pltpu.SemaphoreType.DMA((nc,)),
            pltpu.SemaphoreType.DMA((nc,)),
        ],
        compiler_params=params(call_id),
        name="mlp_grads",
    )(n2, ge, hidden, gate, up)


def attn_grads_body(lay_sizes, hauls, *refs):
    nf, nc, nt, seqs = lay_sizes
    (x_ref, d_ref, g_ref, mixed_ref), outs, scratch, loads = hauls.split(refs, 4, 4)
    kept, away, came = scratch[:3]
    copy = core_exchange(scratch[1:], nt)
    wide, half = away.shape[-2:]
    greet(nf, nc, nt)
    start_all(loads)

    @pl.loop(0, nc)
    def _(s):
        columns = pl.ds(pl.multiple_of(s * wide, wide), wide)
        first = dot(x_ref[:, columns], d_ref[...], TN)
        last = dot(g_ref[:, columns], mixed_ref[...], TN)
        for i in range(4):
            part, at = (first, i) if i < 3 else (last, 0)
            step = 3 if i < 3 else 1
            kept[s, i] = part[:, at * half : (at + 1) * half]
            away[s, i] = part[:, (step + at) * half : (step + at + 1) * half].astype(BF16)
        copy(s).start()

    @pl.loop(0, nc)
    def _(s):
        copy(s).wait_recv()
        for i in range(4):
            outs[i][s] = (kept[s, i] + came[s, i].astype(F32)).astype(BF16)

    @pl.loop(0, nc)
    def _(s):
        copy(s).wait_send()

    finish_all(loads)


def attn_grads(lay, x, grads, g, mixed, call_id, hauls):
    width, heads, nc = x.shape[1], mixed.shape[-1], lay.nc
    piece = (width // nc, heads // 2)
    hauls = Hauls(lay, hauls)
    in_vmem = pl.BlockSpec(memory_space=pltpu.VMEM)
    return pl.pallas_call(
        functools.partial(attn_grads_body, lay.sizes, hauls),
        in_specs=[in_vmem] * 4 + hauls.in_specs,
        out_specs=[in_vmem] * 4 + hauls.out_specs,
        out_shape=[jax.ShapeDtypeStruct((nc,) + piece, BF16)] * 4 + hauls.shapes,
        scratch_shapes=[
            pltpu.VMEM((nc, 4) + piece, F32),
            pltpu.VMEM((nc, 4) + piece, BF16),
            pltpu.VMEM((nc, 4) + piece, BF16),
            pltpu.SemaphoreType.DMA((nc,)),
            pltpu.SemaphoreType.DMA((nc,)),
        ]
        + hauls.scratch,
        compiler_params=params(call_id),
        name="attn_grads",
    )(x, grads, g, mixed, *hauls.operands)


def attend_back_body(lay_sizes, hauls, *refs):
    nf, nc, nt, seqs = lay_sizes
    ins, (out_ref,), scratch, loads = hauls.split(refs, 11, 1)
    q_ref, k_ref, v_ref, g_ref, wo0, wo1, qpos_ref, kpos_ref, cosine, sine, put = ins

    @pl.when(pl.program_id(0) == 0)
    def _():
        greet(nf, nc, nt)
        start_all(loads)

    scale = 1.0 / math.sqrt(DH)
    seen = kpos_ref[...] <= qpos_ref[0]
    half = wo0.shape[-1]
    for side, weight in enumerate((wo0, wo1)):
        grad_mixed = chunk_dot(g_ref.at[0], weight).astype(BF16)
        for h in range(half // DH):
            cols = slice(side * half + h * DH, side * half + (h + 1) * DH)
            q, k, v = q_ref[0, :, cols], k_ref[0, :, cols], v_ref[0, :, cols]
            g = grad_mixed[:, h * DH : (h + 1) * DH]
            scores = jnp.where(seen, dot(k, q, NT) * scale, MASKED)
            powers = jnp.exp(scores - jnp.max(scores, axis=0, keepdims=True))
            probs = powers / jnp.sum(powers, axis=0, keepdims=True)
            grad_probs = dot(v, g, NT)
            centre = jnp.sum(probs * grad_probs, axis=0, keepdims=True)
            grad_scores = (probs * (grad_probs - centre)).astype(BF16)

            def at(part):
                first = (3 * side + part) * half + h * DH
                return slice(first, first + DH)

            out_ref[0, :, at(2)] = dot(probs.astype(BF16), g).astype(BF16)
            dk = dot(grad_scores, q) * scale
            out_ref[0, :, at(1)] = turn(dk, cosine[...], -sine[...]).astype(BF16)
            dq = dot(grad_scores, k, TN) * scale
            high = dq.astype(BF16)
            low = (dq - high.astype(F32)).astype(BF16)
            dq = dot(put[0], high) + dot(put[0], low)
            out_ref[0, :, at(0)] = turn(dq, cosine[...], -sine[...]).astype(BF16)

    @pl.when(pl.program_id(0) == seqs - 1)
    def _():
        finish_all(loads)


def attend_back(lay, q, k, v, g, weights, qpos, kpos, cosine, sine, put, call_id, hauls):
    seqs, count, heads = q.shape
    width = g.shape[-1]
    length = k.shape[1]
    hauls = Hauls(lay, hauls)
    per_seq = lambda s: (s, 0, 0)
    once = lambda s: (0, 0)
    return pl.pallas_call(
        functools.partial(attend_back_body, lay.sizes, hauls),
        grid=(seqs,),
        in_specs=[
            pl.BlockSpec((1, count, heads), per_seq),
            pl.BlockSpec((1, length, heads), per_seq),
            pl.BlockSpec((1, length, heads), per_seq),
            pl.BlockSpec((1, count, width), per_seq),
            pl.BlockSpec(weights[0].shape, lambda s: (0, 0, 0)),
            pl.BlockSpec(weights[1].shape, lambda s: (0, 0, 0)),
            pl.BlockSpec((1, 1, count), per_seq),
            pl.BlockSpec((length, 1), once),
            pl.BlockSpec((length, DH), once),
            pl.BlockSpec((length, DH), once),
            pl.BlockSpec((1, length, count), per_seq),
        ]
        + hauls.in_specs,
        out_specs=[pl.BlockSpec((1, length, 3 * heads), per_seq)] + hauls.out_specs,
        out_shape=[jax.ShapeDtypeStruct((seqs, length, 3 * heads), BF16)] + hauls.shapes,
        scratch_shapes=hauls.scratch,
        compiler_params=params(call_id),
        name="attend_back",
    )(q, k, v, g, *weights, qpos, kpos, cosine, sine, put, *hauls.operands)


def unpack_body(gate, up_a, up_b, down_a, down_b, gate_up, down):
    half = up_a.shape[1]

    def total(ref):
        return jnp.sum(ref[...].astype(F32), axis=0)

    gate_up[0, 0] = total(gate)
    gate_up[0, 1, 0:half] = total(up_a)
    gate_up[0, 1, half:] = total(up_b)
    down[0, 0:half] = total(down_a)
    down[0, half:] = total(down_b)


def unpack(lay, *parts):
    ff, wide = parts[0].shape[1:]
    experts, rep = lay.experts, lay.rep
    return pl.pallas_call(
        unpack_body,
        grid=(experts,),
        in_specs=[pl.BlockSpec((rep,) + p.shape[1:], lambda e: (e, 0, 0)) for p in parts],
        out_specs=[
            pl.BlockSpec((1, 2, ff, wide), lambda e: (e, 0, 0, 0)),
            pl.BlockSpec((1, ff, wide), lambda e: (e, 0, 0)),
        ],
        out_shape=[
            jax.ShapeDtypeStruct((experts, 2, ff, wide), F32),
            jax.ShapeDtypeStruct((experts, ff, wide), F32),
        ],
        compiler_params=pltpu.CompilerParams(vmem_limit_bytes=VMEM_LIMIT),
        name="unpack",
    )(*parts)


def row_of(small_ref, line):
    planes = [small_ref[s, line : line + 1] for s in range(small_ref.shape[0])]
    return jnp.concatenate(planes, axis=1).astype(F32)


def choices(ids, expert, experts, cap):
    rows = ids.shape[0]
    before = lax.broadcasted_iota(jnp.int32, (rows, rows), 1)
    before = (before < lax.broadcasted_iota(jnp.int32, (rows, rows), 0)).astype(BF16)
    lanes = lax.broadcasted_iota(jnp.int32, (rows, DH), 1).astype(F32)
    member = jnp.where(jnp.logical_or(ids[:, 0:1] == lanes, ids[:, 1:2] == lanes), 1.0, 0.0)
    ranks = dot(before, member.astype(BF16))
    columns = lax.broadcasted_iota(jnp.int32, (rows, experts * cap), 1).astype(F32)
    maps = []
    for slot in range(2):
        chosen = ids[:, slot : slot + 1]
        rank = jnp.sum(jnp.where(lanes == chosen, ranks, 0.0), axis=-1, keepdims=True)
        ahead = chosen - expert.astype(F32)
        ahead = jnp.where(ahead < 0.0, ahead + experts, ahead)
        maps.append(jnp.where(columns == ahead * cap + rank, 1.0, 0.0).astype(BF16))
    return maps


def slot_gates(normed, small_ref, ids, first):
    planes, lines, wide = small_ref.shape
    logits = 0.0
    for s in range(planes):
        logits = logits + dot(normed[:, s * wide : (s + 1) * wide], small_ref[s], NT)
    lanes = lax.broadcasted_iota(jnp.int32, logits.shape, 1).astype(F32)
    picked = [
        jnp.sum(jnp.where(lanes == ids[:, k : k + 1] + first, logits, 0.0), axis=-1, keepdims=True)
        for k in range(2)
    ]
    return jax.nn.sigmoid(picked[0] - picked[1]), jax.nn.sigmoid(picked[1] - picked[0])


def norm_of(values, gain):
    inverse = lax.rsqrt(jnp.mean(values * values, axis=-1, keepdims=True) + EPSILON)
    scaled = values * inverse
    return inverse, scaled, (scaled * gain).astype(BF16)


def norm_back(grad, gain, inverse, scaled):
    turned = grad * gain
    return inverse * (turned - scaled * jnp.mean(turned * scaled, axis=-1, keepdims=True))


def logits_back(gates, choice, ids, first):
    mean = gates[0] * choice[0] + gates[1] * choice[1]
    lanes = lax.broadcasted_iota(jnp.int32, (ids.shape[0], DH), 1).astype(F32)
    out = 0.0
    for k in range(2):
        inner = gates[k] * (choice[k] - mean)
        out = out + jnp.where(lanes == ids[:, k : k + 1] + first, inner, 0.0)
    return out


def exact_tn(left, right):
    total = 0.0
    for _ in range(3):
        part = left.astype(BF16)
        total = total + dot(part, right, TN)
        left = left - part.astype(F32)
    return total


def owner_forward_body(rep, experts, x_ref, ids_ref, small_ref, rows_ref, residual_ref, out_ref):
    expert = lax.axis_index("ctx") // rep
    cap = rows_ref.shape[0] // experts
    ids = ids_ref[...]
    x = x_ref[...].astype(F32)
    normed_one = norm_of(x, row_of(small_ref, 0))[2]
    gates = slot_gates(normed_one, small_ref, ids[:, 0:2], 2)
    maps = choices(ids[:, 0:2], expert, experts, cap)
    residual = x + (gates[0] * dot(maps[0], rows_ref[...]) + gates[1] * dot(maps[1], rows_ref[...]))
    residual_ref[...] = residual
    normed_two = norm_of(residual, row_of(small_ref, 1))[2]
    maps = choices(ids[:, 2:4], expert, experts, cap)
    out_ref[...] = dot(maps[0] + maps[1], normed_two, TN).astype(BF16)


def owner_middle_body(rep, experts, *refs):
    x_ref, ids_ref, small_ref, up_ref, residual_ref, branch_ref, expert_ref, grad_ref = refs[:8]
    layer_ref, grad_res_ref, out_ref, logits_ref, terms_ref = refs[8:]
    expert = lax.axis_index("ctx") // rep
    cap = branch_ref.shape[0] // experts
    ids = ids_ref[...]
    upstream, residual = up_ref[...].astype(F32), residual_ref[...]
    gain_two = row_of(small_ref, 1)
    inverse_two, scaled_two, normed_two = norm_of(residual, gain_two)
    gates = slot_gates(normed_two, small_ref, ids[:, 2:4], 2 + experts)
    maps = choices(ids[:, 2:4], expert, experts, cap)
    choice, total = [], 0.0
    for k in range(2):
        expert_out = dot(maps[k], expert_ref[...])
        choice.append(jnp.sum(upstream * expert_out, axis=-1, keepdims=True))
        total = total + gates[k] * expert_out
    layer_ref[...] = (residual + total).astype(BF16)
    logits_two = logits_back(gates, choice, ids[:, 2:4], 2 + experts)
    grad = dot(maps[0] + maps[1], grad_ref[...])
    for e in range(experts):
        line = 2 + experts + e
        grad = grad + logits_two[:, line : line + 1] * row_of(small_ref, line)
    grad_res = upstream + norm_back(grad, gain_two, inverse_two, scaled_two)
    grad_res_ref[...] = grad_res
    gain_grad = jnp.sum(grad * scaled_two, axis=0, keepdims=True)
    normed_one = norm_of(x_ref[...].astype(F32), row_of(small_ref, 0))[2]
    gates = slot_gates(normed_one, small_ref, ids[:, 0:2], 2)
    maps = choices(ids[:, 0:2], expert, experts, cap)
    choice, out = [], 0.0
    for k in range(2):
        branch = dot(maps[k], branch_ref[...])
        choice.append(jnp.sum(grad_res * branch, axis=-1, keepdims=True))
        out = out + dot(maps[k], (gates[k] * grad_res).astype(BF16), TN)
    out_ref[...] = out.astype(BF16)
    logits_one = logits_back(gates, choice, ids[:, 0:2], 2)
    logits_ref[...] = logits_one
    lines = terms_ref.shape[0]
    terms = exact_tn(logits_one, normed_one) + exact_tn(logits_two, normed_two)
    place = lax.broadcasted_iota(jnp.int32, terms_ref.shape, 0)
    terms_ref[...] = jnp.where(place == 1, gain_grad, terms[:lines])


def owner_back_body(experts, x_ref, small_ref, rows_ref, logits_ref, grad_res_ref, layer_ref, terms_ref, both_ref, out_ref):
    gain = row_of(small_ref, 0)
    inverse, scaled, _ = norm_of(x_ref[...].astype(F32), gain)
    grad = 0.0
    for j in range(rows_ref.shape[0]):
        grad = grad + rows_ref[j].astype(F32)
    for e in range(experts):
        grad = grad + logits_ref[:, 2 + e : 3 + e] * row_of(small_ref, 2 + e)
    both_ref[0] = layer_ref[...]
    both_ref[1] = (grad_res_ref[...] + norm_back(grad, gain, inverse, scaled)).astype(BF16)
    gain_grad = jnp.sum(grad * scaled, axis=0, keepdims=True)
    place = lax.broadcasted_iota(jnp.int32, terms_ref.shape, 0)
    terms = jnp.where(place == 0, gain_grad, terms_ref[...])
    planes, chips, _, part = out_ref.shape
    for plane in range(planes):
        for chip in range(chips):
            first = (chip * planes + plane) * part
            out_ref[plane, chip] = terms[:, first : first + part]


def own_kernel(body, name, results, *operands):
    in_vmem = pl.BlockSpec(memory_space=pltpu.VMEM)
    return pl.pallas_call(
        body,
        in_specs=[in_vmem] * len(operands),
        out_specs=[in_vmem] * len(results),
        out_shape=[jax.ShapeDtypeStruct(dims, kind) for dims, kind in results],
        compiler_params=pltpu.CompilerParams(vmem_limit_bytes=VMEM_LIMIT),
        name=name,
    )(*operands)


def ranks_of(member):
    count = member.shape[-1]
    before = (jnp.arange(count)[:, None] < jnp.arange(count)[None, :]).astype(BF16)
    return jnp.einsum("...m,mn->...n", member.astype(BF16), before, preferred_element_type=F32)


def pick_maps(ids, expert, cap):
    member = jnp.any(ids == expert[..., None, None], axis=-1)
    rank = ranks_of(member).astype(jnp.int32)
    place = jnp.arange(cap, dtype=jnp.int32)[:, None]
    return jnp.logical_and(member[..., None, :], rank[..., None, :] == place)


def per_device(
    tokens,
    cotangent,
    attn_ids,
    mlp_ids,
    span_ids,
    attn_gain,
    attn_router,
    kv_weight,
    query_weight,
    output_weight,
    mlp_gain,
    mlp_router,
    gate_up_weight,
    down_weight,
):
    experts = query_weight.shape[0]
    lay = Layout(experts)
    nf, nc, rep, seqs = lay.nf, lay.nc, lay.rep, lay.seqs
    rows, width = tokens.shape
    cap = 3 * rows // 4
    expert = lay.c // rep

    def to_planes(array, index_of, both=False):
        index = index_of(0)
        shape = array.shape[len(index) :]
        return Haul(array, lambda ref, d: ref.at[index_of(d)] if index else ref, shape, both)

    expert_of = (expert + jnp.arange(experts)) % experts
    pick_own_m = pick_maps(jnp.broadcast_to(mlp_ids, (experts, rows, 2)), expert_of, cap)

    def dispatch(pick, values):
        return jnp.einsum(
            "jrn,nd->jrd", pick.astype(BF16), values, preferred_element_type=F32
        ).astype(BF16)

    ids = jnp.concatenate([attn_ids, mlp_ids], axis=1).astype(BF16)
    payload = jnp.concatenate([tokens, jnp.pad(ids, ((0, 0), (0, 124)))], axis=1)
    small = jnp.concatenate([attn_gain[None], mlp_gain[None], attn_router.T, mlp_router.T])
    small = jnp.pad(small, ((0, -small.shape[0] % 16), (0, 0)))
    g_own = dispatch(pick_own_m, cotangent)
    by_plane = lambda *more: lambda d: (d // rep,) + more
    x_all, small_all, g_mine, _, q_own, q_sib, kv_own, kv_sib = opening(
        lay,
        payload,
        small,
        g_own,
        1,
        [to_planes(query_weight, by_plane(), True), Relay(kv_weight)],
    )
    gate_up_turned = gate_up_weight.swapaxes(-1, -2)
    down_turned = down_weight.swapaxes(-1, -2)

    own_ids = ids.astype(F32)

    half_len = rows // 2
    offsets = jnp.arange(rows, dtype=jnp.int32)
    pos = jnp.where(
        offsets[None, :] < half_len,
        span_ids[:, 0:1] * half_len + offsets[None, :],
        span_ids[:, 1:2] * half_len + offsets[None, :] - half_len,
    )
    pos = pos.astype(F32).reshape(-1, 1)
    freqs = ROPE_BASE ** (-jnp.arange(DH // 2, dtype=F32) / (DH // 2))

    cosine, sine = jnp.cos(pos * freqs), jnp.sin(pos * freqs)
    cosine = jnp.concatenate([cosine, cosine], axis=-1)
    sine = jnp.concatenate([-sine, sine], axis=-1)

    normed_all, q, k, v, mixed, put, pos_q, other, o_own, o_sib, gate_own, gate_sib, g_blocks = attend(
        lay,
        x_all.reshape(seqs, nc * rows, -1),
        small_all,
        [q_own, q_sib, kv_own, kv_sib],
        cosine,
        sine,
        pos,
        cap,
        9,
        [
            to_planes(output_weight, by_plane(), True),
            to_planes(gate_up_turned, by_plane(0), True),
            Share(lay, g_mine),
        ],
    )
    g_blocks = g_blocks.reshape(seqs, experts * cap, width)
    heads = q.shape[-1]
    half = heads // 2
    branch_rows, up_own, up_sib = collect(
        lay,
        [mixed[None]],
        [o_own, o_sib],
        [((0, 0, 0, half, 0, None), (0, 0, half, half, 1, None))],
        rep,
        experts,
        2,
        hauls=[to_planes(gate_up_turned, by_plane(1), True)],
    )
    branch_rows = branch_rows.reshape(-1, width)
    residual, n2_own = own_kernel(
        functools.partial(owner_forward_body, rep, experts),
        "owner_forward",
        [((rows, width), F32), ((experts * cap, width), BF16)],
        tokens,
        own_ids,
        small_all,
        branch_rows,
    )

    n2, down_own, down_sib = spread(
        lay,
        n2_own.reshape(experts, cap, width),
        rep,
        3,
        [to_planes(down_turned, by_plane(), True)],
    )
    n2 = n2.reshape(seqs, experts * cap, width)
    grad_expert, hidden, grad_gate, grad_up = experts_apply(
        lay,
        n2,
        g_blocks,
        small_all,
        other,
        gate_own,
        gate_sib,
        up_own,
        up_sib,
        down_own,
        down_sib,
    )
    ff = hidden.shape[-1]
    gate_grads, up_a, up_b, down_a, down_b = mlp_grads(
        lay,
        n2.reshape(-1, width),
        grad_expert.reshape(-1, width),
        *(a.reshape(2, -1, ff) for a in (hidden, grad_gate, grad_up)),
        4,
    )
    by_piece = lambda d: (d,)
    expert_rows, grad_rows, gate_back = collect(
        lay,
        [hidden, grad_gate, grad_up],
        [gate_own, up_own, down_own, gate_sib, up_sib, down_sib],
        [
            tuple((0, side, 0, ff, 3 * side + 2, None) for side in range(2)),
            tuple((1 + i, side, 0, ff, 3 * side + i, None) for side in range(2) for i in range(2)),
        ],
        rep,
        experts,
        5,
        NN,
        [to_planes(gate_grads, by_piece)],
    )
    lines = -(-(2 + 2 * experts) // 16) * 16
    layer_out, grad_residual, gb_own, logits_one, terms = own_kernel(
        functools.partial(owner_middle_body, rep, experts),
        "owner_middle",
        [
            ((rows, width), BF16),
            ((rows, width), F32),
            ((experts * cap, width), BF16),
            ((rows, DH), F32),
            ((lines, width), F32),
        ],
        tokens,
        own_ids,
        small_all,
        cotangent,
        residual,
        branch_rows,
        expert_rows.reshape(-1, width),
        grad_rows.reshape(-1, width),
    )

    gb, up_a = spread(lay, gb_own.reshape(experts, cap, width), rep, 6, [to_planes(up_a, by_piece)])
    gb = gb.reshape(seqs, experts * cap, width)
    dqkv, up_b = attend_back(
        lay,
        q,
        k,
        v,
        gb,
        [o_own, o_sib],
        pos_q,
        pos,
        cosine,
        sine,
        put,
        11,
        [to_planes(up_b, by_piece)],
    )
    q_grads, k_grads, v_grads, o_grads, down_a = attn_grads(
        lay,
        normed_all.reshape(-1, width),
        dqkv.reshape(-1, 3 * heads),
        gb.reshape(-1, width),
        mixed.reshape(-1, heads),
        10,
        [to_planes(down_a, by_piece)],
    )
    grad_one_rows, down_b, o_back, q_back = collect(
        lay,
        [dqkv[None]],
        [q_own, kv_own, q_sib, kv_sib],
        [
            tuple(
                (0, 0, (3 * s + i) * half, half, 2 * s + (i > 0), None if i == 0 else i - 1)
                for i in range(3)
                for s in range(2)
            )
        ],
        1,
        nc,
        7,
        hauls=[to_planes(grads, by_piece) for grads in (down_b, o_grads, q_grads)],
        by_plane=True,
    )

    both, terms = own_kernel(
        functools.partial(owner_back_body, experts),
        "owner_back",
        [((2, rows, width), BF16), ((nc, nf, lines, width // (nf * nc)), F32)],
        tokens,
        small_all,
        grad_one_rows,
        logits_one,
        grad_residual,
        layer_out,
        terms,
    )
    terms, both_out, k_back, v_back = finish(
        lay, terms, both, 8, [to_planes(grads, by_piece) for grads in (k_grads, v_grads)]
    )
    layer_out, grad_tokens = both_out[0], both_out[1]

    def by_expert(came):
        out = came.astype(F32)
        if rep > 1:
            out = jnp.sum(out.reshape((experts, rep) + out.shape[1:]), axis=1)
        return out

    grad_query_weight, grad_output_weight = by_expert(q_back), by_expert(o_back)
    grad_kv_weight = jnp.stack([jnp.sum(g.astype(F32), axis=0) for g in (k_back, v_back)])
    grad_gate_up, grad_down = unpack(lay, gate_back, up_a, up_b, down_a, down_b)
    grad_gate_up, grad_down = grad_gate_up.swapaxes(-1, -2), grad_down.swapaxes(-1, -2)
    return (
        layer_out,
        grad_tokens,
        terms[0],
        terms[2 : 2 + experts].T,
        grad_kv_weight,
        grad_query_weight,
        grad_output_weight,
        terms[1],
        terms[2 + experts : 2 + 2 * experts].T,
        grad_gate_up,
        grad_down,
    )


def solution(mesh):
    placed = (
        P(("fsdp", "ctx"), None),
        P(("fsdp", "ctx"), None),
        P(("fsdp", "ctx"), None),
        P(("fsdp", "ctx"), None),
        P(),
        P("ctx"),
        P("ctx", None),
        P(None, "ctx", ("fsdp", "tp")),
        P(None, "ctx", ("fsdp", "tp")),
        P(None, "ctx", ("fsdp", "tp")),
        P("ctx"),
        P("ctx", None),
        P(None, None, "ctx", ("fsdp", "tp")),
        P(None, "ctx", ("fsdp", "tp")),
    )
    return jax.shard_map(
        per_device,
        mesh=mesh,
        in_specs=placed,
        out_specs=(
            P(("fsdp", "ctx"), None),
            P(("fsdp", "ctx"), None),
            P(("fsdp", "ctx")),
            P(("fsdp", "ctx"), None),
            P(None, "ctx", ("fsdp", "tp")),
            P(None, "ctx", ("fsdp", "tp")),
            P(None, "ctx", ("fsdp", "tp")),
            P(("fsdp", "ctx")),
            P(("fsdp", "ctx"), None),
            P(None, None, "ctx", ("fsdp", "tp")),
            P(None, "ctx", ("fsdp", "tp")),
        ),
        check_vma=False,
    )
```

```python
import functools
import math

import jax
import jax.numpy as jnp
from jax import lax
from jax.experimental import pallas as pl
from jax.experimental.pallas import tpu as pltpu
from jax.sharding import PartitionSpec as P

DH = 128
EPSILON = 1e-06
ROPE_BASE = 10000.0
MASKED = -1e30
HIGH = lax.Precision.HIGHEST
MESH = pl.DeviceIdType.MESH
AXES = ("fsdp", "ctx", "tp")
F32 = jnp.float32
BF16 = jnp.bfloat16
VMEM_LIMIT = 60 * 1024 * 1024
NT = (((1,), (1,)), ((), ()))
NN = (((1,), (0,)), ((), ()))
TN = (((0,), (0,)), ((), ()))


def dot(a, b, dims=NN):
    return lax.dot_general(a, b, dims, preferred_element_type=F32)


class Layout:
    def __init__(self, experts):
        self.nf = lax.axis_size("fsdp")
        self.nc = lax.axis_size("ctx")
        self.nt = lax.axis_size("tp")
        self.experts = experts
        self.rep = self.nc // experts
        self.seqs = self.nf // self.nt
        self.f = lax.axis_index("fsdp")
        self.c = lax.axis_index("ctx")
        self.t = lax.axis_index("tp")
        self.home = self.t == self.f // self.seqs
        self.sizes = (self.nf, self.nc, self.nt, self.seqs)

    def flat(self, f, c, t):
        return (f * self.nc + c) * self.nt + t


def home_pairs(lay, move):
    pairs = []
    for f in range(lay.nf):
        t = f // lay.seqs
        for c in range(lay.nc):
            f2, c2 = move(f, c)
            pairs.append((lay.flat(f, c, t), lay.flat(f2, c2, t)))
    return pairs


def collect_permute(lay, block_of, blocks, stride):
    got, last = [], None
    for j in range(blocks):
        partial = block_of(j, last)
        zeros = jnp.zeros((lay.nf,) + partial.shape[1:], partial.dtype)
        full = lax.dynamic_update_slice_in_dim(zeros, partial, lay.t * lay.seqs, 0)
        last = lax.psum_scatter(full, "fsdp", scatter_dimension=0, tiled=True)[0]
        if j > 0:
            pairs = home_pairs(lay, lambda f, c: (f, (c - stride * j) % lay.nc))
            last = lax.ppermute(last, AXES, pairs)
        got.append(last)
    return jnp.stack(got)


class Haul:
    def __init__(self, array, piece=None, shape=None, both=False):
        self.array, self.piece, self.both = array, piece, both
        self.shape = array.shape if shape is None else shape

    def out_shapes(self, nc):
        dims = self.shape if self.piece is None else (nc,) + self.shape
        return [jax.ShapeDtypeStruct(dims, self.array.dtype)] * (2 if self.both else 1)

    def scratch(self, nc):
        return [pltpu.SemaphoreType.DMA((nc,))] * (4 if self.both else 2)

    def bind(self, place, src, outs, sems):
        load = Load()
        load.piece, load.both, load.place = self.piece, self.both, place
        load.src, load.outs, load.sems = src, outs, sems
        return load


def by_gap(at, size, gaps):
    order = []
    for gap in dict.fromkeys(gap for gap in gaps if gap > 0):
        order += [(gap, at - gap >= 0), (size - gap, at + gap < size)]
    return order


def start_order(size):
    return [size - 1, *range(1, size - 1)]


def wait_order(size):
    return [1, size - 1, *range(2, size - 1)] if size > 1 else []


def ahead_by_gap(at, size):
    return [(size - j, there) for j, there in by_gap(at, size, start_order(size))]


class Load:
    def along_ctx(self, j):
        nc, c, nt, t = self.place
        return pltpu.make_async_remote_copy(
            src_ref=self.piece(self.src, lax.rem(c + j, nc)),
            dst_ref=self.outs[0].at[c],
            send_sem=self.sems[0].at[j],
            recv_sem=self.sems[1].at[j],
            device_id={"ctx": lax.rem(c + j, nc)},
            device_id_type=MESH,
        )

    def landed(self, j):
        nc, c, nt, t = self.place
        here = self.outs[0].at[lax.rem(c - j + nc, nc)]
        return pltpu.make_async_remote_copy(
            src_ref=here,
            dst_ref=here,
            send_sem=self.sems[0].at[j],
            recv_sem=self.sems[1].at[j],
            device_id={"ctx": lax.rem(c + j, nc)},
            device_id_type=MESH,
        )

    def to_core(self, j):
        nc, c, nt, t = self.place
        if self.piece is None:
            src, dst, at = self.src, self.outs[0], 0
        else:
            source = lax.rem(c - j + nc, nc)
            src = self.piece(self.src, c) if j == 0 else self.outs[0].at[source]
            dst, at = self.outs[1].at[source], 2
        return pltpu.make_async_remote_copy(
            src_ref=src,
            dst_ref=dst,
            send_sem=self.sems[at].at[j],
            recv_sem=self.sems[at + 1].at[j],
            device_id={"tp": lax.rem(t + 1, nt)},
            device_id_type=MESH,
        )

    def keep(self):
        nc, c, nt, t = self.place
        return pltpu.make_async_copy(
            self.piece(self.src, c), self.outs[0].at[c], self.sems[0].at[0]
        )

    def start(self):
        if self.piece is None:
            self.to_core(0).start()
            return
        for j, there in ahead_by_gap(self.place[1], self.place[0]):
            pl.when(there)(lambda j=j: self.along_ctx(j).start())
        self.keep().start()
        if self.both:
            self.to_core(0).start()

    def pass_on(self):
        if self.piece is None:
            return
        for j, there in by_gap(self.place[1], self.place[0], wait_order(self.place[0])):

            @pl.when(there)
            def _():
                self.landed(j).wait_recv()
                if self.both:
                    self.to_core(j).start()

    def finish(self):
        if self.piece is None:
            self.to_core(0).wait()
            return
        self.keep().wait()
        for j in range(self.place[0]):
            if j > 0:
                self.along_ctx(j).wait_send()
            if self.both:
                self.to_core(j).wait()


class Relay:
    both = True

    def __init__(self, array):
        self.array = array

    def out_shapes(self, nc):
        return [jax.ShapeDtypeStruct((nc,) + self.array.shape, self.array.dtype)] * 2

    def scratch(self, nc):
        return [pltpu.SemaphoreType.DMA((2, nc))] * 2 + [pltpu.SemaphoreType.DMA((nc,))] * 2

    def bind(self, place, src, outs, sems):
        load = RelayLoad()
        load.place, load.src, load.outs, load.sems = place, src, outs, sems
        return load


def relay_step(place, way, k, src, dst, send_sem, recv_sem):
    nc, c = place[:2]
    step = 1 - 2 * way
    copy = pltpu.make_async_remote_copy(
        src_ref=src,
        dst_ref=dst,
        send_sem=send_sem.at[way, k],
        recv_sem=recv_sem.at[way, k],
        device_id={"ctx": lax.rem(c + step + nc, nc)},
        device_id_type=MESH,
    )
    sent = jnp.logical_and(c - step * k >= 0, c - step * k < nc)
    sent = jnp.logical_and(sent, jnp.logical_and(c + step >= 0, c + step < nc))
    return copy, sent


def relayed(place, way, k):
    nc, c = place[:2]
    source = c - (1 - 2 * way) * k
    return lax.rem(source + nc, nc), jnp.logical_and(source >= 0, source < nc)


class RelayLoad:
    def copy(self, way, k):
        source = relayed(self.place, way, k)[0]
        src = self.src if k == 0 else self.outs[0].at[source]
        return relay_step(self.place, way, k, src, self.outs[0].at[source], *self.sems[:2])

    def arrival(self, way, k):
        source, there = relayed(self.place, way, k)
        here = self.outs[0].at[source]
        return pltpu.make_async_remote_copy(
            src_ref=here,
            dst_ref=here,
            send_sem=self.sems[0].at[way, k],
            recv_sem=self.sems[1].at[way, k - 1],
            device_id={"ctx": lax.rem(self.place[1] + 1, self.place[0])},
            device_id_type=MESH,
        ), there

    def to_core(self, source):
        nc, c, nt, t = self.place
        return pltpu.make_async_remote_copy(
            src_ref=self.outs[0].at[source],
            dst_ref=self.outs[1].at[source],
            send_sem=self.sems[2].at[source],
            recv_sem=self.sems[3].at[source],
            device_id={"tp": lax.rem(t + 1, nt)},
            device_id_type=MESH,
        )

    def own_to_core(self):
        nc, c, nt, t = self.place
        return pltpu.make_async_remote_copy(
            src_ref=self.src,
            dst_ref=self.outs[1].at[c],
            send_sem=self.sems[2].at[c],
            recv_sem=self.sems[3].at[c],
            device_id={"tp": lax.rem(t + 1, nt)},
            device_id_type=MESH,
        )

    def keep(self):
        nc, c = self.place[:2]
        return pltpu.make_async_copy(self.src, self.outs[0].at[c], self.sems[0].at[0, nc - 1])

    def start(self):
        for way in range(2):
            copy, sent = self.copy(way, 0)
            pl.when(sent)(copy.start)
        self.keep().start()
        self.own_to_core().start()

    def pass_on(self):
        nc = self.place[0]
        for k in range(1, nc):
            for way in range(2):
                arrival, there = self.arrival(way, k)
                source = relayed(self.place, way, k)[0]
                copy, sent = self.copy(way, k)

                @pl.when(there)
                def _():
                    arrival.wait_recv()
                    self.to_core(source).start()

                if k < nc - 1:
                    pl.when(sent)(copy.start)

    def finish(self):
        nc, c = self.place[:2]
        self.keep().wait()
        for k in range(nc - 1):
            for way in range(2):
                copy, sent = self.copy(way, k)
                pl.when(sent)(copy.wait_send)
        for source in range(nc):

            @pl.when(c != source)
            def _():
                self.to_core(source).wait()

        self.own_to_core().wait()


class Share:
    both = False

    def __init__(self, lay, array):
        self.lay_sizes, self.array = lay.sizes, array

    def out_shapes(self, nc):
        nt, seqs = self.lay_sizes[2:]
        n, rows, width = self.array.shape
        return [jax.ShapeDtypeStruct((seqs, n, rows, nt * width), self.array.dtype)]

    def scratch(self, nc):
        nf, _, nt, seqs = self.lay_sizes
        return [pltpu.SemaphoreType.DMA((nf,)), pltpu.SemaphoreType.DMA((seqs, nt))]

    def bind(self, place, src, outs, sems):
        load = SharedLoad()
        load.lay_sizes, load.src, load.out, load.sems = self.lay_sizes, src, outs[0], sems
        return load


class SharedLoad:
    def target(self, slot, core):
        width = self.src.shape[-1]
        return self.out.at[slot, :, :, pl.ds(pl.multiple_of(core * width, 128), width)]

    def to_chip(self, k):
        nf, _, nt, seqs = self.lay_sizes
        f, t = lax.axis_index("fsdp"), lax.axis_index("tp")
        own = lax.rem(f, seqs)
        return pltpu.make_async_remote_copy(
            src_ref=self.src,
            dst_ref=self.target(own, t),
            send_sem=self.sems[0].at[k],
            recv_sem=self.sems[1].at[own, t],
            device_id={"fsdp": lax.rem(f + k, nf), "tp": f // seqs},
            device_id_type=MESH,
        )

    def keep(self):
        f, t = lax.axis_index("fsdp"), lax.axis_index("tp")
        own = lax.rem(f, self.lay_sizes[3])
        return pltpu.make_async_copy(self.src, self.target(own, t), self.sems[0].at[0])

    def at_home(self):
        return lax.axis_index("tp") == lax.axis_index("fsdp") // self.lay_sizes[3]

    def start(self):
        for k in range(1, self.lay_sizes[0]):
            self.to_chip(k).start()
        pl.when(self.at_home())(lambda: self.keep().start())
        pl.when(jnp.logical_not(self.at_home()))(lambda: self.to_chip(0).start())

    def pass_on(self):
        pass

    def finish(self):
        nf, _, nt, seqs = self.lay_sizes
        f, t = lax.axis_index("fsdp"), lax.axis_index("tp")
        for i in range(seqs):
            for core in range(nt):
                mine = jnp.logical_and(f == t * seqs + i, t == core)

                @pl.when(jnp.logical_not(mine))
                def _():
                    pltpu.make_async_remote_copy(
                        src_ref=self.target(i, core),
                        dst_ref=self.target(i, core),
                        send_sem=self.sems[0].at[0],
                        recv_sem=self.sems[1].at[i, core],
                        device_id={"fsdp": lax.rem(f + 1, nf)},
                        device_id_type=MESH,
                    ).wait_recv()

        for k in range(1, nf):
            self.to_chip(k).wait_send()
        pl.when(self.at_home())(lambda: self.keep().wait())
        pl.when(jnp.logical_not(self.at_home()))(lambda: self.to_chip(0).wait_send())


class Hauls:
    def __init__(self, lay, hauls):
        self.nc, self.hauls = lay.nc, list(hauls)
        self.operands = [h.array for h in self.hauls]
        self.shapes = [shape for h in self.hauls for shape in h.out_shapes(lay.nc)]
        self.scratch = [sem for h in self.hauls for sem in h.scratch(lay.nc)]
        anywhere = pl.BlockSpec(memory_space=pl.ANY)
        self.in_specs = [anywhere] * len(self.operands)
        self.out_specs = [anywhere] * len(self.shapes)

    def split(self, refs, n_in, n_out):
        more_in, more_out, sems = len(self.operands), len(self.shapes), len(self.scratch)
        ins, refs = refs[:n_in], refs[n_in:]
        srcs, refs = refs[:more_in], refs[more_in:]
        outs, refs = refs[:n_out], refs[n_out:]
        dsts, refs = refs[:more_out], refs[more_out:]
        scratch = refs[: len(refs) - sems]
        refs = refs[len(refs) - sems :]
        c, t = lax.axis_index("ctx"), lax.axis_index("tp")
        place = (self.nc, c, lax.axis_size("tp"), t)
        loads = []
        for haul, src in zip(self.hauls, srcs):
            count, held = len(haul.out_shapes(self.nc)), len(haul.scratch(self.nc))
            loads.append(haul.bind(place, src, dsts[:count], refs[:held]))
            dsts, refs = dsts[count:], refs[held:]
        return ins, outs, scratch, loads


def start_all(loads):
    for load in loads:
        load.start()


def finish_all(loads):
    for load in loads:
        load.pass_on()
    for load in loads:
        load.finish()


def greet(nf, nc, nt, whole_plane=False):
    f, c, t = lax.axis_index("fsdp"), lax.axis_index("ctx"), lax.axis_index("tp")
    barrier = pltpu.get_barrier_semaphore()
    peers = [{"ctx": lax.rem(c + gap, nc)} for gap in range(1, nc)]
    for k in range(nf):
        for u in range(nt):
            if (k, u) != (0, 0) and (k == 0 or u == 0 or whole_plane):
                peers.append({"fsdp": lax.rem(f + k, nf), "tp": lax.rem(t + u, nt)})
    for peer in peers:
        pl.semaphore_signal(barrier, inc=1, device_id=peer, device_id_type=MESH)
    pl.semaphore_wait(barrier, len(peers))


def params(call_id):
    return pltpu.CompilerParams(
        collective_id=call_id, has_side_effects=True, vmem_limit_bytes=VMEM_LIMIT
    )


def opening_body(lay_sizes, experts, hauls, *refs):
    nf, nc, nt, seqs = lay_sizes
    (src, small, later), (out, smalls, mine, stage), sems, loads = hauls.split(refs, 3, 4)
    zsend, zrecv, psend, precv, ssend, srecv, lsend, lrecv, here = sems
    f, c, t = lax.axis_index("fsdp"), lax.axis_index("ctx"), lax.axis_index("tp")
    place = (nc, c, nt, t)
    own = lax.rem(f, seqs)
    home = t == f // seqs
    rows, width = stage.shape[1], mine.shape[2]
    greet(nf, nc, nt, True)

    def half(ref, core):
        return ref.at[pl.ds(pl.multiple_of(core * rows, 16), rows)]

    def relay(way, k):
        source = relayed(place, way, k)[0]
        from_ref = half(src, t) if k == 0 else stage.at[source]
        return relay_step(place, way, k, from_ref, stage.at[source], zsend, zrecv)

    def in_plane(source, k, first):
        return pltpu.make_async_remote_copy(
            src_ref=half(src, t) if first else stage.at[source],
            dst_ref=half(out.at[own, source], t),
            send_sem=psend.at[source, k],
            recv_sem=precv.at[own, source, t],
            device_id={"fsdp": lax.rem(f + k, nf), "tp": f // seqs},
            device_id_type=MESH,
        )

    def keep(source, first):
        from_ref = half(src, t) if first else stage.at[source]
        return pltpu.make_async_copy(from_ref, half(out.at[own, source], t), here.at[source])

    def share(source, first=False):
        for k in range(1, nf):
            in_plane(source, k, first).start()
        pl.when(home)(lambda: keep(source, first).start())
        pl.when(jnp.logical_not(home))(lambda: in_plane(source, 0, first).start())

    def small_along_ctx(j, source):
        return pltpu.make_async_remote_copy(
            src_ref=small,
            dst_ref=smalls.at[source],
            send_sem=ssend.at[j],
            recv_sem=srecv.at[j],
            device_id={"ctx": lax.rem(c + j, nc)},
            device_id_type=MESH,
        )

    def later_along_ctx(j):
        return pltpu.make_async_remote_copy(
            src_ref=later.at[j, :, pl.ds(pl.multiple_of(t * width, 128), width)],
            dst_ref=mine.at[j],
            send_sem=lsend.at[j],
            recv_sem=lrecv.at[j],
            device_id={"ctx": lax.rem(c + (nc // experts) * j, nc)},
            device_id_type=MESH,
        )

    def keep_later():
        src_ref = later.at[0, :, pl.ds(pl.multiple_of(t * width, 128), width)]
        return pltpu.make_async_copy(src_ref, mine.at[0], lsend.at[0])

    for way in range(2):
        copy, sent = relay(way, 0)
        pl.when(sent)(lambda: copy.start())
    for j in range(1, nc):
        small_along_ctx(j, c).start()
    keep_small = pltpu.make_async_copy(small, smalls.at[c], ssend.at[0])
    keep_small.start()
    share(c, True)
    loads[0].start()
    keep_later().start()

    for k in range(1, nc):
        for way in range(2):
            source, there = relayed(place, way, k)

            @pl.when(there)
            def _():
                pltpu.make_async_remote_copy(
                    src_ref=stage.at[source],
                    dst_ref=stage.at[source],
                    send_sem=zsend.at[way, k],
                    recv_sem=zrecv.at[way, k - 1],
                    device_id={"ctx": lax.rem(c + 1, nc)},
                    device_id_type=MESH,
                ).wait_recv()
                if k < nc - 1:
                    copy, sent = relay(way, k)
                    pl.when(sent)(lambda: copy.start())
                share(source)

    start_all(loads[1:])
    for j in range(1, experts):
        later_along_ctx(j).start()

    for i in range(seqs):
        for core in range(nt):
            mine_here = jnp.logical_and(f == t * seqs + i, t == core)

            @pl.when(jnp.logical_not(mine_here))
            def _():
                for source in range(nc):
                    landing = half(out.at[i, source], core)
                    pltpu.make_async_remote_copy(
                        src_ref=landing,
                        dst_ref=landing,
                        send_sem=psend.at[source, 0],
                        recv_sem=precv.at[i, source, core],
                        device_id={"fsdp": lax.rem(f + 1, nf)},
                        device_id_type=MESH,
                    ).wait_recv()

    for j in range(1, nc):
        small_along_ctx(j, lax.rem(c - j + nc, nc)).wait_recv()
        small_along_ctx(j, c).wait_send()
    keep_small.wait()
    keep_later().wait()
    for k in range(nc - 1):
        for way in range(2):
            copy, sent = relay(way, k)
            pl.when(sent)(lambda: copy.wait_send())
    for source in range(nc):
        for k in range(1, nf):
            in_plane(source, k, False).wait_send()
        pl.when(home)(lambda: keep(source, False).wait())
        pl.when(jnp.logical_not(home))(lambda: in_plane(source, 0, False).wait_send())
    for j in range(1, experts):
        later_along_ctx(j).wait()
    finish_all(loads)


def opening(lay, rows, small, later, call_id, hauls):
    count, width = rows.shape
    nf, nc, nt, seqs = lay.sizes
    hauls = Hauls(lay, hauls)
    experts = lay.experts
    dma = pltpu.SemaphoreType.DMA
    anywhere = pl.BlockSpec(memory_space=pl.ANY)
    shapes = [
        jax.ShapeDtypeStruct((seqs, nc, count, width), rows.dtype),
        jax.ShapeDtypeStruct((nc,) + small.shape, small.dtype),
        jax.ShapeDtypeStruct(later.shape[:2] + (later.shape[2] // nt,), later.dtype),
        jax.ShapeDtypeStruct((nc, count // nt, width), rows.dtype),
    ]
    return pl.pallas_call(
        functools.partial(opening_body, lay.sizes, experts, hauls),
        out_shape=shapes + hauls.shapes,
        in_specs=[anywhere] * 3 + hauls.in_specs,
        out_specs=[anywhere] * 4 + hauls.out_specs,
        scratch_shapes=[
            dma((2, nc)),
            dma((2, nc)),
            dma((nc, nf)),
            dma((seqs, nc, nt)),
            dma((nc,)),
            dma((nc,)),
            dma((experts,)),
            dma((experts,)),
            dma((nc,)),
        ]
        + hauls.scratch,
        compiler_params=params(call_id),
        name=f"opening{call_id}",
    )(rows, small, later, *hauls.operands)


def spread_body(lay_sizes, stride, blocks, hauls, *refs):
    nf, nc, nt, seqs = lay_sizes
    (src,), (out,), (zsend, zrecv, psend, precv, here), loads = hauls.split(refs, 1, 1)
    f, c, t = lax.axis_index("fsdp"), lax.axis_index("ctx"), lax.axis_index("tp")
    own = lax.rem(f, seqs)
    home = t == f // seqs
    greet(nf, nc, nt)

    def along_ctx(j):
        return pltpu.make_async_remote_copy(
            src_ref=src.at[j],
            dst_ref=out.at[own, j],
            send_sem=zsend.at[j],
            recv_sem=zrecv.at[j],
            device_id={"ctx": lax.rem(c + stride * j, nc)},
            device_id_type=MESH,
        )

    def in_plane(j, k):
        return pltpu.make_async_remote_copy(
            src_ref=src.at[0] if j == 0 else out.at[own, j],
            dst_ref=out.at[own, j],
            send_sem=psend.at[j, k],
            recv_sem=precv.at[own, j],
            device_id={"fsdp": lax.rem(f + k, nf)},
            device_id_type=MESH,
        )

    keep = pltpu.make_async_copy(src.at[0], out.at[own, 0], here)

    @pl.when(home)
    def _():
        for j, there in ahead_by_gap(c // stride, blocks):
            pl.when(there)(lambda j=j: along_ctx(j).start())
        for k in range(1, nf):
            in_plane(0, k).start()
        keep.start()

    @pl.when(jnp.logical_not(home))
    def _():
        start_all(loads)

    @pl.when(home)
    def _():
        for j, there in by_gap(c // stride, blocks, wait_order(blocks)):

            @pl.when(there)
            def _():
                along_ctx(j).wait_recv()
                for k in range(1, nf):
                    in_plane(j, k).start()

        start_all(loads)
        keep.wait()

    for i in range(seqs):

        @pl.when(jnp.logical_not(jnp.logical_and(home, own == i)))
        def _():
            for j in range(blocks):
                pltpu.make_async_remote_copy(
                    src_ref=out.at[i, j],
                    dst_ref=out.at[i, j],
                    send_sem=psend.at[j, 0],
                    recv_sem=precv.at[i, j],
                    device_id={"fsdp": lax.rem(f + 1, nf)},
                    device_id_type=MESH,
                ).wait_recv()

    @pl.when(home)
    def _():
        for j in range(1, blocks):
            along_ctx(j).wait_send()
        for j in range(blocks):
            for k in range(1, nf):
                in_plane(j, k).wait_send()

    finish_all(loads)


def spread(lay, rows, stride, call_id, hauls=()):
    blocks = rows.shape[0]
    hauls = Hauls(lay, hauls)
    dma = pltpu.SemaphoreType.DMA
    anywhere = pl.BlockSpec(memory_space=pl.ANY)
    return pl.pallas_call(
        functools.partial(spread_body, lay.sizes, stride, blocks, hauls),
        out_shape=[jax.ShapeDtypeStruct((lay.seqs,) + rows.shape, rows.dtype)] + hauls.shapes,
        in_specs=[anywhere] + hauls.in_specs,
        out_specs=[anywhere] + hauls.out_specs,
        scratch_shapes=[
            dma((blocks,)),
            dma((blocks,)),
            dma((blocks, lay.nf)),
            dma((lay.seqs, blocks)),
            dma,
        ]
        + hauls.scratch,
        compiler_params=params(call_id),
        name=f"spread{call_id}",
    )(rows, *hauls.operands)


def collect_body(lay_sizes, stride, blocks, by_plane, dims, sets, n_a, n_w, hauls, *refs):
    nf, nc, nt, seqs = lay_sizes
    ins, outs, scratch, loads = hauls.split(refs, n_a + n_w, len(sets))
    lefts, rights = ins[:n_a], ins[n_a:]
    part, came, psend, precv, zsend, zrecv = scratch
    f, c, t = lax.axis_index("fsdp"), lax.axis_index("ctx"), lax.axis_index("tp")
    own = lax.rem(f, seqs)
    home = t == f // seqs
    greet(nf, nc, nt)
    start_all(loads)
    wide = part.shape[-1]
    rows = part.shape[-2] // blocks

    def to_chip(n, slot, s):
        chip = t * seqs + slot
        gap = lax.rem(f - chip + nf, nf) - 1
        return pltpu.make_async_remote_copy(
            src_ref=part.at[n, slot, s],
            dst_ref=came.at[n, gap, s],
            send_sem=psend.at[n, slot, s],
            recv_sem=precv.at[n, gap, s],
            device_id={"fsdp": chip},
            device_id_type=MESH,
        )

    def block(j):
        at = lax.rem(c - j + nc, nc) if by_plane else j
        return pl.ds(pl.multiple_of(at * rows, 16), rows)

    def to_owner(n, s, j):
        return pltpu.make_async_remote_copy(
            src_ref=part.at[n, own, s, block(j)],
            dst_ref=outs[n].at[j, :, pl.ds(pl.multiple_of(s * wide, wide), wide)],
            send_sem=zsend.at[n, s, j],
            recv_sem=zrecv.at[n, s, j],
            device_id={"ctx": lax.rem(c - stride * j + nc, nc)},
            device_id_type=MESH,
        )

    for n, terms in enumerate(sets):

        @pl.loop(0, seqs * nc)
        def _(i):
            s = lax.rem(i, nc)
            slot = lax.rem(own + 1 + i // nc, seqs)
            acc = None
            for which, lead, first, size, weight, row in terms:
                left = lefts[which][lead, slot, :, first : first + size]
                if isinstance(weight, tuple):
                    halves = [dot(left, rights[half][s], dims) for half in weight]
                    term = jnp.concatenate(halves, axis=1)
                else:
                    right = rights[weight][s] if row is None else rights[weight][s, row]
                    term = dot(left, right, dims)
                acc = term if acc is None else acc + term
            part[n, slot, s] = acc.astype(BF16)

            @pl.when(t * seqs + slot != f)
            def _():
                to_chip(n, slot, s).start()

    for n in range(len(sets)):

        @pl.when(home)
        def _():
            @pl.loop(0, nc)
            def _(s):
                for r in range(nf - 1):
                    pltpu.make_async_remote_copy(
                        src_ref=came.at[n, r, s],
                        dst_ref=came.at[n, r, s],
                        send_sem=psend.at[n, 0, s],
                        recv_sem=precv.at[n, r, s],
                        device_id={"fsdp": lax.rem(f + 1, nf)},
                        device_id_type=MESH,
                    ).wait_recv()
                for j in reversed(range(blocks)):
                    where = block(j)
                    summed = part[n, own, s, where].astype(F32)
                    for r in range(nf - 1):
                        summed = summed + came[n, r, s, where].astype(F32)
                    if j == 0:
                        outs[n][0, :, pl.ds(pl.multiple_of(s * wide, wide), wide)] = summed.astype(BF16)
                    else:
                        part[n, own, s, where] = summed.astype(BF16)
                for j, there in by_gap(c // stride, blocks, start_order(blocks)):
                    pl.when(there)(lambda j=j: to_owner(n, s, j).start())

    @pl.when(home)
    def _():
        for n in range(len(sets)):
            for s in range(nc):
                for j in range(1, blocks):
                    to_owner(n, s, j).wait()

    @pl.when(jnp.logical_not(home))
    def _():
        for out in outs:
            out[...] = jnp.zeros_like(out)

    for slot in range(seqs):

        @pl.when(t * seqs + slot != f)
        def _():
            for n in range(len(sets)):
                for s in range(nc):
                    to_chip(n, slot, s).wait_send()

    finish_all(loads)


def collect(lay, lefts, rights, sets, stride, blocks, call_id, dims=NT, hauls=(), by_plane=False):
    seqs, count = lefts[0].shape[1:3]
    nc, wide = rights[0].shape[0], rights[0].shape[-2 if dims == NT else -1]
    rows, width = count // blocks, nc * wide
    held = len(sets) * (seqs + lay.nf) * count * width * 2
    held += sum(a.size for a in lefts) * 9 // 4 + sum(w.size for w in rights) * 2
    if held > VMEM_LIMIT:

        def block_of(terms, j, last):
            at = (lay.c - j) % nc if by_plane else j
            here = [lax.dynamic_slice_in_dim(a, at * rows, rows, 2) for a in lefts]
            if last is not None:
                here = lax.optimization_barrier((here, last))[0]
            partial = 0.0
            for which, lead, first, size, weight, row in terms:
                if isinstance(weight, tuple):
                    right = jnp.concatenate([rights[half] for half in weight], axis=-1)
                else:
                    right = rights[weight] if row is None else rights[weight][:, row]
                partial = partial + jnp.einsum(
                    "srh,pdh->srpd" if dims == NT else "srh,phd->srpd",
                    here[which][lead, :, :, first : first + size],
                    right,
                    preferred_element_type=F32,
                )
            return partial.astype(BF16).reshape(seqs, rows, width)

        sums = [
            collect_permute(lay, functools.partial(block_of, terms), blocks, stride) for terms in sets
        ]
        return [*sums, *haul_alone(lay, hauls, call_id)]
    hauls = Hauls(lay, hauls)
    dma = pltpu.SemaphoreType.DMA
    in_vmem = pl.BlockSpec(memory_space=pltpu.VMEM)
    return pl.pallas_call(
        functools.partial(
            collect_body,
            lay.sizes,
            stride,
            blocks,
            by_plane,
            dims,
            sets,
            len(lefts),
            len(rights),
            hauls,
        ),
        out_shape=[jax.ShapeDtypeStruct((blocks, rows, width), BF16)] * len(sets) + hauls.shapes,
        in_specs=[in_vmem] * (len(lefts) + len(rights)) + hauls.in_specs,
        out_specs=[in_vmem] * len(sets) + hauls.out_specs,
        scratch_shapes=[
            pltpu.VMEM((len(sets), seqs, nc, count, wide), BF16),
            pltpu.VMEM((len(sets), lay.nf - 1, nc, count, wide), BF16),
            dma((len(sets), seqs, nc)),
            dma((len(sets), lay.nf - 1, nc)),
            dma((len(sets), nc, blocks)),
            dma((len(sets), nc, blocks)),
        ]
        + hauls.scratch,
        compiler_params=params(call_id),
        name=f"collect{call_id}",
    )(*lefts, *rights, *hauls.operands)


def haul_alone_body(lay_sizes, hauls, *refs):
    nf, nc, nt, seqs = lay_sizes
    loads = hauls.split(refs, 0, 0)[3]
    greet(nf, nc, nt)
    start_all(loads)
    finish_all(loads)


def haul_alone(lay, hauls, call_id):
    if not hauls:
        return []
    hauls = Hauls(lay, hauls)
    return pl.pallas_call(
        functools.partial(haul_alone_body, lay.sizes, hauls),
        out_shape=hauls.shapes,
        in_specs=hauls.in_specs,
        out_specs=hauls.out_specs,
        scratch_shapes=hauls.scratch,
        compiler_params=params(call_id),
        name=f"haul{call_id}",
    )(*hauls.operands)


def finish_body(lay_sizes, hauls, *refs):
    nf, nc, nt, seqs = lay_sizes
    (terms, grad), (sums, grad_out), scratch, loads = hauls.split(refs, 2, 2)
    landed, middle, total, zsend, zrecv, psend, precv, tsend, trecv = scratch
    f, c, t = lax.axis_index("fsdp"), lax.axis_index("ctx"), lax.axis_index("tp")
    home = t == f // seqs
    barrier = pltpu.get_barrier_semaphore()
    others = [(k, u) for k in range(nf) for u in range(nt) if (k, u) != (0, 0)]
    for j in range(1, nc):
        pl.semaphore_signal(
            barrier, inc=1, device_id={"ctx": lax.rem(c + j, nc)}, device_id_type=MESH
        )
    for k, u in others:
        pl.semaphore_signal(
            barrier,
            inc=1,
            device_id={"fsdp": lax.rem(f + k, nf), "tp": lax.rem(t + u, nt)},
            device_id_type=MESH,
        )
    pl.semaphore_wait(barrier, nc - 1 + len(others))

    def along_ctx(j):
        return pltpu.make_async_remote_copy(
            src_ref=terms.at[lax.rem(c + j, nc)],
            dst_ref=middle.at[j],
            send_sem=zsend.at[j],
            recv_sem=zrecv.at[j],
            device_id={"ctx": lax.rem(c + j, nc)},
            device_id_type=MESH,
        )

    def in_plane(k, u):
        chip = lax.rem(f + k, nf)
        return pltpu.make_async_remote_copy(
            src_ref=total.at[chip],
            dst_ref=landed.at[f],
            send_sem=psend.at[k, u],
            recv_sem=precv.at[f],
            device_id={"fsdp": chip, "tp": lax.rem(t + u, nt)},
            device_id_type=MESH,
        )

    def to_core(u):
        return pltpu.make_async_remote_copy(
            src_ref=grad,
            dst_ref=grad_out,
            send_sem=tsend.at[u],
            recv_sem=trecv.at[0],
            device_id={"tp": lax.rem(t + u, nt)},
            device_id_type=MESH,
        )

    @pl.when(home)
    def _():
        for j in range(1, nc):
            along_ctx(j).start()
        for u in range(1, nt):
            to_core(u).start()

    start_all(loads)

    @pl.when(home)
    def _():
        grad_out[...] = grad[...]
        summed = terms[c]
        for j in range(1, nc):
            along_ctx(j).wait_recv()
            summed = summed + middle[j]
        total[...] = summed
        for k, u in others:
            in_plane(k, u).start()
        landed[f] = total[f]

    for chip in range(nf):

        @pl.when(jnp.logical_not(jnp.logical_and(home, f == chip)))
        def _():
            pltpu.make_async_remote_copy(
                src_ref=landed.at[chip],
                dst_ref=landed.at[chip],
                send_sem=psend.at[0, 0],
                recv_sem=precv.at[chip],
                device_id={"fsdp": lax.rem(f + 1, nf)},
                device_id_type=MESH,
            ).wait_recv()

    sums[...] = jnp.sum(landed[...], axis=0)

    @pl.when(home)
    def _():
        for j in range(1, nc):
            along_ctx(j).wait_send()
        for k, u in others:
            in_plane(k, u).wait_send()
        for u in range(1, nt):
            to_core(u).wait_send()

    @pl.when(jnp.logical_not(home))
    def _():
        to_core(1).wait_recv()

    finish_all(loads)


def finish(lay, terms, grad, call_id, hauls=()):
    lines, part = terms.shape[2:]
    hauls = Hauls(lay, hauls)
    dma = pltpu.SemaphoreType.DMA
    in_vmem = pl.BlockSpec(memory_space=pltpu.VMEM)
    return pl.pallas_call(
        functools.partial(finish_body, lay.sizes, hauls),
        out_shape=[
            jax.ShapeDtypeStruct((lines, part), F32),
            jax.ShapeDtypeStruct(grad.shape, grad.dtype),
        ]
        + hauls.shapes,
        in_specs=[in_vmem] * 2 + hauls.in_specs,
        out_specs=[in_vmem] * 2 + hauls.out_specs,
        scratch_shapes=[
            pltpu.VMEM((lay.nf, lines, part), F32),
            pltpu.VMEM((lay.nc, lay.nf, lines, part), F32),
            pltpu.VMEM((lay.nf, lines, part), F32),
            dma((lay.nc,)),
            dma((lay.nc,)),
            dma((lay.nf, lay.nt)),
            dma((lay.nf,)),
            dma((lay.nt,)),
            dma((1,)),
        ]
        + hauls.scratch,
        compiler_params=params(call_id),
        name=f"finish{call_id}",
    )(terms, grad, *hauls.operands)


def turn(values, cosine, sine):
    return values * cosine + pltpu.roll(values, DH // 2, axis=1) * sine


def chunk_dot(a_ref, weights, row=None, dims=NN):
    planes, wide = weights.shape[0], weights.shape[-2 if dims == NN else -1]
    acc = None
    for s in range(planes):
        weight = weights[s] if row is None else weights[s, row]
        term = dot(a_ref[:, s * wide : (s + 1) * wide], weight, dims)
        acc = term if acc is None else acc + term
    return acc


def pick_columns(ids, expert, planes, cap):
    count = ids.shape[0]
    rows = count // lax.axis_size("ctx")
    member = jnp.where(jnp.logical_or(ids[:, 0:1] == expert, ids[:, 1:2] == expert), 1.0, 0.0)
    before = lax.broadcasted_iota(jnp.int32, (rows, rows), 1)
    before = (before < lax.broadcasted_iota(jnp.int32, (rows, rows), 0)).astype(BF16)
    places = []
    for plane in range(count // rows):
        here = member[plane * rows : (plane + 1) * rows]
        rank = dot(before, jnp.broadcast_to(here, (rows, DH)).astype(BF16))[:, 0:1]
        first = -1.0
        for n, chosen in enumerate(planes):
            first = jnp.where(chosen == plane, float(n * cap), first)
        places.append(jnp.where(jnp.logical_and(here > 0.5, first >= 0.0), rank + first, -1.0))
    place = jnp.concatenate(places, axis=0)
    columns = lax.broadcasted_iota(jnp.int32, (count, len(planes) * cap), 1).astype(F32)
    return jnp.where(place == columns, 1.0, 0.0)


def attend_body(lay_sizes, rep, hauls, *refs):
    nf, nc, nt, seqs = lay_sizes
    ins, outs, scratch, loads = hauls.split(refs, 10, 8)
    x_ref, ids_ref, small_ref, q0, q1, kv0, kv1, cos_ref, sin_ref, pos_ref = ins
    normed_ref, q_ref, k_ref, v_ref, mixed_ref, put_ref, qpos_ref, other_ref = outs
    c = lax.axis_index("ctx")
    expert = c // rep

    @pl.when(pl.program_id(0) == 0)
    def _():
        greet(nf, nc, nt, True)
        start_all(loads)

    wide = small_ref.shape[-1]
    total = 0.0
    for s in range(nc):
        x = x_ref[0, :, s * wide : (s + 1) * wide].astype(F32)
        total = total + jnp.sum(x * x, axis=-1, keepdims=True)
    inverse = lax.rsqrt(total * (1.0 / (nc * wide)) + EPSILON)
    for s in range(nc):
        columns = slice(s * wide, (s + 1) * wide)
        gain = small_ref[s, 0:1].astype(F32)
        normed_ref[0, :, columns] = (x_ref[0, :, columns].astype(F32) * inverse * gain).astype(BF16)
    normed = normed_ref.at[0]

    cap = qpos_ref.shape[-1] * rep // nc
    planes = [lax.rem(c - rep * j + nc, nc) for j in range(nc // rep)]
    ids = ids_ref[0].astype(F32)
    pick = pick_columns(ids[:, 0:2], expert.astype(F32), planes, cap)
    put_ref[0] = pick.astype(BF16)
    qpos_ref[0] = jnp.sum(pick * pos_ref[...], axis=0, keepdims=True)
    seen = pos_ref[...] <= qpos_ref[0]
    pick_m = pick_columns(ids[:, 2:4], expert.astype(F32), planes, cap).astype(BF16)
    other = jnp.where(ids[:, 2:3] == expert.astype(F32), ids[:, 3:4], ids[:, 2:3])
    other = dot(pick_m, jnp.broadcast_to(other, (other.shape[0], DH)).astype(BF16), TN)
    other_ref[0] = other[:, 0:1]

    cosine, sine = cos_ref[...], sin_ref[...]
    half = q0.shape[-1]
    for side, (query, key_value) in enumerate(((q0, kv0), (q1, kv1))):
        v_ref[0, :, side * half : (side + 1) * half] = chunk_dot(normed, key_value, 1).astype(BF16)
        keys = chunk_dot(normed, key_value, 0)
        queries = chunk_dot(normed, query)
        for h in range(half // DH):
            cols = slice(side * half + h * DH, side * half + (h + 1) * DH)
            here = slice(h * DH, (h + 1) * DH)
            k_ref[0, :, cols] = turn(keys[:, here], cosine, sine).astype(BF16)
            turned = turn(queries[:, here], cosine, sine).astype(BF16)
            q_ref[0, :, cols] = dot(put_ref[0], turned, TN).astype(BF16)
    for h in range(2 * half // DH):
        cols = slice(h * DH, (h + 1) * DH)
        scores = dot(k_ref[0, :, cols], q_ref[0, :, cols], NT) * (1.0 / math.sqrt(DH))
        scores = jnp.where(seen, scores, MASKED)
        powers = jnp.exp(scores - jnp.max(scores, axis=0, keepdims=True))
        probs = (powers / jnp.sum(powers, axis=0, keepdims=True)).astype(BF16)
        mixed_ref[0, :, cols] = dot(probs, v_ref[0, :, cols], TN).astype(BF16)

    @pl.when(pl.program_id(0) == seqs - 1)
    def _():
        finish_all(loads)


def attend(lay, x, small, weights, cosine, sine, pos, cap, call_id, hauls):
    seqs, count = x.shape[:2]
    width = lay.nc * small.shape[-1]
    heads = 2 * weights[0].shape[-1]
    picked = lay.experts * cap
    hauls = Hauls(lay, hauls)
    per_seq = lambda i: (i, 0, 0)
    once = pl.Buffered(1)
    weight_specs = [
        pl.BlockSpec(w.shape, lambda i, n=w.ndim: (0,) * n, pipeline_mode=once) for w in weights
    ]
    results = [
        ((count, width), BF16),
        ((picked, heads), BF16),
        ((count, heads), BF16),
        ((count, heads), BF16),
        ((picked, heads), BF16),
        ((count, picked), BF16),
        ((1, picked), F32),
        ((picked, 1), F32),
    ]
    return pl.pallas_call(
        functools.partial(attend_body, lay.sizes, lay.rep, hauls),
        grid=(seqs,),
        in_specs=[
            pl.BlockSpec((1, count, width), per_seq),
            pl.BlockSpec((1, count, DH), lambda i: (i, 0, width // DH)),
            pl.BlockSpec(small.shape, lambda i: (0, 0, 0)),
            *weight_specs,
            pl.BlockSpec((count, DH), lambda i: (0, 0)),
            pl.BlockSpec((count, DH), lambda i: (0, 0)),
            pl.BlockSpec((count, 1), lambda i: (0, 0)),
        ]
        + hauls.in_specs,
        out_specs=[pl.BlockSpec((1,) + dims, per_seq) for dims, _ in results] + hauls.out_specs,
        out_shape=[jax.ShapeDtypeStruct((seqs,) + dims, kind) for dims, kind in results]
        + hauls.shapes,
        scratch_shapes=hauls.scratch,
        compiler_params=params(call_id),
        name="attend",
    )(x, x, small, *weights, cosine, sine, pos, *hauls.operands)


def experts_body(lay_sizes, rep, experts, hauls, *refs):
    nf, nc, nt, seqs = lay_sizes
    ins, outs, scratch, loads = hauls.split(refs, 10, 4)
    n_ref, g_ref, small_ref, other_ref, gate0, up0, gate1, up1, down0, down1 = ins
    ge_ref, hidden_ref, gate_ref, up_ref = outs
    late, late_sem = scratch
    greet(nf, nc, nt)
    start_all(loads)
    c = lax.axis_index("ctx")
    lanes = lax.broadcasted_iota(jnp.int32, (1, small_ref.shape[1]), 1) - (2 + experts)

    @pl.loop(0, seqs)
    def _(slot):
        logits = chunk_dot(n_ref.at[slot], small_ref, None, NT)
        mine = jnp.sum(jnp.where(lanes == c // rep, logits, 0.0), axis=-1, keepdims=True)
        theirs = jnp.where(lanes.astype(F32) == other_ref[slot], logits, 0.0)
        theirs = jnp.sum(theirs, axis=-1, keepdims=True)
        ge_ref[slot] = (jax.nn.sigmoid(mine - theirs) * g_ref[slot].astype(F32)).astype(BF16)
        for side, (gate_weight, up_weight) in enumerate(((gate0, up0), (gate1, up1))):
            gate_pre = chunk_dot(n_ref.at[slot], gate_weight, None, NT)
            up_pre = chunk_dot(n_ref.at[slot], up_weight, None, NT)
            sigmoid_gate = jax.nn.sigmoid(gate_pre)
            silu_gate = gate_pre * sigmoid_gate
            silu_slope = sigmoid_gate + silu_gate * (1.0 - sigmoid_gate)
            hidden_ref[side, slot] = (silu_gate * up_pre).astype(BF16)
            gate_ref[side, slot] = (up_pre * silu_slope).astype(BF16)
            up_ref[side, slot] = silu_gate.astype(BF16)

    finish_all(loads)
    copies = [
        pltpu.make_async_copy(loads[0].outs[side], late.at[side], late_sem.at[side])
        for side in range(2)
    ]
    for copy in copies:
        copy.start()
    for copy in copies:
        copy.wait()
    half = late.shape[-1]

    @pl.loop(0, seqs)
    def _(slot):
        for side, early in enumerate((down0, down1)):
            grad_hidden = 0.0
            for s in range(nc):
                for at, weight in ((0, early[s]), (half, late[side, s])):
                    first = 2 * half * s + at
                    term = dot(ge_ref[slot, :, first : first + half], weight, NT)
                    grad_hidden = grad_hidden + term
            gate_ref[side, slot] = (grad_hidden * gate_ref[side, slot].astype(F32)).astype(BF16)
            up_ref[side, slot] = (grad_hidden * up_ref[side, slot].astype(F32)).astype(BF16)


def experts_apply(lay, n2, g, small, other, weights, call_id, haul):
    seqs, count, width = n2.shape
    ff = weights[0].shape[-2]
    hauls = Hauls(lay, [haul])
    in_vmem = pl.BlockSpec(memory_space=pltpu.VMEM)
    return pl.pallas_call(
        functools.partial(experts_body, lay.sizes, lay.rep, lay.experts, hauls),
        in_specs=[in_vmem] * 10 + hauls.in_specs,
        out_specs=[in_vmem] * 4 + hauls.out_specs,
        out_shape=[jax.ShapeDtypeStruct(n2.shape, BF16)]
        + [jax.ShapeDtypeStruct((2, seqs, count, ff), BF16)] * 3
        + hauls.shapes,
        scratch_shapes=[
            pltpu.VMEM((2,) + hauls.shapes[0].shape, BF16),
            pltpu.SemaphoreType.DMA((2,)),
        ]
        + hauls.scratch,
        compiler_params=params(call_id),
        name="experts",
    )(n2, g, small, other, *weights, *hauls.operands)


def core_exchange(refs, nt):
    away, came, send_sem, recv_sem = refs

    def copy(s):
        return pltpu.make_async_remote_copy(
            src_ref=away.at[s],
            dst_ref=came.at[s],
            send_sem=send_sem.at[s],
            recv_sem=recv_sem.at[s],
            device_id={"tp": lax.rem(lax.axis_index("tp") + 1, nt)},
            device_id_type=MESH,
        )

    return copy


def greet_core(nt):
    barrier = pltpu.get_barrier_semaphore()
    other = lax.rem(lax.axis_index("tp") + 1, nt)
    pl.semaphore_signal(barrier, inc=1, device_id={"tp": other}, device_id_type=MESH)
    pl.semaphore_wait(barrier, 1)


def mlp_grads_body(nc, nt, n_ref, ge_ref, hidden_ref, gate_ref, up_ref, *refs):
    out, (away, came) = refs[0], refs[1:3]
    copy = core_exchange(refs[1:], nt)
    ff, wide = away.shape[-2:]
    pairs = ((gate_ref, n_ref), (up_ref, n_ref), (hidden_ref, ge_ref))
    greet_core(nt)

    @pl.loop(0, nc)
    def _(s):
        columns = pl.ds(pl.multiple_of(s * wide, wide), wide)
        for i, (left, right) in enumerate(pairs):
            away[s, i] = dot(left[1], right[:, columns], TN).astype(BF16)
        copy(s).start()

    @pl.loop(0, nc)
    def _(s):
        columns = pl.ds(pl.multiple_of(s * wide, wide), wide)
        copy(s).wait_recv()
        for i, (left, right) in enumerate(pairs):
            own = dot(left[0], right[:, columns], TN)
            out[s, i * ff : (i + 1) * ff] = (own + came[s, i].astype(F32)).astype(BF16)

    @pl.loop(0, nc)
    def _(s):
        copy(s).wait_send()


def mlp_grads(lay, n2, ge, hidden, gate, up, call_id):
    width, ff, nc = n2.shape[1], hidden.shape[-1], lay.nc
    piece = (3, ff, width // nc)
    in_vmem = pl.BlockSpec(memory_space=pltpu.VMEM)
    return pl.pallas_call(
        functools.partial(mlp_grads_body, nc, lay.nt),
        in_specs=[in_vmem] * 5,
        out_specs=in_vmem,
        out_shape=jax.ShapeDtypeStruct((nc, 3 * ff, width // nc), BF16),
        scratch_shapes=[
            pltpu.VMEM((nc,) + piece, BF16),
            pltpu.VMEM((nc,) + piece, BF16),
            pltpu.SemaphoreType.DMA((nc,)),
            pltpu.SemaphoreType.DMA((nc,)),
        ],
        compiler_params=params(call_id),
        name="mlp_grads",
    )(n2, ge, hidden, gate, up)


def attn_grads_body(lay_sizes, hauls, *refs):
    nf, nc, nt, seqs = lay_sizes
    (x_ref, d_ref, g_ref, mixed_ref), outs, scratch, loads = hauls.split(refs, 4, 4)
    kept, away, came = scratch[:3]
    copy = core_exchange(scratch[1:], nt)
    wide, half = away.shape[-2:]
    greet(nf, nc, nt)
    start_all(loads)

    @pl.loop(0, nc)
    def _(s):
        columns = pl.ds(pl.multiple_of(s * wide, wide), wide)
        first = dot(x_ref[:, columns], d_ref[...], TN)
        last = dot(g_ref[:, columns], mixed_ref[...], TN)
        for i in range(4):
            part, at = (first, i) if i < 3 else (last, 0)
            step = 3 if i < 3 else 1
            kept[s, i] = part[:, at * half : (at + 1) * half]
            away[s, i] = part[:, (step + at) * half : (step + at + 1) * half].astype(BF16)
        copy(s).start()

    @pl.loop(0, nc)
    def _(s):
        copy(s).wait_recv()
        for i in range(4):
            outs[i][s] = (kept[s, i] + came[s, i].astype(F32)).astype(BF16)

    @pl.loop(0, nc)
    def _(s):
        copy(s).wait_send()

    finish_all(loads)


def attn_grads(lay, x, grads, g, mixed, call_id, hauls):
    width, heads, nc = x.shape[1], mixed.shape[-1], lay.nc
    piece = (width // nc, heads // 2)
    hauls = Hauls(lay, hauls)
    in_vmem = pl.BlockSpec(memory_space=pltpu.VMEM)
    return pl.pallas_call(
        functools.partial(attn_grads_body, lay.sizes, hauls),
        in_specs=[in_vmem] * 4 + hauls.in_specs,
        out_specs=[in_vmem] * 4 + hauls.out_specs,
        out_shape=[jax.ShapeDtypeStruct((nc,) + piece, BF16)] * 4 + hauls.shapes,
        scratch_shapes=[
            pltpu.VMEM((nc, 4) + piece, F32),
            pltpu.VMEM((nc, 4) + piece, BF16),
            pltpu.VMEM((nc, 4) + piece, BF16),
            pltpu.SemaphoreType.DMA((nc,)),
            pltpu.SemaphoreType.DMA((nc,)),
        ]
        + hauls.scratch,
        compiler_params=params(call_id),
        name="attn_grads",
    )(x, grads, g, mixed, *hauls.operands)


def attend_back_body(lay_sizes, hauls, *refs):
    nf, nc, nt, seqs = lay_sizes
    ins, (out_ref,), scratch, loads = hauls.split(refs, 11, 1)
    q_ref, k_ref, v_ref, g_ref, wo0, wo1, qpos_ref, kpos_ref, cosine, sine, put = ins

    @pl.when(pl.program_id(0) == 0)
    def _():
        greet(nf, nc, nt)
        start_all(loads)

    scale = 1.0 / math.sqrt(DH)
    seen = kpos_ref[...] <= qpos_ref[0]
    half = wo0.shape[-1]
    for side, weight in enumerate((wo0, wo1)):
        grad_mixed = chunk_dot(g_ref.at[0], weight).astype(BF16)
        for h in range(half // DH):
            cols = slice(side * half + h * DH, side * half + (h + 1) * DH)
            q, k, v = q_ref[0, :, cols], k_ref[0, :, cols], v_ref[0, :, cols]
            g = grad_mixed[:, h * DH : (h + 1) * DH]
            scores = jnp.where(seen, dot(k, q, NT) * scale, MASKED)
            powers = jnp.exp(scores - jnp.max(scores, axis=0, keepdims=True))
            probs = powers / jnp.sum(powers, axis=0, keepdims=True)
            grad_probs = dot(v, g, NT)
            centre = jnp.sum(probs * grad_probs, axis=0, keepdims=True)
            grad_scores = (probs * (grad_probs - centre)).astype(BF16)

            def at(part):
                first = (3 * side + part) * half + h * DH
                return slice(first, first + DH)

            out_ref[0, :, at(2)] = dot(probs.astype(BF16), g).astype(BF16)
            dk = dot(grad_scores, q) * scale
            out_ref[0, :, at(1)] = turn(dk, cosine[...], -sine[...]).astype(BF16)
            dq = dot(grad_scores, k, TN) * scale
            high = dq.astype(BF16)
            low = (dq - high.astype(F32)).astype(BF16)
            dq = dot(put[0], high) + dot(put[0], low)
            out_ref[0, :, at(0)] = turn(dq, cosine[...], -sine[...]).astype(BF16)

    @pl.when(pl.program_id(0) == seqs - 1)
    def _():
        finish_all(loads)


def attend_back(lay, q, k, v, g, weights, qpos, kpos, cosine, sine, put, call_id, hauls):
    seqs, count, heads = q.shape
    width = g.shape[-1]
    length = k.shape[1]
    hauls = Hauls(lay, hauls)
    per_seq = lambda s: (s, 0, 0)
    once = lambda s: (0, 0)
    return pl.pallas_call(
        functools.partial(attend_back_body, lay.sizes, hauls),
        grid=(seqs,),
        in_specs=[
            pl.BlockSpec((1, count, heads), per_seq),
            pl.BlockSpec((1, length, heads), per_seq),
            pl.BlockSpec((1, length, heads), per_seq),
            pl.BlockSpec((1, count, width), per_seq),
            pl.BlockSpec(weights[0].shape, lambda s: (0, 0, 0)),
            pl.BlockSpec(weights[1].shape, lambda s: (0, 0, 0)),
            pl.BlockSpec((1, 1, count), per_seq),
            pl.BlockSpec((length, 1), once),
            pl.BlockSpec((length, DH), once),
            pl.BlockSpec((length, DH), once),
            pl.BlockSpec((1, length, count), per_seq),
        ]
        + hauls.in_specs,
        out_specs=[pl.BlockSpec((1, length, 3 * heads), per_seq)] + hauls.out_specs,
        out_shape=[jax.ShapeDtypeStruct((seqs, length, 3 * heads), BF16)] + hauls.shapes,
        scratch_shapes=hauls.scratch,
        compiler_params=params(call_id),
        name="attend_back",
    )(q, k, v, g, *weights, qpos, kpos, cosine, sine, put, *hauls.operands)


def unpack_body(bounds, *refs):
    gate_up, down = refs[-2:]
    ff = down.shape[1]
    for part, first, last in zip(refs, bounds, bounds[1:]):
        for i in range(3):
            low, high = max(first, i * ff), min(last, (i + 1) * ff)
            if low < high:
                total = jnp.sum(part[:, low - first : high - first].astype(F32), axis=0)
                if i < 2:
                    gate_up[0, i, low - i * ff : high - i * ff] = total
                else:
                    down[0, low - i * ff : high - i * ff] = total


def unpack(lay, parts, bounds):
    ff, wide = bounds[-1] // 3, parts[0].shape[2]
    experts, rep = lay.experts, lay.rep
    return pl.pallas_call(
        functools.partial(unpack_body, bounds),
        grid=(experts,),
        in_specs=[pl.BlockSpec((rep,) + p.shape[1:], lambda e: (e, 0, 0)) for p in parts],
        out_specs=[
            pl.BlockSpec((1, 2, ff, wide), lambda e: (e, 0, 0, 0)),
            pl.BlockSpec((1, ff, wide), lambda e: (e, 0, 0)),
        ],
        out_shape=[
            jax.ShapeDtypeStruct((experts, 2, ff, wide), F32),
            jax.ShapeDtypeStruct((experts, ff, wide), F32),
        ],
        compiler_params=pltpu.CompilerParams(vmem_limit_bytes=VMEM_LIMIT),
        name="unpack",
    )(*parts)


def row_of(small_ref, line):
    planes = [small_ref[s, line : line + 1] for s in range(small_ref.shape[0])]
    return jnp.concatenate(planes, axis=1).astype(F32)


def choices(ids, expert, experts, cap):
    rows = ids.shape[0]
    before = lax.broadcasted_iota(jnp.int32, (rows, rows), 1)
    before = (before < lax.broadcasted_iota(jnp.int32, (rows, rows), 0)).astype(BF16)
    lanes = lax.broadcasted_iota(jnp.int32, (rows, DH), 1).astype(F32)
    member = jnp.where(jnp.logical_or(ids[:, 0:1] == lanes, ids[:, 1:2] == lanes), 1.0, 0.0)
    ranks = dot(before, member.astype(BF16))
    columns = lax.broadcasted_iota(jnp.int32, (rows, experts * cap), 1).astype(F32)
    maps = []
    for slot in range(2):
        chosen = ids[:, slot : slot + 1]
        rank = jnp.sum(jnp.where(lanes == chosen, ranks, 0.0), axis=-1, keepdims=True)
        ahead = chosen - expert.astype(F32)
        ahead = jnp.where(ahead < 0.0, ahead + experts, ahead)
        maps.append(jnp.where(columns == ahead * cap + rank, 1.0, 0.0).astype(BF16))
    return maps


def slot_gates(normed, small_ref, ids, first):
    planes, lines, wide = small_ref.shape
    logits = 0.0
    for s in range(planes):
        logits = logits + dot(normed[:, s * wide : (s + 1) * wide], small_ref[s], NT)
    lanes = lax.broadcasted_iota(jnp.int32, logits.shape, 1).astype(F32)
    picked = [
        jnp.sum(jnp.where(lanes == ids[:, k : k + 1] + first, logits, 0.0), axis=-1, keepdims=True)
        for k in range(2)
    ]
    return jax.nn.sigmoid(picked[0] - picked[1]), jax.nn.sigmoid(picked[1] - picked[0])


def norm_of(values, gain):
    inverse = lax.rsqrt(jnp.mean(values * values, axis=-1, keepdims=True) + EPSILON)
    scaled = values * inverse
    return inverse, scaled, (scaled * gain).astype(BF16)


def norm_back(grad, gain, inverse, scaled):
    turned = grad * gain
    return inverse * (turned - scaled * jnp.mean(turned * scaled, axis=-1, keepdims=True))


def logits_back(gates, choice, ids, first):
    mean = gates[0] * choice[0] + gates[1] * choice[1]
    lanes = lax.broadcasted_iota(jnp.int32, (ids.shape[0], DH), 1).astype(F32)
    out = 0.0
    for k in range(2):
        inner = gates[k] * (choice[k] - mean)
        out = out + jnp.where(lanes == ids[:, k : k + 1] + first, inner, 0.0)
    return out


def exact_tn(left, right):
    total = 0.0
    for _ in range(3):
        part = left.astype(BF16)
        total = total + dot(part, right, TN)
        left = left - part.astype(F32)
    return total


def owner_forward_body(rep, experts, x_ref, ids_ref, small_ref, rows_ref, residual_ref, out_ref):
    expert = lax.axis_index("ctx") // rep
    cap = rows_ref.shape[0] // experts
    ids = ids_ref[...]
    x = x_ref[...].astype(F32)
    normed_one = norm_of(x, row_of(small_ref, 0))[2]
    gates = slot_gates(normed_one, small_ref, ids[:, 0:2], 2)
    maps = choices(ids[:, 0:2], expert, experts, cap)
    residual = x + (gates[0] * dot(maps[0], rows_ref[...]) + gates[1] * dot(maps[1], rows_ref[...]))
    residual_ref[...] = residual
    normed_two = norm_of(residual, row_of(small_ref, 1))[2]
    maps = choices(ids[:, 2:4], expert, experts, cap)
    out_ref[...] = dot(maps[0] + maps[1], normed_two, TN).astype(BF16)


def owner_middle_body(rep, experts, *refs):
    x_ref, ids_ref, small_ref, up_ref, residual_ref, branch_ref, expert_ref, grad_ref = refs[:8]
    layer_ref, grad_res_ref, out_ref, logits_ref, terms_ref = refs[8:]
    expert = lax.axis_index("ctx") // rep
    cap = branch_ref.shape[0] // experts
    ids = ids_ref[...]
    upstream, residual = up_ref[...].astype(F32), residual_ref[...]
    gain_two = row_of(small_ref, 1)
    inverse_two, scaled_two, normed_two = norm_of(residual, gain_two)
    gates = slot_gates(normed_two, small_ref, ids[:, 2:4], 2 + experts)
    maps = choices(ids[:, 2:4], expert, experts, cap)
    choice, total = [], 0.0
    for k in range(2):
        expert_out = dot(maps[k], expert_ref[...])
        choice.append(jnp.sum(upstream * expert_out, axis=-1, keepdims=True))
        total = total + gates[k] * expert_out
    layer_ref[...] = (residual + total).astype(BF16)
    logits_two = logits_back(gates, choice, ids[:, 2:4], 2 + experts)
    grad = dot(maps[0] + maps[1], grad_ref[...])
    for e in range(experts):
        line = 2 + experts + e
        grad = grad + logits_two[:, line : line + 1] * row_of(small_ref, line)
    grad_res = upstream + norm_back(grad, gain_two, inverse_two, scaled_two)
    grad_res_ref[...] = grad_res
    gain_grad = jnp.sum(grad * scaled_two, axis=0, keepdims=True)
    normed_one = norm_of(x_ref[...].astype(F32), row_of(small_ref, 0))[2]
    gates = slot_gates(normed_one, small_ref, ids[:, 0:2], 2)
    maps = choices(ids[:, 0:2], expert, experts, cap)
    choice, out = [], 0.0
    for k in range(2):
        branch = dot(maps[k], branch_ref[...])
        choice.append(jnp.sum(grad_res * branch, axis=-1, keepdims=True))
        out = out + dot(maps[k], (gates[k] * grad_res).astype(BF16), TN)
    out_ref[...] = out.astype(BF16)
    logits_one = logits_back(gates, choice, ids[:, 0:2], 2)
    logits_ref[...] = logits_one
    lines = terms_ref.shape[0]
    terms = exact_tn(logits_one, normed_one) + exact_tn(logits_two, normed_two)
    place = lax.broadcasted_iota(jnp.int32, terms_ref.shape, 0)
    terms_ref[...] = jnp.where(place == 1, gain_grad, terms[:lines])


def owner_back_body(experts, x_ref, small_ref, rows_ref, logits_ref, grad_res_ref, layer_ref, terms_ref, both_ref, out_ref):
    gain = row_of(small_ref, 0)
    inverse, scaled, _ = norm_of(x_ref[...].astype(F32), gain)
    grad = 0.0
    for j in range(rows_ref.shape[0]):
        grad = grad + rows_ref[j].astype(F32)
    for e in range(experts):
        grad = grad + logits_ref[:, 2 + e : 3 + e] * row_of(small_ref, 2 + e)
    both_ref[0] = layer_ref[...]
    both_ref[1] = (grad_res_ref[...] + norm_back(grad, gain, inverse, scaled)).astype(BF16)
    gain_grad = jnp.sum(grad * scaled, axis=0, keepdims=True)
    place = lax.broadcasted_iota(jnp.int32, terms_ref.shape, 0)
    terms = jnp.where(place == 0, gain_grad, terms_ref[...])
    planes, chips, _, part = out_ref.shape
    for plane in range(planes):
        for chip in range(chips):
            first = (chip * planes + plane) * part
            out_ref[plane, chip] = terms[:, first : first + part]


def own_kernel(body, name, results, *operands):
    in_vmem = pl.BlockSpec(memory_space=pltpu.VMEM)
    return pl.pallas_call(
        body,
        in_specs=[in_vmem] * len(operands),
        out_specs=[in_vmem] * len(results),
        out_shape=[jax.ShapeDtypeStruct(dims, kind) for dims, kind in results],
        compiler_params=pltpu.CompilerParams(vmem_limit_bytes=VMEM_LIMIT),
        name=name,
    )(*operands)


def ranks_of(member):
    count = member.shape[-1]
    before = (jnp.arange(count)[:, None] < jnp.arange(count)[None, :]).astype(BF16)
    return jnp.einsum("...m,mn->...n", member.astype(BF16), before, preferred_element_type=F32)


def pick_maps(ids, expert, cap):
    member = jnp.any(ids == expert[..., None, None], axis=-1)
    rank = ranks_of(member).astype(jnp.int32)
    place = jnp.arange(cap, dtype=jnp.int32)[:, None]
    return jnp.logical_and(member[..., None, :], rank[..., None, :] == place)


def per_device(
    tokens,
    cotangent,
    attn_ids,
    mlp_ids,
    span_ids,
    attn_gain,
    attn_router,
    kv_weight,
    query_weight,
    output_weight,
    mlp_gain,
    mlp_router,
    gate_up_weight,
    down_weight,
):
    experts = query_weight.shape[0]
    lay = Layout(experts)
    nf, nc, rep, seqs = lay.nf, lay.nc, lay.rep, lay.seqs
    rows, width = tokens.shape
    cap = 3 * rows // 4
    expert = lay.c // rep

    def to_planes(array, index_of, both=False):
        index = index_of(0)
        shape = array.shape[len(index) :]
        return Haul(array, lambda ref, d: ref.at[index_of(d)] if index else ref, shape, both)

    expert_of = (expert + jnp.arange(experts)) % experts
    pick_own_m = pick_maps(jnp.broadcast_to(mlp_ids, (experts, rows, 2)), expert_of, cap)

    def dispatch(pick, values):
        return jnp.einsum(
            "jrn,nd->jrd", pick.astype(BF16), values, preferred_element_type=F32
        ).astype(BF16)

    ids = jnp.concatenate([attn_ids, mlp_ids], axis=1).astype(BF16)
    payload = jnp.concatenate([tokens, jnp.pad(ids, ((0, 0), (0, 124)))], axis=1)
    small = jnp.concatenate([attn_gain[None], mlp_gain[None], attn_router.T, mlp_router.T])
    small = jnp.pad(small, ((0, -small.shape[0] % 16), (0, 0)))
    g_own = dispatch(pick_own_m, cotangent)
    by_plane = lambda *more: lambda d: (d // rep,) + more
    x_all, small_all, g_mine, _, q_own, q_sib, kv_own, kv_sib = opening(
        lay,
        payload,
        small,
        g_own,
        1,
        [to_planes(query_weight, by_plane(), True), Relay(kv_weight)],
    )
    gate_up_turned = gate_up_weight.swapaxes(-1, -2)
    down_turned = down_weight.swapaxes(-1, -2)

    own_ids = ids.astype(F32)

    half_len = rows // 2
    offsets = jnp.arange(rows, dtype=jnp.int32)
    pos = jnp.where(
        offsets[None, :] < half_len,
        span_ids[:, 0:1] * half_len + offsets[None, :],
        span_ids[:, 1:2] * half_len + offsets[None, :] - half_len,
    )
    pos = pos.astype(F32).reshape(-1, 1)
    freqs = ROPE_BASE ** (-jnp.arange(DH // 2, dtype=F32) / (DH // 2))

    cosine, sine = jnp.cos(pos * freqs), jnp.sin(pos * freqs)
    cosine = jnp.concatenate([cosine, cosine], axis=-1)
    sine = jnp.concatenate([-sine, sine], axis=-1)

    normed_all, q, k, v, mixed, put, pos_q, other, o_own, o_sib, gate_own, gate_sib, g_blocks = attend(
        lay,
        x_all.reshape(seqs, nc * rows, -1),
        small_all,
        [q_own, q_sib, kv_own, kv_sib],
        cosine,
        sine,
        pos,
        cap,
        9,
        [
            to_planes(output_weight, by_plane(), True),
            to_planes(gate_up_turned, by_plane(0), True),
            Share(lay, g_mine),
        ],
    )
    g_blocks = g_blocks.reshape(seqs, experts * cap, width)
    heads = q.shape[-1]
    half = heads // 2
    branch_rows, up_own, up_sib = collect(
        lay,
        [mixed[None]],
        [o_own, o_sib],
        [((0, 0, 0, half, 0, None), (0, 0, half, half, 1, None))],
        rep,
        experts,
        2,
        hauls=[to_planes(gate_up_turned, by_plane(1), True)],
    )
    branch_rows = branch_rows.reshape(-1, width)
    residual, n2_own = own_kernel(
        functools.partial(owner_forward_body, rep, experts),
        "owner_forward",
        [((rows, width), F32), ((experts * cap, width), BF16)],
        tokens,
        own_ids,
        small_all,
        branch_rows,
    )

    wide, ff = width // nc, down_turned.shape[1]

    def down_columns(half):
        columns = pl.ds(half * (wide // 2), wide // 2)
        return Haul(
            down_turned, lambda ref, d: ref.at[d // rep, :, columns], (ff, wide // 2), True
        )

    n2, first_own, first_sib = spread(
        lay,
        n2_own.reshape(experts, cap, width),
        rep,
        3,
        [down_columns(0)],
    )
    n2 = n2.reshape(seqs, experts * cap, width)
    grad_expert, hidden, grad_gate, grad_up, second_own, second_sib = experts_apply(
        lay,
        n2,
        g_blocks,
        small_all,
        other,
        [gate_own, up_own, gate_sib, up_sib, first_own, first_sib],
        12,
        down_columns(1),
    )
    mlp_back = mlp_grads(
        lay,
        n2.reshape(-1, width),
        grad_expert.reshape(-1, width),
        *(a.reshape(2, -1, ff) for a in (hidden, grad_gate, grad_up)),
        4,
    )
    shares = (480, 352, 432, 464, 384)
    bounds = [0]
    for share in shares:
        bounds.append(bounds[-1] + share)
    bounds = [3 * ff * bound // bounds[-1] // 16 * 16 for bound in bounds]

    def carried(n):
        first, last = bounds[n : n + 2]
        rows_of = lambda ref, d: ref.at[d, pl.ds(first, last - first)]
        return Haul(mlp_back, rows_of, (last - first, wide))

    by_piece = lambda d: (d,)
    expert_rows, grad_rows, back_a = collect(
        lay,
        [hidden, grad_gate, grad_up],
        [gate_own, up_own, first_own, second_own, gate_sib, up_sib, first_sib, second_sib],
        [
            tuple((0, side, 0, ff, (4 * side + 2, 4 * side + 3), None) for side in range(2)),
            tuple((1 + i, side, 0, ff, 4 * side + i, None) for side in range(2) for i in range(2)),
        ],
        rep,
        experts,
        5,
        NN,
        [carried(0)],
    )
    lines = -(-(2 + 2 * experts) // 16) * 16
    layer_out, grad_residual, gb_own, logits_one, terms = own_kernel(
        functools.partial(owner_middle_body, rep, experts),
        "owner_middle",
        [
            ((rows, width), BF16),
            ((rows, width), F32),
            ((experts * cap, width), BF16),
            ((rows, DH), F32),
            ((lines, width), F32),
        ],
        tokens,
        own_ids,
        small_all,
        cotangent,
        residual,
        branch_rows,
        expert_rows.reshape(-1, width),
        grad_rows.reshape(-1, width),
    )

    gb, back_b = spread(lay, gb_own.reshape(experts, cap, width), rep, 6, [carried(1)])
    gb = gb.reshape(seqs, experts * cap, width)
    dqkv, back_c = attend_back(
        lay,
        q,
        k,
        v,
        gb,
        [o_own, o_sib],
        pos_q,
        pos,
        cosine,
        sine,
        put,
        11,
        [carried(2)],
    )
    q_grads, k_grads, v_grads, o_grads, back_d = attn_grads(
        lay,
        normed_all.reshape(-1, width),
        dqkv.reshape(-1, 3 * heads),
        gb.reshape(-1, width),
        mixed.reshape(-1, heads),
        10,
        [carried(3)],
    )
    grad_one_rows, back_e, o_back, q_back = collect(
        lay,
        [dqkv[None]],
        [q_own, kv_own, q_sib, kv_sib],
        [
            tuple(
                (0, 0, (3 * s + i) * half, half, 2 * s + (i > 0), None if i == 0 else i - 1)
                for i in range(3)
                for s in range(2)
            )
        ],
        1,
        nc,
        7,
        hauls=[carried(4), to_planes(o_grads, by_piece), to_planes(q_grads, by_piece)],
        by_plane=True,
    )

    both, terms = own_kernel(
        functools.partial(owner_back_body, experts),
        "owner_back",
        [((2, rows, width), BF16), ((nc, nf, lines, width // (nf * nc)), F32)],
        tokens,
        small_all,
        grad_one_rows,
        logits_one,
        grad_residual,
        layer_out,
        terms,
    )
    terms, both_out, k_back, v_back = finish(
        lay, terms, both, 8, [to_planes(grads, by_piece) for grads in (k_grads, v_grads)]
    )
    layer_out, grad_tokens = both_out[0], both_out[1]

    def by_expert(came):
        out = came.astype(F32)
        if rep > 1:
            out = jnp.sum(out.reshape((experts, rep) + out.shape[1:]), axis=1)
        return out

    grad_query_weight, grad_output_weight = by_expert(q_back), by_expert(o_back)
    grad_kv_weight = jnp.stack([jnp.sum(g.astype(F32), axis=0) for g in (k_back, v_back)])
    grad_gate_up, grad_down = unpack(lay, [back_a, back_b, back_c, back_d, back_e], bounds)
    grad_gate_up, grad_down = grad_gate_up.swapaxes(-1, -2), grad_down.swapaxes(-1, -2)
    return (
        layer_out,
        grad_tokens,
        terms[0],
        terms[2 : 2 + experts].T,
        grad_kv_weight,
        grad_query_weight,
        grad_output_weight,
        terms[1],
        terms[2 + experts : 2 + 2 * experts].T,
        grad_gate_up,
        grad_down,
    )


def solution(mesh):
    placed = (
        P(("fsdp", "ctx"), None),
        P(("fsdp", "ctx"), None),
        P(("fsdp", "ctx"), None),
        P(("fsdp", "ctx"), None),
        P(),
        P("ctx"),
        P("ctx", None),
        P(None, "ctx", ("fsdp", "tp")),
        P(None, "ctx", ("fsdp", "tp")),
        P(None, "ctx", ("fsdp", "tp")),
        P("ctx"),
        P("ctx", None),
        P(None, None, "ctx", ("fsdp", "tp")),
        P(None, "ctx", ("fsdp", "tp")),
    )
    return jax.shard_map(
        per_device,
        mesh=mesh,
        in_specs=placed,
        out_specs=(
            P(("fsdp", "ctx"), None),
            P(("fsdp", "ctx"), None),
            P(("fsdp", "ctx")),
            P(("fsdp", "ctx"), None),
            P(None, "ctx", ("fsdp", "tp")),
            P(None, "ctx", ("fsdp", "tp")),
            P(None, "ctx", ("fsdp", "tp")),
            P(("fsdp", "ctx")),
            P(("fsdp", "ctx"), None),
            P(None, None, "ctx", ("fsdp", "tp")),
            P(None, "ctx", ("fsdp", "tp")),
        ),
        check_vma=False,
    )
```

```python
import functools
import math

import jax
import jax.numpy as jnp
from jax import lax
from jax.experimental import pallas as pl
from jax.experimental.pallas import tpu as pltpu
from jax.sharding import PartitionSpec as P

DH = 128
EPSILON = 1e-06
ROPE_BASE = 10000.0
MASKED = -1e30
HIGH = lax.Precision.HIGHEST
MESH = pl.DeviceIdType.MESH
AXES = ("fsdp", "ctx", "tp")
F32 = jnp.float32
BF16 = jnp.bfloat16
VMEM_LIMIT = 60 * 1024 * 1024
NT = (((1,), (1,)), ((), ()))
NN = (((1,), (0,)), ((), ()))
TN = (((0,), (0,)), ((), ()))


def dot(a, b, dims=NN):
    return lax.dot_general(a, b, dims, preferred_element_type=F32)


class Layout:
    def __init__(self, experts):
        self.nf = lax.axis_size("fsdp")
        self.nc = lax.axis_size("ctx")
        self.nt = lax.axis_size("tp")
        self.experts = experts
        self.rep = self.nc // experts
        self.seqs = self.nf // self.nt
        self.f = lax.axis_index("fsdp")
        self.c = lax.axis_index("ctx")
        self.t = lax.axis_index("tp")
        self.home = self.t == self.f // self.seqs
        self.sizes = (self.nf, self.nc, self.nt, self.seqs)

    def flat(self, f, c, t):
        return (f * self.nc + c) * self.nt + t


def home_pairs(lay, move):
    pairs = []
    for f in range(lay.nf):
        t = f // lay.seqs
        for c in range(lay.nc):
            f2, c2 = move(f, c)
            pairs.append((lay.flat(f, c, t), lay.flat(f2, c2, t)))
    return pairs


def collect_permute(lay, block_of, blocks, stride):
    got, last = [], None
    for j in range(blocks):
        partial = block_of(j, last)
        zeros = jnp.zeros((lay.nf,) + partial.shape[1:], partial.dtype)
        full = lax.dynamic_update_slice_in_dim(zeros, partial, lay.t * lay.seqs, 0)
        last = lax.psum_scatter(full, "fsdp", scatter_dimension=0, tiled=True)[0]
        if j > 0:
            pairs = home_pairs(lay, lambda f, c: (f, (c - stride * j) % lay.nc))
            last = lax.ppermute(last, AXES, pairs)
        got.append(last)
    return jnp.stack(got)


class Haul:
    def __init__(self, array, piece=None, shape=None, both=False):
        self.array, self.piece, self.both = array, piece, both
        self.shape = array.shape if shape is None else shape

    def out_shapes(self, nc):
        dims = self.shape if self.piece is None else (nc,) + self.shape
        return [jax.ShapeDtypeStruct(dims, self.array.dtype)] * (2 if self.both else 1)

    def scratch(self, nc):
        return [pltpu.SemaphoreType.DMA((nc,))] * (4 if self.both else 2)

    def bind(self, place, src, outs, sems):
        load = Load()
        load.piece, load.both, load.place = self.piece, self.both, place
        load.src, load.outs, load.sems = src, outs, sems
        return load


def by_gap(at, size, gaps):
    order = []
    for gap in dict.fromkeys(gap for gap in gaps if gap > 0):
        order += [(gap, at - gap >= 0), (size - gap, at + gap < size)]
    return order


def start_order(size):
    return [size - 1, *range(1, size - 1)]


def wait_order(size):
    return [1, size - 1, *range(2, size - 1)] if size > 1 else []


def ahead_by_gap(at, size):
    return [(size - j, there) for j, there in by_gap(at, size, start_order(size))]


class Load:
    def along_ctx(self, j):
        nc, c, nt, t = self.place
        return pltpu.make_async_remote_copy(
            src_ref=self.piece(self.src, lax.rem(c + j, nc)),
            dst_ref=self.outs[0].at[c],
            send_sem=self.sems[0].at[j],
            recv_sem=self.sems[1].at[j],
            device_id={"ctx": lax.rem(c + j, nc)},
            device_id_type=MESH,
        )

    def landed(self, j):
        nc, c, nt, t = self.place
        here = self.outs[0].at[lax.rem(c - j + nc, nc)]
        return pltpu.make_async_remote_copy(
            src_ref=here,
            dst_ref=here,
            send_sem=self.sems[0].at[j],
            recv_sem=self.sems[1].at[j],
            device_id={"ctx": lax.rem(c + j, nc)},
            device_id_type=MESH,
        )

    def to_core(self, j):
        nc, c, nt, t = self.place
        if self.piece is None:
            src, dst, at = self.src, self.outs[0], 0
        else:
            source = lax.rem(c - j + nc, nc)
            src = self.piece(self.src, c) if j == 0 else self.outs[0].at[source]
            dst, at = self.outs[1].at[source], 2
        return pltpu.make_async_remote_copy(
            src_ref=src,
            dst_ref=dst,
            send_sem=self.sems[at].at[j],
            recv_sem=self.sems[at + 1].at[j],
            device_id={"tp": lax.rem(t + 1, nt)},
            device_id_type=MESH,
        )

    def keep(self):
        nc, c, nt, t = self.place
        return pltpu.make_async_copy(
            self.piece(self.src, c), self.outs[0].at[c], self.sems[0].at[0]
        )

    def start(self):
        if self.piece is None:
            self.to_core(0).start()
            return
        for j, there in ahead_by_gap(self.place[1], self.place[0]):
            pl.when(there)(lambda j=j: self.along_ctx(j).start())
        self.keep().start()
        if self.both:
            self.to_core(0).start()

    def pass_on(self):
        if self.piece is None:
            return
        for j, there in by_gap(self.place[1], self.place[0], wait_order(self.place[0])):

            @pl.when(there)
            def _():
                self.landed(j).wait_recv()
                if self.both:
                    self.to_core(j).start()

    def finish(self):
        if self.piece is None:
            self.to_core(0).wait()
            return
        self.keep().wait()
        for j in range(self.place[0]):
            if j > 0:
                self.along_ctx(j).wait_send()
            if self.both:
                self.to_core(j).wait()


class Relay:
    both = True

    def __init__(self, array):
        self.array = array

    def out_shapes(self, nc):
        return [jax.ShapeDtypeStruct((nc,) + self.array.shape, self.array.dtype)] * 2

    def scratch(self, nc):
        return [pltpu.SemaphoreType.DMA((2, nc))] * 2 + [pltpu.SemaphoreType.DMA((nc,))] * 2

    def bind(self, place, src, outs, sems):
        load = RelayLoad()
        load.place, load.src, load.outs, load.sems = place, src, outs, sems
        return load


def relay_step(place, way, k, src, dst, send_sem, recv_sem):
    nc, c = place[:2]
    step = 1 - 2 * way
    copy = pltpu.make_async_remote_copy(
        src_ref=src,
        dst_ref=dst,
        send_sem=send_sem.at[way, k],
        recv_sem=recv_sem.at[way, k],
        device_id={"ctx": lax.rem(c + step + nc, nc)},
        device_id_type=MESH,
    )
    sent = jnp.logical_and(c - step * k >= 0, c - step * k < nc)
    sent = jnp.logical_and(sent, jnp.logical_and(c + step >= 0, c + step < nc))
    return copy, sent


def relayed(place, way, k):
    nc, c = place[:2]
    source = c - (1 - 2 * way) * k
    return lax.rem(source + nc, nc), jnp.logical_and(source >= 0, source < nc)


class RelayLoad:
    def copy(self, way, k):
        source = relayed(self.place, way, k)[0]
        src = self.src if k == 0 else self.outs[0].at[source]
        return relay_step(self.place, way, k, src, self.outs[0].at[source], *self.sems[:2])

    def arrival(self, way, k):
        source, there = relayed(self.place, way, k)
        here = self.outs[0].at[source]
        return pltpu.make_async_remote_copy(
            src_ref=here,
            dst_ref=here,
            send_sem=self.sems[0].at[way, k],
            recv_sem=self.sems[1].at[way, k - 1],
            device_id={"ctx": lax.rem(self.place[1] + 1, self.place[0])},
            device_id_type=MESH,
        ), there

    def to_core(self, source):
        nc, c, nt, t = self.place
        return pltpu.make_async_remote_copy(
            src_ref=self.outs[0].at[source],
            dst_ref=self.outs[1].at[source],
            send_sem=self.sems[2].at[source],
            recv_sem=self.sems[3].at[source],
            device_id={"tp": lax.rem(t + 1, nt)},
            device_id_type=MESH,
        )

    def own_to_core(self):
        nc, c, nt, t = self.place
        return pltpu.make_async_remote_copy(
            src_ref=self.src,
            dst_ref=self.outs[1].at[c],
            send_sem=self.sems[2].at[c],
            recv_sem=self.sems[3].at[c],
            device_id={"tp": lax.rem(t + 1, nt)},
            device_id_type=MESH,
        )

    def keep(self):
        nc, c = self.place[:2]
        return pltpu.make_async_copy(self.src, self.outs[0].at[c], self.sems[0].at[0, nc - 1])

    def start(self):
        for way in range(2):
            copy, sent = self.copy(way, 0)
            pl.when(sent)(copy.start)
        self.keep().start()
        self.own_to_core().start()

    def pass_on(self):
        nc = self.place[0]
        for k in range(1, nc):
            for way in range(2):
                arrival, there = self.arrival(way, k)
                source = relayed(self.place, way, k)[0]
                copy, sent = self.copy(way, k)

                @pl.when(there)
                def _():
                    arrival.wait_recv()
                    self.to_core(source).start()

                if k < nc - 1:
                    pl.when(sent)(copy.start)

    def finish(self):
        nc, c = self.place[:2]
        self.keep().wait()
        for k in range(nc - 1):
            for way in range(2):
                copy, sent = self.copy(way, k)
                pl.when(sent)(copy.wait_send)
        for source in range(nc):

            @pl.when(c != source)
            def _():
                self.to_core(source).wait()

        self.own_to_core().wait()


class Share:
    both = False

    def __init__(self, lay, array):
        self.lay_sizes, self.array = lay.sizes, array

    def out_shapes(self, nc):
        nt, seqs = self.lay_sizes[2:]
        n, rows, width = self.array.shape
        return [jax.ShapeDtypeStruct((seqs, n, rows, nt * width), self.array.dtype)]

    def scratch(self, nc):
        nf, _, nt, seqs = self.lay_sizes
        return [pltpu.SemaphoreType.DMA((nf,)), pltpu.SemaphoreType.DMA((seqs, nt))]

    def bind(self, place, src, outs, sems):
        load = SharedLoad()
        load.lay_sizes, load.src, load.out, load.sems = self.lay_sizes, src, outs[0], sems
        return load


class SharedLoad:
    def target(self, slot, core):
        width = self.src.shape[-1]
        return self.out.at[slot, :, :, pl.ds(pl.multiple_of(core * width, 128), width)]

    def to_chip(self, k):
        nf, _, nt, seqs = self.lay_sizes
        f, t = lax.axis_index("fsdp"), lax.axis_index("tp")
        own = lax.rem(f, seqs)
        return pltpu.make_async_remote_copy(
            src_ref=self.src,
            dst_ref=self.target(own, t),
            send_sem=self.sems[0].at[k],
            recv_sem=self.sems[1].at[own, t],
            device_id={"fsdp": lax.rem(f + k, nf), "tp": f // seqs},
            device_id_type=MESH,
        )

    def keep(self):
        f, t = lax.axis_index("fsdp"), lax.axis_index("tp")
        own = lax.rem(f, self.lay_sizes[3])
        return pltpu.make_async_copy(self.src, self.target(own, t), self.sems[0].at[0])

    def at_home(self):
        return lax.axis_index("tp") == lax.axis_index("fsdp") // self.lay_sizes[3]

    def start(self):
        for k in range(1, self.lay_sizes[0]):
            self.to_chip(k).start()
        pl.when(self.at_home())(lambda: self.keep().start())
        pl.when(jnp.logical_not(self.at_home()))(lambda: self.to_chip(0).start())

    def pass_on(self):
        pass

    def finish(self):
        nf, _, nt, seqs = self.lay_sizes
        f, t = lax.axis_index("fsdp"), lax.axis_index("tp")
        for i in range(seqs):
            for core in range(nt):
                mine = jnp.logical_and(f == t * seqs + i, t == core)

                @pl.when(jnp.logical_not(mine))
                def _():
                    pltpu.make_async_remote_copy(
                        src_ref=self.target(i, core),
                        dst_ref=self.target(i, core),
                        send_sem=self.sems[0].at[0],
                        recv_sem=self.sems[1].at[i, core],
                        device_id={"fsdp": lax.rem(f + 1, nf)},
                        device_id_type=MESH,
                    ).wait_recv()

        for k in range(1, nf):
            self.to_chip(k).wait_send()
        pl.when(self.at_home())(lambda: self.keep().wait())
        pl.when(jnp.logical_not(self.at_home()))(lambda: self.to_chip(0).wait_send())


class Hauls:
    def __init__(self, lay, hauls):
        self.nc, self.hauls = lay.nc, list(hauls)
        self.operands = [h.array for h in self.hauls]
        self.shapes = [shape for h in self.hauls for shape in h.out_shapes(lay.nc)]
        self.scratch = [sem for h in self.hauls for sem in h.scratch(lay.nc)]
        anywhere = pl.BlockSpec(memory_space=pl.ANY)
        self.in_specs = [anywhere] * len(self.operands)
        self.out_specs = [anywhere] * len(self.shapes)

    def split(self, refs, n_in, n_out):
        more_in, more_out, sems = len(self.operands), len(self.shapes), len(self.scratch)
        ins, refs = refs[:n_in], refs[n_in:]
        srcs, refs = refs[:more_in], refs[more_in:]
        outs, refs = refs[:n_out], refs[n_out:]
        dsts, refs = refs[:more_out], refs[more_out:]
        scratch = refs[: len(refs) - sems]
        refs = refs[len(refs) - sems :]
        c, t = lax.axis_index("ctx"), lax.axis_index("tp")
        place = (self.nc, c, lax.axis_size("tp"), t)
        loads = []
        for haul, src in zip(self.hauls, srcs):
            count, held = len(haul.out_shapes(self.nc)), len(haul.scratch(self.nc))
            loads.append(haul.bind(place, src, dsts[:count], refs[:held]))
            dsts, refs = dsts[count:], refs[held:]
        return ins, outs, scratch, loads


def start_all(loads):
    for load in loads:
        load.start()


def finish_all(loads):
    for load in loads:
        load.pass_on()
    for load in loads:
        load.finish()


def greet(nf, nc, nt, whole_plane=False):
    f, c, t = lax.axis_index("fsdp"), lax.axis_index("ctx"), lax.axis_index("tp")
    barrier = pltpu.get_barrier_semaphore()
    peers = [{"ctx": lax.rem(c + gap, nc)} for gap in range(1, nc)]
    for k in range(nf):
        for u in range(nt):
            if (k, u) != (0, 0) and (k == 0 or u == 0 or whole_plane):
                peers.append({"fsdp": lax.rem(f + k, nf), "tp": lax.rem(t + u, nt)})
    for peer in peers:
        pl.semaphore_signal(barrier, inc=1, device_id=peer, device_id_type=MESH)
    pl.semaphore_wait(barrier, len(peers))


def params(call_id):
    return pltpu.CompilerParams(
        collective_id=call_id, has_side_effects=True, vmem_limit_bytes=VMEM_LIMIT
    )


def opening_body(lay_sizes, experts, hauls, *refs):
    nf, nc, nt, seqs = lay_sizes
    (src, small, later), (out, smalls, mine, stage), sems, loads = hauls.split(refs, 3, 4)
    zsend, zrecv, psend, precv, ssend, srecv, lsend, lrecv, here = sems
    f, c, t = lax.axis_index("fsdp"), lax.axis_index("ctx"), lax.axis_index("tp")
    place = (nc, c, nt, t)
    own = lax.rem(f, seqs)
    home = t == f // seqs
    rows, width = stage.shape[1], mine.shape[2]
    greet(nf, nc, nt, True)

    def half(ref, core):
        return ref.at[pl.ds(pl.multiple_of(core * rows, 16), rows)]

    def relay(way, k):
        source = relayed(place, way, k)[0]
        from_ref = half(src, t) if k == 0 else stage.at[source]
        return relay_step(place, way, k, from_ref, stage.at[source], zsend, zrecv)

    def in_plane(source, k, first):
        return pltpu.make_async_remote_copy(
            src_ref=half(src, t) if first else stage.at[source],
            dst_ref=half(out.at[own, source], t),
            send_sem=psend.at[source, k],
            recv_sem=precv.at[own, source, t],
            device_id={"fsdp": lax.rem(f + k, nf), "tp": f // seqs},
            device_id_type=MESH,
        )

    def keep(source, first):
        from_ref = half(src, t) if first else stage.at[source]
        return pltpu.make_async_copy(from_ref, half(out.at[own, source], t), here.at[source])

    def share(source, first=False):
        for k in range(1, nf):
            in_plane(source, k, first).start()
        pl.when(home)(lambda: keep(source, first).start())
        pl.when(jnp.logical_not(home))(lambda: in_plane(source, 0, first).start())

    def small_along_ctx(j, source):
        return pltpu.make_async_remote_copy(
            src_ref=small,
            dst_ref=smalls.at[source],
            send_sem=ssend.at[j],
            recv_sem=srecv.at[j],
            device_id={"ctx": lax.rem(c + j, nc)},
            device_id_type=MESH,
        )

    def later_along_ctx(j):
        return pltpu.make_async_remote_copy(
            src_ref=later.at[j, :, pl.ds(pl.multiple_of(t * width, 128), width)],
            dst_ref=mine.at[j],
            send_sem=lsend.at[j],
            recv_sem=lrecv.at[j],
            device_id={"ctx": lax.rem(c + (nc // experts) * j, nc)},
            device_id_type=MESH,
        )

    def keep_later():
        src_ref = later.at[0, :, pl.ds(pl.multiple_of(t * width, 128), width)]
        return pltpu.make_async_copy(src_ref, mine.at[0], lsend.at[0])

    for way in range(2):
        copy, sent = relay(way, 0)
        pl.when(sent)(lambda: copy.start())
    for j in range(1, nc):
        small_along_ctx(j, c).start()
    keep_small = pltpu.make_async_copy(small, smalls.at[c], ssend.at[0])
    keep_small.start()
    share(c, True)
    loads[0].start()
    keep_later().start()

    for k in range(1, nc):
        for way in range(2):
            source, there = relayed(place, way, k)

            @pl.when(there)
            def _():
                pltpu.make_async_remote_copy(
                    src_ref=stage.at[source],
                    dst_ref=stage.at[source],
                    send_sem=zsend.at[way, k],
                    recv_sem=zrecv.at[way, k - 1],
                    device_id={"ctx": lax.rem(c + 1, nc)},
                    device_id_type=MESH,
                ).wait_recv()
                if k < nc - 1:
                    copy, sent = relay(way, k)
                    pl.when(sent)(lambda: copy.start())
                share(source)

    start_all(loads[1:])
    for j in range(1, experts):
        later_along_ctx(j).start()

    for i in range(seqs):
        for core in range(nt):
            mine_here = jnp.logical_and(f == t * seqs + i, t == core)

            @pl.when(jnp.logical_not(mine_here))
            def _():
                for source in range(nc):
                    landing = half(out.at[i, source], core)
                    pltpu.make_async_remote_copy(
                        src_ref=landing,
                        dst_ref=landing,
                        send_sem=psend.at[source, 0],
                        recv_sem=precv.at[i, source, core],
                        device_id={"fsdp": lax.rem(f + 1, nf)},
                        device_id_type=MESH,
                    ).wait_recv()

    for j in range(1, nc):
        small_along_ctx(j, lax.rem(c - j + nc, nc)).wait_recv()
        small_along_ctx(j, c).wait_send()
    keep_small.wait()
    keep_later().wait()
    for k in range(nc - 1):
        for way in range(2):
            copy, sent = relay(way, k)
            pl.when(sent)(lambda: copy.wait_send())
    for source in range(nc):
        for k in range(1, nf):
            in_plane(source, k, False).wait_send()
        pl.when(home)(lambda: keep(source, False).wait())
        pl.when(jnp.logical_not(home))(lambda: in_plane(source, 0, False).wait_send())
    for j in range(1, experts):
        later_along_ctx(j).wait()
    finish_all(loads)


def opening(lay, rows, small, later, call_id, hauls):
    count, width = rows.shape
    nf, nc, nt, seqs = lay.sizes
    hauls = Hauls(lay, hauls)
    experts = lay.experts
    dma = pltpu.SemaphoreType.DMA
    anywhere = pl.BlockSpec(memory_space=pl.ANY)
    shapes = [
        jax.ShapeDtypeStruct((seqs, nc, count, width), rows.dtype),
        jax.ShapeDtypeStruct((nc,) + small.shape, small.dtype),
        jax.ShapeDtypeStruct(later.shape[:2] + (later.shape[2] // nt,), later.dtype),
        jax.ShapeDtypeStruct((nc, count // nt, width), rows.dtype),
    ]
    return pl.pallas_call(
        functools.partial(opening_body, lay.sizes, experts, hauls),
        out_shape=shapes + hauls.shapes,
        in_specs=[anywhere] * 3 + hauls.in_specs,
        out_specs=[anywhere] * 4 + hauls.out_specs,
        scratch_shapes=[
            dma((2, nc)),
            dma((2, nc)),
            dma((nc, nf)),
            dma((seqs, nc, nt)),
            dma((nc,)),
            dma((nc,)),
            dma((experts,)),
            dma((experts,)),
            dma((nc,)),
        ]
        + hauls.scratch,
        compiler_params=params(call_id),
        name=f"opening{call_id}",
    )(rows, small, later, *hauls.operands)


def spread_body(lay_sizes, stride, blocks, hauls, *refs):
    nf, nc, nt, seqs = lay_sizes
    (src,), (out,), (zsend, zrecv, psend, precv, here), loads = hauls.split(refs, 1, 1)
    f, c, t = lax.axis_index("fsdp"), lax.axis_index("ctx"), lax.axis_index("tp")
    own = lax.rem(f, seqs)
    home = t == f // seqs
    greet(nf, nc, nt)

    def along_ctx(j):
        return pltpu.make_async_remote_copy(
            src_ref=src.at[j],
            dst_ref=out.at[own, j],
            send_sem=zsend.at[j],
            recv_sem=zrecv.at[j],
            device_id={"ctx": lax.rem(c + stride * j, nc)},
            device_id_type=MESH,
        )

    def in_plane(j, k):
        return pltpu.make_async_remote_copy(
            src_ref=src.at[0] if j == 0 else out.at[own, j],
            dst_ref=out.at[own, j],
            send_sem=psend.at[j, k],
            recv_sem=precv.at[own, j],
            device_id={"fsdp": lax.rem(f + k, nf)},
            device_id_type=MESH,
        )

    keep = pltpu.make_async_copy(src.at[0], out.at[own, 0], here)

    @pl.when(home)
    def _():
        for j, there in ahead_by_gap(c // stride, blocks):
            pl.when(there)(lambda j=j: along_ctx(j).start())
        for k in range(1, nf):
            in_plane(0, k).start()
        keep.start()

    @pl.when(jnp.logical_not(home))
    def _():
        start_all(loads)

    @pl.when(home)
    def _():
        for j, there in by_gap(c // stride, blocks, wait_order(blocks)):

            @pl.when(there)
            def _():
                along_ctx(j).wait_recv()
                for k in range(1, nf):
                    in_plane(j, k).start()

        start_all(loads)
        keep.wait()

    for i in range(seqs):

        @pl.when(jnp.logical_not(jnp.logical_and(home, own == i)))
        def _():
            for j in range(blocks):
                pltpu.make_async_remote_copy(
                    src_ref=out.at[i, j],
                    dst_ref=out.at[i, j],
                    send_sem=psend.at[j, 0],
                    recv_sem=precv.at[i, j],
                    device_id={"fsdp": lax.rem(f + 1, nf)},
                    device_id_type=MESH,
                ).wait_recv()

    @pl.when(home)
    def _():
        for j in range(1, blocks):
            along_ctx(j).wait_send()
        for j in range(blocks):
            for k in range(1, nf):
                in_plane(j, k).wait_send()

    finish_all(loads)


def spread(lay, rows, stride, call_id, hauls=()):
    blocks = rows.shape[0]
    hauls = Hauls(lay, hauls)
    dma = pltpu.SemaphoreType.DMA
    anywhere = pl.BlockSpec(memory_space=pl.ANY)
    return pl.pallas_call(
        functools.partial(spread_body, lay.sizes, stride, blocks, hauls),
        out_shape=[jax.ShapeDtypeStruct((lay.seqs,) + rows.shape, rows.dtype)] + hauls.shapes,
        in_specs=[anywhere] + hauls.in_specs,
        out_specs=[anywhere] + hauls.out_specs,
        scratch_shapes=[
            dma((blocks,)),
            dma((blocks,)),
            dma((blocks, lay.nf)),
            dma((lay.seqs, blocks)),
            dma,
        ]
        + hauls.scratch,
        compiler_params=params(call_id),
        name=f"spread{call_id}",
    )(rows, *hauls.operands)


def collect_body(lay_sizes, stride, blocks, by_plane, dims, sets, n_a, n_w, hauls, *refs):
    nf, nc, nt, seqs = lay_sizes
    ins, outs, scratch, loads = hauls.split(refs, n_a + n_w, len(sets))
    lefts, rights = ins[:n_a], ins[n_a:]
    part, came, psend, precv, zsend, zrecv = scratch
    f, c, t = lax.axis_index("fsdp"), lax.axis_index("ctx"), lax.axis_index("tp")
    own = lax.rem(f, seqs)
    home = t == f // seqs
    greet(nf, nc, nt)
    start_all(loads)
    wide = part.shape[-1]
    rows = part.shape[-2] // blocks

    def to_chip(n, slot, s):
        chip = t * seqs + slot
        gap = lax.rem(f - chip + nf, nf) - 1
        return pltpu.make_async_remote_copy(
            src_ref=part.at[n, slot, s],
            dst_ref=came.at[n, gap, s],
            send_sem=psend.at[n, slot, s],
            recv_sem=precv.at[n, gap, s],
            device_id={"fsdp": chip},
            device_id_type=MESH,
        )

    def block(j):
        at = lax.rem(c - j + nc, nc) if by_plane else j
        return pl.ds(pl.multiple_of(at * rows, 16), rows)

    def to_owner(n, s, j):
        return pltpu.make_async_remote_copy(
            src_ref=part.at[n, own, s, block(j)],
            dst_ref=outs[n].at[j, :, pl.ds(pl.multiple_of(s * wide, wide), wide)],
            send_sem=zsend.at[n, s, j],
            recv_sem=zrecv.at[n, s, j],
            device_id={"ctx": lax.rem(c - stride * j + nc, nc)},
            device_id_type=MESH,
        )

    for n, terms in enumerate(sets):

        @pl.loop(0, seqs * nc)
        def _(i):
            s = lax.rem(i, nc)
            slot = lax.rem(own + 1 + i // nc, seqs)
            acc = None
            for which, lead, first, size, weight, row in terms:
                right = rights[weight][s] if row is None else rights[weight][s, row]
                term = dot(lefts[which][lead, slot, :, first : first + size], right, dims)
                acc = term if acc is None else acc + term
            part[n, slot, s] = acc.astype(BF16)

            @pl.when(t * seqs + slot != f)
            def _():
                to_chip(n, slot, s).start()

    for n in range(len(sets)):

        @pl.when(home)
        def _():
            @pl.loop(0, nc)
            def _(s):
                for r in range(nf - 1):
                    pltpu.make_async_remote_copy(
                        src_ref=came.at[n, r, s],
                        dst_ref=came.at[n, r, s],
                        send_sem=psend.at[n, 0, s],
                        recv_sem=precv.at[n, r, s],
                        device_id={"fsdp": lax.rem(f + 1, nf)},
                        device_id_type=MESH,
                    ).wait_recv()
                for j in reversed(range(blocks)):
                    where = block(j)
                    summed = part[n, own, s, where].astype(F32)
                    for r in range(nf - 1):
                        summed = summed + came[n, r, s, where].astype(F32)
                    if j == 0:
                        outs[n][0, :, pl.ds(pl.multiple_of(s * wide, wide), wide)] = summed.astype(BF16)
                    else:
                        part[n, own, s, where] = summed.astype(BF16)
                for j, there in by_gap(c // stride, blocks, start_order(blocks)):
                    pl.when(there)(lambda j=j: to_owner(n, s, j).start())

    @pl.when(home)
    def _():
        for n in range(len(sets)):
            for s in range(nc):
                for j in range(1, blocks):
                    to_owner(n, s, j).wait()

    @pl.when(jnp.logical_not(home))
    def _():
        for out in outs:
            out[...] = jnp.zeros_like(out)

    for slot in range(seqs):

        @pl.when(t * seqs + slot != f)
        def _():
            for n in range(len(sets)):
                for s in range(nc):
                    to_chip(n, slot, s).wait_send()

    finish_all(loads)


def collect(lay, lefts, rights, sets, stride, blocks, call_id, dims=NT, hauls=(), by_plane=False):
    seqs, count = lefts[0].shape[1:3]
    nc, wide = rights[0].shape[0], rights[0].shape[-2 if dims == NT else -1]
    rows, width = count // blocks, nc * wide
    held = len(sets) * (seqs + lay.nf) * count * width * 2
    held += sum(a.size for a in lefts) * 9 // 4 + sum(w.size for w in rights) * 2
    if held > VMEM_LIMIT:

        def block_of(terms, j, last):
            at = (lay.c - j) % nc if by_plane else j
            here = [lax.dynamic_slice_in_dim(a, at * rows, rows, 2) for a in lefts]
            if last is not None:
                here = lax.optimization_barrier((here, last))[0]
            partial = 0.0
            for which, lead, first, size, weight, row in terms:
                partial = partial + jnp.einsum(
                    "srh,pdh->srpd" if dims == NT else "srh,phd->srpd",
                    here[which][lead, :, :, first : first + size],
                    rights[weight] if row is None else rights[weight][:, row],
                    preferred_element_type=F32,
                )
            return partial.astype(BF16).reshape(seqs, rows, width)

        sums = [
            collect_permute(lay, functools.partial(block_of, terms), blocks, stride) for terms in sets
        ]
        return [*sums, *haul_alone(lay, hauls, call_id)]
    hauls = Hauls(lay, hauls)
    dma = pltpu.SemaphoreType.DMA
    in_vmem = pl.BlockSpec(memory_space=pltpu.VMEM)
    return pl.pallas_call(
        functools.partial(
            collect_body,
            lay.sizes,
            stride,
            blocks,
            by_plane,
            dims,
            sets,
            len(lefts),
            len(rights),
            hauls,
        ),
        out_shape=[jax.ShapeDtypeStruct((blocks, rows, width), BF16)] * len(sets) + hauls.shapes,
        in_specs=[in_vmem] * (len(lefts) + len(rights)) + hauls.in_specs,
        out_specs=[in_vmem] * len(sets) + hauls.out_specs,
        scratch_shapes=[
            pltpu.VMEM((len(sets), seqs, nc, count, wide), BF16),
            pltpu.VMEM((len(sets), lay.nf - 1, nc, count, wide), BF16),
            dma((len(sets), seqs, nc)),
            dma((len(sets), lay.nf - 1, nc)),
            dma((len(sets), nc, blocks)),
            dma((len(sets), nc, blocks)),
        ]
        + hauls.scratch,
        compiler_params=params(call_id),
        name=f"collect{call_id}",
    )(*lefts, *rights, *hauls.operands)


def haul_alone_body(lay_sizes, hauls, *refs):
    nf, nc, nt, seqs = lay_sizes
    loads = hauls.split(refs, 0, 0)[3]
    greet(nf, nc, nt)
    start_all(loads)
    finish_all(loads)


def haul_alone(lay, hauls, call_id):
    if not hauls:
        return []
    hauls = Hauls(lay, hauls)
    return pl.pallas_call(
        functools.partial(haul_alone_body, lay.sizes, hauls),
        out_shape=hauls.shapes,
        in_specs=hauls.in_specs,
        out_specs=hauls.out_specs,
        scratch_shapes=hauls.scratch,
        compiler_params=params(call_id),
        name=f"haul{call_id}",
    )(*hauls.operands)


def finish_body(lay_sizes, hauls, *refs):
    nf, nc, nt, seqs = lay_sizes
    (terms, grad), (sums, grad_out), scratch, loads = hauls.split(refs, 2, 2)
    landed, middle, total, zsend, zrecv, psend, precv, tsend, trecv = scratch
    f, c, t = lax.axis_index("fsdp"), lax.axis_index("ctx"), lax.axis_index("tp")
    home = t == f // seqs
    barrier = pltpu.get_barrier_semaphore()
    others = [(k, u) for k in range(nf) for u in range(nt) if (k, u) != (0, 0)]
    for j in range(1, nc):
        pl.semaphore_signal(
            barrier, inc=1, device_id={"ctx": lax.rem(c + j, nc)}, device_id_type=MESH
        )
    for k, u in others:
        pl.semaphore_signal(
            barrier,
            inc=1,
            device_id={"fsdp": lax.rem(f + k, nf), "tp": lax.rem(t + u, nt)},
            device_id_type=MESH,
        )
    pl.semaphore_wait(barrier, nc - 1 + len(others))

    def along_ctx(j):
        return pltpu.make_async_remote_copy(
            src_ref=terms.at[lax.rem(c + j, nc)],
            dst_ref=middle.at[j],
            send_sem=zsend.at[j],
            recv_sem=zrecv.at[j],
            device_id={"ctx": lax.rem(c + j, nc)},
            device_id_type=MESH,
        )

    def in_plane(k, u):
        chip = lax.rem(f + k, nf)
        return pltpu.make_async_remote_copy(
            src_ref=total.at[chip],
            dst_ref=landed.at[f],
            send_sem=psend.at[k, u],
            recv_sem=precv.at[f],
            device_id={"fsdp": chip, "tp": lax.rem(t + u, nt)},
            device_id_type=MESH,
        )

    def to_core(u):
        return pltpu.make_async_remote_copy(
            src_ref=grad,
            dst_ref=grad_out,
            send_sem=tsend.at[u],
            recv_sem=trecv.at[0],
            device_id={"tp": lax.rem(t + u, nt)},
            device_id_type=MESH,
        )

    @pl.when(home)
    def _():
        for j in range(1, nc):
            along_ctx(j).start()
        for u in range(1, nt):
            to_core(u).start()

    start_all(loads)

    @pl.when(home)
    def _():
        grad_out[...] = grad[...]
        summed = terms[c]
        for j in range(1, nc):
            along_ctx(j).wait_recv()
            summed = summed + middle[j]
        total[...] = summed
        for k, u in others:
            in_plane(k, u).start()
        landed[f] = total[f]

    for chip in range(nf):

        @pl.when(jnp.logical_not(jnp.logical_and(home, f == chip)))
        def _():
            pltpu.make_async_remote_copy(
                src_ref=landed.at[chip],
                dst_ref=landed.at[chip],
                send_sem=psend.at[0, 0],
                recv_sem=precv.at[chip],
                device_id={"fsdp": lax.rem(f + 1, nf)},
                device_id_type=MESH,
            ).wait_recv()

    sums[...] = jnp.sum(landed[...], axis=0)

    @pl.when(home)
    def _():
        for j in range(1, nc):
            along_ctx(j).wait_send()
        for k, u in others:
            in_plane(k, u).wait_send()
        for u in range(1, nt):
            to_core(u).wait_send()

    @pl.when(jnp.logical_not(home))
    def _():
        to_core(1).wait_recv()

    finish_all(loads)


def finish(lay, terms, grad, call_id, hauls=()):
    lines, part = terms.shape[2:]
    hauls = Hauls(lay, hauls)
    dma = pltpu.SemaphoreType.DMA
    in_vmem = pl.BlockSpec(memory_space=pltpu.VMEM)
    return pl.pallas_call(
        functools.partial(finish_body, lay.sizes, hauls),
        out_shape=[
            jax.ShapeDtypeStruct((lines, part), F32),
            jax.ShapeDtypeStruct(grad.shape, grad.dtype),
        ]
        + hauls.shapes,
        in_specs=[in_vmem] * 2 + hauls.in_specs,
        out_specs=[in_vmem] * 2 + hauls.out_specs,
        scratch_shapes=[
            pltpu.VMEM((lay.nf, lines, part), F32),
            pltpu.VMEM((lay.nc, lay.nf, lines, part), F32),
            pltpu.VMEM((lay.nf, lines, part), F32),
            dma((lay.nc,)),
            dma((lay.nc,)),
            dma((lay.nf, lay.nt)),
            dma((lay.nf,)),
            dma((lay.nt,)),
            dma((1,)),
        ]
        + hauls.scratch,
        compiler_params=params(call_id),
        name=f"finish{call_id}",
    )(terms, grad, *hauls.operands)


def turn(values, cosine, sine):
    return values * cosine + pltpu.roll(values, DH // 2, axis=1) * sine


def chunk_dot(a_ref, weights, row=None, dims=NN):
    planes, wide = weights.shape[0], weights.shape[-2 if dims == NN else -1]
    acc = None
    for s in range(planes):
        weight = weights[s] if row is None else weights[s, row]
        term = dot(a_ref[:, s * wide : (s + 1) * wide], weight, dims)
        acc = term if acc is None else acc + term
    return acc


def pick_columns(ids, expert, planes, cap):
    count = ids.shape[0]
    rows = count // lax.axis_size("ctx")
    member = jnp.where(jnp.logical_or(ids[:, 0:1] == expert, ids[:, 1:2] == expert), 1.0, 0.0)
    before = lax.broadcasted_iota(jnp.int32, (rows, rows), 1)
    before = (before < lax.broadcasted_iota(jnp.int32, (rows, rows), 0)).astype(BF16)
    places = []
    for plane in range(count // rows):
        here = member[plane * rows : (plane + 1) * rows]
        rank = dot(before, jnp.broadcast_to(here, (rows, DH)).astype(BF16))[:, 0:1]
        first = -1.0
        for n, chosen in enumerate(planes):
            first = jnp.where(chosen == plane, float(n * cap), first)
        places.append(jnp.where(jnp.logical_and(here > 0.5, first >= 0.0), rank + first, -1.0))
    place = jnp.concatenate(places, axis=0)
    columns = lax.broadcasted_iota(jnp.int32, (count, len(planes) * cap), 1).astype(F32)
    return jnp.where(place == columns, 1.0, 0.0)


def attend_body(lay_sizes, rep, hauls, *refs):
    nf, nc, nt, seqs = lay_sizes
    ins, outs, scratch, loads = hauls.split(refs, 10, 8)
    x_ref, ids_ref, small_ref, q0, q1, kv0, kv1, cos_ref, sin_ref, pos_ref = ins
    normed_ref, q_ref, k_ref, v_ref, mixed_ref, put_ref, qpos_ref, other_ref = outs
    c = lax.axis_index("ctx")
    expert = c // rep

    @pl.when(pl.program_id(0) == 0)
    def _():
        greet(nf, nc, nt, True)
        start_all(loads)

    wide = small_ref.shape[-1]
    total = 0.0
    for s in range(nc):
        x = x_ref[0, :, s * wide : (s + 1) * wide].astype(F32)
        total = total + jnp.sum(x * x, axis=-1, keepdims=True)
    inverse = lax.rsqrt(total * (1.0 / (nc * wide)) + EPSILON)
    for s in range(nc):
        columns = slice(s * wide, (s + 1) * wide)
        gain = small_ref[s, 0:1].astype(F32)
        normed_ref[0, :, columns] = (x_ref[0, :, columns].astype(F32) * inverse * gain).astype(BF16)
    normed = normed_ref.at[0]

    cap = qpos_ref.shape[-1] * rep // nc
    planes = [lax.rem(c - rep * j + nc, nc) for j in range(nc // rep)]
    ids = ids_ref[0].astype(F32)
    pick = pick_columns(ids[:, 0:2], expert.astype(F32), planes, cap)
    put_ref[0] = pick.astype(BF16)
    qpos_ref[0] = jnp.sum(pick * pos_ref[...], axis=0, keepdims=True)
    seen = pos_ref[...] <= qpos_ref[0]
    pick_m = pick_columns(ids[:, 2:4], expert.astype(F32), planes, cap).astype(BF16)
    other = jnp.where(ids[:, 2:3] == expert.astype(F32), ids[:, 3:4], ids[:, 2:3])
    other = dot(pick_m, jnp.broadcast_to(other, (other.shape[0], DH)).astype(BF16), TN)
    other_ref[0] = other[:, 0:1]

    cosine, sine = cos_ref[...], sin_ref[...]
    half = q0.shape[-1]
    for side, (query, key_value) in enumerate(((q0, kv0), (q1, kv1))):
        v_ref[0, :, side * half : (side + 1) * half] = chunk_dot(normed, key_value, 1).astype(BF16)
        keys = chunk_dot(normed, key_value, 0)
        queries = chunk_dot(normed, query)
        for h in range(half // DH):
            cols = slice(side * half + h * DH, side * half + (h + 1) * DH)
            here = slice(h * DH, (h + 1) * DH)
            k_ref[0, :, cols] = turn(keys[:, here], cosine, sine).astype(BF16)
            turned = turn(queries[:, here], cosine, sine).astype(BF16)
            q_ref[0, :, cols] = dot(put_ref[0], turned, TN).astype(BF16)
    for h in range(2 * half // DH):
        cols = slice(h * DH, (h + 1) * DH)
        scores = dot(k_ref[0, :, cols], q_ref[0, :, cols], NT) * (1.0 / math.sqrt(DH))
        scores = jnp.where(seen, scores, MASKED)
        powers = jnp.exp(scores - jnp.max(scores, axis=0, keepdims=True))
        probs = (powers / jnp.sum(powers, axis=0, keepdims=True)).astype(BF16)
        mixed_ref[0, :, cols] = dot(probs, v_ref[0, :, cols], TN).astype(BF16)

    @pl.when(pl.program_id(0) == seqs - 1)
    def _():
        finish_all(loads)


def attend(lay, x, small, weights, cosine, sine, pos, cap, call_id, hauls):
    seqs, count = x.shape[:2]
    width = lay.nc * small.shape[-1]
    heads = 2 * weights[0].shape[-1]
    picked = lay.experts * cap
    hauls = Hauls(lay, hauls)
    per_seq = lambda i: (i, 0, 0)
    once = pl.Buffered(1)
    weight_specs = [
        pl.BlockSpec(w.shape, lambda i, n=w.ndim: (0,) * n, pipeline_mode=once) for w in weights
    ]
    results = [
        ((count, width), BF16),
        ((picked, heads), BF16),
        ((count, heads), BF16),
        ((count, heads), BF16),
        ((picked, heads), BF16),
        ((count, picked), BF16),
        ((1, picked), F32),
        ((picked, 1), F32),
    ]
    return pl.pallas_call(
        functools.partial(attend_body, lay.sizes, lay.rep, hauls),
        grid=(seqs,),
        in_specs=[
            pl.BlockSpec((1, count, width), per_seq),
            pl.BlockSpec((1, count, DH), lambda i: (i, 0, width // DH)),
            pl.BlockSpec(small.shape, lambda i: (0, 0, 0)),
            *weight_specs,
            pl.BlockSpec((count, DH), lambda i: (0, 0)),
            pl.BlockSpec((count, DH), lambda i: (0, 0)),
            pl.BlockSpec((count, 1), lambda i: (0, 0)),
        ]
        + hauls.in_specs,
        out_specs=[pl.BlockSpec((1,) + dims, per_seq) for dims, _ in results] + hauls.out_specs,
        out_shape=[jax.ShapeDtypeStruct((seqs,) + dims, kind) for dims, kind in results]
        + hauls.shapes,
        scratch_shapes=hauls.scratch,
        compiler_params=params(call_id),
        name="attend",
    )(x, x, small, *weights, cosine, sine, pos, *hauls.operands)


def experts_body(rep, experts, n_ref, g_ref, small_ref, other_ref, *refs):
    weights, (ge_ref, hidden_ref, gate_ref, up_ref) = refs[:6], refs[6:]
    c = lax.axis_index("ctx")
    lanes = lax.broadcasted_iota(jnp.int32, (1, small_ref.shape[1]), 1) - (2 + experts)
    logits = chunk_dot(n_ref.at[0], small_ref, None, NT)
    mine = jnp.sum(jnp.where(lanes == c // rep, logits, 0.0), axis=-1, keepdims=True)
    theirs = jnp.where(lanes.astype(F32) == other_ref[0], logits, 0.0)
    theirs = jnp.sum(theirs, axis=-1, keepdims=True)
    ge_ref[0] = (jax.nn.sigmoid(mine - theirs) * g_ref[0].astype(F32)).astype(BF16)
    for side in range(2):
        gate_weight, up_weight, down_weight = weights[side::2]
        gate_pre = chunk_dot(n_ref.at[0], gate_weight, None, NT)
        up_pre = chunk_dot(n_ref.at[0], up_weight, None, NT)
        grad_hidden = chunk_dot(ge_ref.at[0], down_weight, None, NT)
        sigmoid_gate = jax.nn.sigmoid(gate_pre)
        silu_gate = gate_pre * sigmoid_gate
        hidden_ref[side, 0] = (silu_gate * up_pre).astype(BF16)
        silu_slope = sigmoid_gate + silu_gate * (1.0 - sigmoid_gate)
        gate_ref[side, 0] = (grad_hidden * up_pre * silu_slope).astype(BF16)
        up_ref[side, 0] = (grad_hidden * silu_gate).astype(BF16)


def experts_apply(lay, n2, g, small, other, *weights):
    seqs, count, width = n2.shape
    ff = weights[0].shape[-2]
    per_seq = lambda i: (i, 0, 0)
    once = pl.Buffered(1)
    wide = pl.BlockSpec((2, 1, count, ff), lambda i: (0, i, 0, 0))
    return pl.pallas_call(
        functools.partial(experts_body, lay.rep, lay.experts),
        grid=(seqs,),
        in_specs=[
            pl.BlockSpec((1, count, width), per_seq),
            pl.BlockSpec((1, count, width), per_seq),
            pl.BlockSpec(small.shape, lambda i: (0, 0, 0)),
            pl.BlockSpec((1, count, 1), per_seq),
        ]
        + [pl.BlockSpec(w.shape, lambda i: (0, 0, 0), pipeline_mode=once) for w in weights],
        out_specs=[pl.BlockSpec((1, count, width), per_seq), wide, wide, wide],
        out_shape=[jax.ShapeDtypeStruct(n2.shape, BF16)]
        + [jax.ShapeDtypeStruct((2, seqs, count, ff), BF16)] * 3,
        compiler_params=pltpu.CompilerParams(vmem_limit_bytes=VMEM_LIMIT),
        name="experts",
    )(n2, g, small, other, *weights)


def core_exchange(refs, nt):
    away, came, send_sem, recv_sem = refs

    def copy(s):
        return pltpu.make_async_remote_copy(
            src_ref=away.at[s],
            dst_ref=came.at[s],
            send_sem=send_sem.at[s],
            recv_sem=recv_sem.at[s],
            device_id={"tp": lax.rem(lax.axis_index("tp") + 1, nt)},
            device_id_type=MESH,
        )

    return copy


def mlp_grads_body(lay_sizes, hauls, *refs):
    nf, nc, nt, seqs = lay_sizes
    ins, (out,), scratch, loads = hauls.split(refs, 5, 1)
    n_ref, ge_ref, hidden_ref, gate_ref, up_ref = ins
    away, came, send_sem, recv_sem = scratch
    ff, wide = away.shape[-2:]
    pairs = ((gate_ref, n_ref), (up_ref, n_ref), (hidden_ref, ge_ref))
    greet(nf, nc, nt)

    def copy(first, last, s):
        group = pl.ds(first, last - first)
        return pltpu.make_async_remote_copy(
            src_ref=away.at[s, group],
            dst_ref=came.at[s, group],
            send_sem=send_sem.at[min(first, 1), s],
            recv_sem=recv_sem.at[min(first, 1), s],
            device_id={"tp": lax.rem(lax.axis_index("tp") + 1, nt)},
            device_id_type=MESH,
        )

    for first, last in ((0, 1), (1, 3)):

        @pl.loop(0, nc)
        def _(s):
            columns = pl.ds(pl.multiple_of(s * wide, wide), wide)
            for i in range(first, last):
                left, right = pairs[i]
                away[s, i] = dot(left[1], right[:, columns], TN).astype(BF16)
            copy(first, last, s).start()

        @pl.loop(0, nc)
        def _(s):
            columns = pl.ds(pl.multiple_of(s * wide, wide), wide)
            copy(first, last, s).wait_recv()
            for i in range(first, last):
                left, right = pairs[i]
                own = dot(left[0], right[:, columns], TN)
                out[s, i * ff : (i + 1) * ff] = (own + came[s, i].astype(F32)).astype(BF16)

        if first == 0:
            for load in loads:
                load.src = out
                load.start()

    for first, last in ((0, 1), (1, 3)):

        @pl.loop(0, nc)
        def _(s):
            copy(first, last, s).wait_send()

    finish_all(loads)


def mlp_grads(lay, n2, ge, hidden, gate, up, early, call_id):
    width, ff, nc = n2.shape[1], hidden.shape[-1], lay.nc
    wide = width // nc
    piece = (3, ff, wide)
    in_vmem = pl.BlockSpec(memory_space=pltpu.VMEM)
    hauls = Hauls(lay, [Haul(n2, lambda ref, d: ref.at[d, pl.ds(0, early)], (early, wide))])
    return pl.pallas_call(
        functools.partial(mlp_grads_body, lay.sizes, hauls),
        in_specs=[in_vmem] * 5 + hauls.in_specs,
        out_specs=[in_vmem] + hauls.out_specs,
        out_shape=[jax.ShapeDtypeStruct((nc, 3 * ff, wide), BF16)] + hauls.shapes,
        scratch_shapes=[
            pltpu.VMEM((nc,) + piece, BF16),
            pltpu.VMEM((nc,) + piece, BF16),
            pltpu.SemaphoreType.DMA((2, nc)),
            pltpu.SemaphoreType.DMA((2, nc)),
        ]
        + hauls.scratch,
        compiler_params=params(call_id),
        name="mlp_grads",
    )(n2, ge, hidden, gate, up, *hauls.operands)


def attn_grads_body(lay_sizes, hauls, *refs):
    nf, nc, nt, seqs = lay_sizes
    (x_ref, d_ref, g_ref, mixed_ref), outs, scratch, loads = hauls.split(refs, 4, 4)
    kept, away, came = scratch[:3]
    copy = core_exchange(scratch[1:], nt)
    wide, half = away.shape[-2:]
    greet(nf, nc, nt)
    start_all(loads)

    @pl.loop(0, nc)
    def _(s):
        columns = pl.ds(pl.multiple_of(s * wide, wide), wide)
        first = dot(x_ref[:, columns], d_ref[...], TN)
        last = dot(g_ref[:, columns], mixed_ref[...], TN)
        for i in range(4):
            part, at = (first, i) if i < 3 else (last, 0)
            step = 3 if i < 3 else 1
            kept[s, i] = part[:, at * half : (at + 1) * half]
            away[s, i] = part[:, (step + at) * half : (step + at + 1) * half].astype(BF16)
        copy(s).start()

    @pl.loop(0, nc)
    def _(s):
        copy(s).wait_recv()
        for i in range(4):
            outs[i][s] = (kept[s, i] + came[s, i].astype(F32)).astype(BF16)

    @pl.loop(0, nc)
    def _(s):
        copy(s).wait_send()

    finish_all(loads)


def attn_grads(lay, x, grads, g, mixed, call_id, hauls):
    width, heads, nc = x.shape[1], mixed.shape[-1], lay.nc
    piece = (width // nc, heads // 2)
    hauls = Hauls(lay, hauls)
    in_vmem = pl.BlockSpec(memory_space=pltpu.VMEM)
    return pl.pallas_call(
        functools.partial(attn_grads_body, lay.sizes, hauls),
        in_specs=[in_vmem] * 4 + hauls.in_specs,
        out_specs=[in_vmem] * 4 + hauls.out_specs,
        out_shape=[jax.ShapeDtypeStruct((nc,) + piece, BF16)] * 4 + hauls.shapes,
        scratch_shapes=[
            pltpu.VMEM((nc, 4) + piece, F32),
            pltpu.VMEM((nc, 4) + piece, BF16),
            pltpu.VMEM((nc, 4) + piece, BF16),
            pltpu.SemaphoreType.DMA((nc,)),
            pltpu.SemaphoreType.DMA((nc,)),
        ]
        + hauls.scratch,
        compiler_params=params(call_id),
        name="attn_grads",
    )(x, grads, g, mixed, *hauls.operands)


def attend_back_body(lay_sizes, hauls, *refs):
    nf, nc, nt, seqs = lay_sizes
    ins, (out_ref,), scratch, loads = hauls.split(refs, 11, 1)
    q_ref, k_ref, v_ref, g_ref, wo0, wo1, qpos_ref, kpos_ref, cosine, sine, put = ins

    @pl.when(pl.program_id(0) == 0)
    def _():
        greet(nf, nc, nt)
        start_all(loads)

    scale = 1.0 / math.sqrt(DH)
    seen = kpos_ref[...] <= qpos_ref[0]
    half = wo0.shape[-1]
    for side, weight in enumerate((wo0, wo1)):
        grad_mixed = chunk_dot(g_ref.at[0], weight).astype(BF16)
        for h in range(half // DH):
            cols = slice(side * half + h * DH, side * half + (h + 1) * DH)
            q, k, v = q_ref[0, :, cols], k_ref[0, :, cols], v_ref[0, :, cols]
            g = grad_mixed[:, h * DH : (h + 1) * DH]
            scores = jnp.where(seen, dot(k, q, NT) * scale, MASKED)
            powers = jnp.exp(scores - jnp.max(scores, axis=0, keepdims=True))
            probs = powers / jnp.sum(powers, axis=0, keepdims=True)
            grad_probs = dot(v, g, NT)
            centre = jnp.sum(probs * grad_probs, axis=0, keepdims=True)
            grad_scores = (probs * (grad_probs - centre)).astype(BF16)

            def at(part):
                first = (3 * side + part) * half + h * DH
                return slice(first, first + DH)

            out_ref[0, :, at(2)] = dot(probs.astype(BF16), g).astype(BF16)
            dk = dot(grad_scores, q) * scale
            out_ref[0, :, at(1)] = turn(dk, cosine[...], -sine[...]).astype(BF16)
            dq = dot(grad_scores, k, TN) * scale
            high = dq.astype(BF16)
            low = (dq - high.astype(F32)).astype(BF16)
            dq = dot(put[0], high) + dot(put[0], low)
            out_ref[0, :, at(0)] = turn(dq, cosine[...], -sine[...]).astype(BF16)

    @pl.when(pl.program_id(0) == seqs - 1)
    def _():
        finish_all(loads)


def attend_back(lay, q, k, v, g, weights, qpos, kpos, cosine, sine, put, call_id, hauls):
    seqs, count, heads = q.shape
    width = g.shape[-1]
    length = k.shape[1]
    hauls = Hauls(lay, hauls)
    per_seq = lambda s: (s, 0, 0)
    once = lambda s: (0, 0)
    return pl.pallas_call(
        functools.partial(attend_back_body, lay.sizes, hauls),
        grid=(seqs,),
        in_specs=[
            pl.BlockSpec((1, count, heads), per_seq),
            pl.BlockSpec((1, length, heads), per_seq),
            pl.BlockSpec((1, length, heads), per_seq),
            pl.BlockSpec((1, count, width), per_seq),
            pl.BlockSpec(weights[0].shape, lambda s: (0, 0, 0)),
            pl.BlockSpec(weights[1].shape, lambda s: (0, 0, 0)),
            pl.BlockSpec((1, 1, count), per_seq),
            pl.BlockSpec((length, 1), once),
            pl.BlockSpec((length, DH), once),
            pl.BlockSpec((length, DH), once),
            pl.BlockSpec((1, length, count), per_seq),
        ]
        + hauls.in_specs,
        out_specs=[pl.BlockSpec((1, length, 3 * heads), per_seq)] + hauls.out_specs,
        out_shape=[jax.ShapeDtypeStruct((seqs, length, 3 * heads), BF16)] + hauls.shapes,
        scratch_shapes=hauls.scratch,
        compiler_params=params(call_id),
        name="attend_back",
    )(q, k, v, g, *weights, qpos, kpos, cosine, sine, put, *hauls.operands)


def unpack_body(bounds, *refs):
    count = len(bounds) - 1
    parts, attention = refs[:count], refs[count : count + 4]
    gate_up, down, query, output, key_value = refs[count + 4 :]
    ff = down.shape[1]

    def total(ref, rows=slice(None)):
        return jnp.sum(ref[:, rows].astype(F32), axis=0)

    for part, first, last in zip(parts, bounds, bounds[1:]):
        for i in range(3):
            low, high = max(first, i * ff), min(last, (i + 1) * ff)
            if low < high:
                values = total(part, slice(low - first, high - first))
                if i < 2:
                    gate_up[0, i, low - i * ff : high - i * ff] = values
                else:
                    down[0, low - i * ff : high - i * ff] = values
    query[0] = total(attention[0])
    output[0] = total(attention[1])
    for i in range(2):
        values = total(attention[2 + i])

        @pl.when(pl.program_id(0) == 0)
        def _():
            key_value[i] = values

        @pl.when(pl.program_id(0) > 0)
        def _():
            key_value[i] = key_value[i] + values


def unpack(lay, parts, bounds, attention):
    ff, wide = bounds[-1] // 3, parts[0].shape[2]
    experts, rep = lay.experts, lay.rep
    dims = attention[0].shape[1:]
    per_expert = pl.BlockSpec((1,) + dims, lambda e: (e, 0, 0))
    operands = [*parts, *attention]
    return pl.pallas_call(
        functools.partial(unpack_body, bounds),
        grid=(experts,),
        in_specs=[pl.BlockSpec((rep,) + p.shape[1:], lambda e: (e, 0, 0)) for p in operands],
        out_specs=[
            pl.BlockSpec((1, 2, ff, wide), lambda e: (e, 0, 0, 0)),
            pl.BlockSpec((1, ff, wide), lambda e: (e, 0, 0)),
            per_expert,
            per_expert,
            pl.BlockSpec((2,) + dims, lambda e: (0, 0, 0)),
        ],
        out_shape=[
            jax.ShapeDtypeStruct((experts, 2, ff, wide), F32),
            jax.ShapeDtypeStruct((experts, ff, wide), F32),
            jax.ShapeDtypeStruct((experts,) + dims, F32),
            jax.ShapeDtypeStruct((experts,) + dims, F32),
            jax.ShapeDtypeStruct((2,) + dims, F32),
        ],
        compiler_params=pltpu.CompilerParams(vmem_limit_bytes=VMEM_LIMIT),
        name="unpack",
    )(*operands)


def row_of(small_ref, line):
    planes = [small_ref[s, line : line + 1] for s in range(small_ref.shape[0])]
    return jnp.concatenate(planes, axis=1).astype(F32)


def choices(ids, expert, experts, cap):
    rows = ids.shape[0]
    before = lax.broadcasted_iota(jnp.int32, (rows, rows), 1)
    before = (before < lax.broadcasted_iota(jnp.int32, (rows, rows), 0)).astype(BF16)
    lanes = lax.broadcasted_iota(jnp.int32, (rows, DH), 1).astype(F32)
    member = jnp.where(jnp.logical_or(ids[:, 0:1] == lanes, ids[:, 1:2] == lanes), 1.0, 0.0)
    ranks = dot(before, member.astype(BF16))
    columns = lax.broadcasted_iota(jnp.int32, (rows, experts * cap), 1).astype(F32)
    maps = []
    for slot in range(2):
        chosen = ids[:, slot : slot + 1]
        rank = jnp.sum(jnp.where(lanes == chosen, ranks, 0.0), axis=-1, keepdims=True)
        ahead = chosen - expert.astype(F32)
        ahead = jnp.where(ahead < 0.0, ahead + experts, ahead)
        maps.append(jnp.where(columns == ahead * cap + rank, 1.0, 0.0).astype(BF16))
    return maps


def slot_gates(normed, small_ref, ids, first):
    planes, lines, wide = small_ref.shape
    logits = 0.0
    for s in range(planes):
        logits = logits + dot(normed[:, s * wide : (s + 1) * wide], small_ref[s], NT)
    lanes = lax.broadcasted_iota(jnp.int32, logits.shape, 1).astype(F32)
    picked = [
        jnp.sum(jnp.where(lanes == ids[:, k : k + 1] + first, logits, 0.0), axis=-1, keepdims=True)
        for k in range(2)
    ]
    return jax.nn.sigmoid(picked[0] - picked[1]), jax.nn.sigmoid(picked[1] - picked[0])


def norm_of(values, gain):
    inverse = lax.rsqrt(jnp.mean(values * values, axis=-1, keepdims=True) + EPSILON)
    scaled = values * inverse
    return inverse, scaled, (scaled * gain).astype(BF16)


def norm_back(grad, gain, inverse, scaled):
    turned = grad * gain
    return inverse * (turned - scaled * jnp.mean(turned * scaled, axis=-1, keepdims=True))


def logits_back(gates, choice, ids, first):
    mean = gates[0] * choice[0] + gates[1] * choice[1]
    lanes = lax.broadcasted_iota(jnp.int32, (ids.shape[0], DH), 1).astype(F32)
    out = 0.0
    for k in range(2):
        inner = gates[k] * (choice[k] - mean)
        out = out + jnp.where(lanes == ids[:, k : k + 1] + first, inner, 0.0)
    return out


def exact_tn(left, right):
    total = 0.0
    for _ in range(3):
        part = left.astype(BF16)
        total = total + dot(part, right, TN)
        left = left - part.astype(F32)
    return total


def owner_forward_body(rep, experts, x_ref, ids_ref, small_ref, rows_ref, residual_ref, out_ref):
    expert = lax.axis_index("ctx") // rep
    cap = rows_ref.shape[0] // experts
    ids = ids_ref[...]
    x = x_ref[...].astype(F32)
    normed_one = norm_of(x, row_of(small_ref, 0))[2]
    gates = slot_gates(normed_one, small_ref, ids[:, 0:2], 2)
    maps = choices(ids[:, 0:2], expert, experts, cap)
    residual = x + (gates[0] * dot(maps[0], rows_ref[...]) + gates[1] * dot(maps[1], rows_ref[...]))
    residual_ref[...] = residual
    normed_two = norm_of(residual, row_of(small_ref, 1))[2]
    maps = choices(ids[:, 2:4], expert, experts, cap)
    out_ref[...] = dot(maps[0] + maps[1], normed_two, TN).astype(BF16)


def owner_middle_body(rep, experts, *refs):
    x_ref, ids_ref, small_ref, up_ref, residual_ref, branch_ref, expert_ref, grad_ref = refs[:8]
    layer_ref, grad_res_ref, out_ref, logits_ref, terms_ref = refs[8:]
    expert = lax.axis_index("ctx") // rep
    cap = branch_ref.shape[0] // experts
    ids = ids_ref[...]
    upstream, residual = up_ref[...].astype(F32), residual_ref[...]
    gain_two = row_of(small_ref, 1)
    inverse_two, scaled_two, normed_two = norm_of(residual, gain_two)
    gates = slot_gates(normed_two, small_ref, ids[:, 2:4], 2 + experts)
    maps = choices(ids[:, 2:4], expert, experts, cap)
    choice, total = [], 0.0
    for k in range(2):
        expert_out = dot(maps[k], expert_ref[...])
        choice.append(jnp.sum(upstream * expert_out, axis=-1, keepdims=True))
        total = total + gates[k] * expert_out
    layer_ref[...] = (residual + total).astype(BF16)
    logits_two = logits_back(gates, choice, ids[:, 2:4], 2 + experts)
    grad = dot(maps[0] + maps[1], grad_ref[...])
    for e in range(experts):
        line = 2 + experts + e
        grad = grad + logits_two[:, line : line + 1] * row_of(small_ref, line)
    grad_res = upstream + norm_back(grad, gain_two, inverse_two, scaled_two)
    grad_res_ref[...] = grad_res
    gain_grad = jnp.sum(grad * scaled_two, axis=0, keepdims=True)
    normed_one = norm_of(x_ref[...].astype(F32), row_of(small_ref, 0))[2]
    gates = slot_gates(normed_one, small_ref, ids[:, 0:2], 2)
    maps = choices(ids[:, 0:2], expert, experts, cap)
    choice, out = [], 0.0
    for k in range(2):
        branch = dot(maps[k], branch_ref[...])
        choice.append(jnp.sum(grad_res * branch, axis=-1, keepdims=True))
        out = out + dot(maps[k], (gates[k] * grad_res).astype(BF16), TN)
    out_ref[...] = out.astype(BF16)
    logits_one = logits_back(gates, choice, ids[:, 0:2], 2)
    logits_ref[...] = logits_one
    lines = terms_ref.shape[0]
    terms = exact_tn(logits_one, normed_one) + exact_tn(logits_two, normed_two)
    place = lax.broadcasted_iota(jnp.int32, terms_ref.shape, 0)
    terms_ref[...] = jnp.where(place == 1, gain_grad, terms[:lines])


def owner_back_body(experts, x_ref, small_ref, rows_ref, logits_ref, grad_res_ref, layer_ref, terms_ref, both_ref, out_ref):
    gain = row_of(small_ref, 0)
    inverse, scaled, _ = norm_of(x_ref[...].astype(F32), gain)
    grad = 0.0
    for j in range(rows_ref.shape[0]):
        grad = grad + rows_ref[j].astype(F32)
    for e in range(experts):
        grad = grad + logits_ref[:, 2 + e : 3 + e] * row_of(small_ref, 2 + e)
    both_ref[0] = layer_ref[...]
    both_ref[1] = (grad_res_ref[...] + norm_back(grad, gain, inverse, scaled)).astype(BF16)
    gain_grad = jnp.sum(grad * scaled, axis=0, keepdims=True)
    place = lax.broadcasted_iota(jnp.int32, terms_ref.shape, 0)
    terms = jnp.where(place == 0, gain_grad, terms_ref[...])
    planes, chips, _, part = out_ref.shape
    for plane in range(planes):
        for chip in range(chips):
            first = (chip * planes + plane) * part
            out_ref[plane, chip] = terms[:, first : first + part]


def own_kernel(body, name, results, *operands):
    in_vmem = pl.BlockSpec(memory_space=pltpu.VMEM)
    return pl.pallas_call(
        body,
        in_specs=[in_vmem] * len(operands),
        out_specs=[in_vmem] * len(results),
        out_shape=[jax.ShapeDtypeStruct(dims, kind) for dims, kind in results],
        compiler_params=pltpu.CompilerParams(vmem_limit_bytes=VMEM_LIMIT),
        name=name,
    )(*operands)


def ranks_of(member):
    count = member.shape[-1]
    before = (jnp.arange(count)[:, None] < jnp.arange(count)[None, :]).astype(BF16)
    return jnp.einsum("...m,mn->...n", member.astype(BF16), before, preferred_element_type=F32)


def pick_maps(ids, expert, cap):
    member = jnp.any(ids == expert[..., None, None], axis=-1)
    rank = ranks_of(member).astype(jnp.int32)
    place = jnp.arange(cap, dtype=jnp.int32)[:, None]
    return jnp.logical_and(member[..., None, :], rank[..., None, :] == place)


def per_device(
    tokens,
    cotangent,
    attn_ids,
    mlp_ids,
    span_ids,
    attn_gain,
    attn_router,
    kv_weight,
    query_weight,
    output_weight,
    mlp_gain,
    mlp_router,
    gate_up_weight,
    down_weight,
):
    experts = query_weight.shape[0]
    lay = Layout(experts)
    nf, nc, rep, seqs = lay.nf, lay.nc, lay.rep, lay.seqs
    rows, width = tokens.shape
    cap = 3 * rows // 4
    expert = lay.c // rep

    def to_planes(array, index_of, both=False):
        index = index_of(0)
        shape = array.shape[len(index) :]
        return Haul(array, lambda ref, d: ref.at[index_of(d)] if index else ref, shape, both)

    expert_of = (expert + jnp.arange(experts)) % experts
    pick_own_m = pick_maps(jnp.broadcast_to(mlp_ids, (experts, rows, 2)), expert_of, cap)

    def dispatch(pick, values):
        return jnp.einsum(
            "jrn,nd->jrd", pick.astype(BF16), values, preferred_element_type=F32
        ).astype(BF16)

    ids = jnp.concatenate([attn_ids, mlp_ids], axis=1).astype(BF16)
    payload = jnp.concatenate([tokens, jnp.pad(ids, ((0, 0), (0, 124)))], axis=1)
    small = jnp.concatenate([attn_gain[None], mlp_gain[None], attn_router.T, mlp_router.T])
    small = jnp.pad(small, ((0, -small.shape[0] % 16), (0, 0)))
    g_own = dispatch(pick_own_m, cotangent)
    by_plane = lambda *more: lambda d: (d // rep,) + more
    x_all, small_all, g_mine, _, q_own, q_sib, kv_own, kv_sib = opening(
        lay,
        payload,
        small,
        g_own,
        1,
        [to_planes(query_weight, by_plane(), True), Relay(kv_weight)],
    )
    gate_up_turned = gate_up_weight.swapaxes(-1, -2)
    down_turned = down_weight.swapaxes(-1, -2)

    own_ids = ids.astype(F32)

    half_len = rows // 2
    offsets = jnp.arange(rows, dtype=jnp.int32)
    pos = jnp.where(
        offsets[None, :] < half_len,
        span_ids[:, 0:1] * half_len + offsets[None, :],
        span_ids[:, 1:2] * half_len + offsets[None, :] - half_len,
    )
    pos = pos.astype(F32).reshape(-1, 1)
    freqs = ROPE_BASE ** (-jnp.arange(DH // 2, dtype=F32) / (DH // 2))

    cosine, sine = jnp.cos(pos * freqs), jnp.sin(pos * freqs)
    cosine = jnp.concatenate([cosine, cosine], axis=-1)
    sine = jnp.concatenate([-sine, sine], axis=-1)

    normed_all, q, k, v, mixed, put, pos_q, other, o_own, o_sib, gate_own, gate_sib, g_blocks = attend(
        lay,
        x_all.reshape(seqs, nc * rows, -1),
        small_all,
        [q_own, q_sib, kv_own, kv_sib],
        cosine,
        sine,
        pos,
        cap,
        9,
        [
            to_planes(output_weight, by_plane(), True),
            to_planes(gate_up_turned, by_plane(0), True),
            Share(lay, g_mine),
        ],
    )
    g_blocks = g_blocks.reshape(seqs, experts * cap, width)
    heads = q.shape[-1]
    half = heads // 2
    branch_rows, up_own, up_sib = collect(
        lay,
        [mixed[None]],
        [o_own, o_sib],
        [((0, 0, 0, half, 0, None), (0, 0, half, half, 1, None))],
        rep,
        experts,
        2,
        hauls=[to_planes(gate_up_turned, by_plane(1), True)],
    )
    branch_rows = branch_rows.reshape(-1, width)
    residual, n2_own = own_kernel(
        functools.partial(owner_forward_body, rep, experts),
        "owner_forward",
        [((rows, width), F32), ((experts * cap, width), BF16)],
        tokens,
        own_ids,
        small_all,
        branch_rows,
    )

    n2, down_own, down_sib = spread(
        lay,
        n2_own.reshape(experts, cap, width),
        rep,
        3,
        [to_planes(down_turned, by_plane(), True)],
    )
    n2 = n2.reshape(seqs, experts * cap, width)
    grad_expert, hidden, grad_gate, grad_up = experts_apply(
        lay,
        n2,
        g_blocks,
        small_all,
        other,
        gate_own,
        gate_sib,
        up_own,
        up_sib,
        down_own,
        down_sib,
    )
    ff = hidden.shape[-1]
    shares = (240, 704, 336, 320, 256, 256)
    bounds = [0]
    for share in shares:
        bounds.append(bounds[-1] + share)
    bounds = [3 * ff * bound // bounds[-1] // 16 * 16 for bound in bounds]
    mlp_back, back_a = mlp_grads(
        lay,
        n2.reshape(-1, width),
        grad_expert.reshape(-1, width),
        *(a.reshape(2, -1, ff) for a in (hidden, grad_gate, grad_up)),
        bounds[1],
        4,
    )

    def carried(n):
        first, last = bounds[n : n + 2]
        rows_of = lambda ref, d: ref.at[d, pl.ds(first, last - first)]
        return Haul(mlp_back, rows_of, (last - first, width // nc))

    by_piece = lambda d: (d,)
    expert_rows, grad_rows, back_b = collect(
        lay,
        [hidden, grad_gate, grad_up],
        [gate_own, up_own, down_own, gate_sib, up_sib, down_sib],
        [
            tuple((0, side, 0, ff, 3 * side + 2, None) for side in range(2)),
            tuple((1 + i, side, 0, ff, 3 * side + i, None) for side in range(2) for i in range(2)),
        ],
        rep,
        experts,
        5,
        NN,
        [carried(1)],
    )
    lines = -(-(2 + 2 * experts) // 16) * 16
    layer_out, grad_residual, gb_own, logits_one, terms = own_kernel(
        functools.partial(owner_middle_body, rep, experts),
        "owner_middle",
        [
            ((rows, width), BF16),
            ((rows, width), F32),
            ((experts * cap, width), BF16),
            ((rows, DH), F32),
            ((lines, width), F32),
        ],
        tokens,
        own_ids,
        small_all,
        cotangent,
        residual,
        branch_rows,
        expert_rows.reshape(-1, width),
        grad_rows.reshape(-1, width),
    )

    gb, back_c = spread(lay, gb_own.reshape(experts, cap, width), rep, 6, [carried(2)])
    gb = gb.reshape(seqs, experts * cap, width)
    dqkv, back_d = attend_back(
        lay,
        q,
        k,
        v,
        gb,
        [o_own, o_sib],
        pos_q,
        pos,
        cosine,
        sine,
        put,
        11,
        [carried(3)],
    )
    q_grads, k_grads, v_grads, o_grads, back_e = attn_grads(
        lay,
        normed_all.reshape(-1, width),
        dqkv.reshape(-1, 3 * heads),
        gb.reshape(-1, width),
        mixed.reshape(-1, heads),
        10,
        [carried(4)],
    )
    grad_one_rows, back_f, o_back, q_back = collect(
        lay,
        [dqkv[None]],
        [q_own, kv_own, q_sib, kv_sib],
        [
            tuple(
                (0, 0, (3 * s + i) * half, half, 2 * s + (i > 0), None if i == 0 else i - 1)
                for i in range(3)
                for s in range(2)
            )
        ],
        1,
        nc,
        7,
        hauls=[carried(5), to_planes(o_grads, by_piece), to_planes(q_grads, by_piece)],
        by_plane=True,
    )

    both, terms = own_kernel(
        functools.partial(owner_back_body, experts),
        "owner_back",
        [((2, rows, width), BF16), ((nc, nf, lines, width // (nf * nc)), F32)],
        tokens,
        small_all,
        grad_one_rows,
        logits_one,
        grad_residual,
        layer_out,
        terms,
    )
    terms, both_out, k_back, v_back = finish(
        lay, terms, both, 8, [to_planes(grads, by_piece) for grads in (k_grads, v_grads)]
    )
    layer_out, grad_tokens = both_out[0], both_out[1]

    grad_gate_up, grad_down, grad_query_weight, grad_output_weight, grad_kv_weight = unpack(
        lay,
        [back_a, back_b, back_c, back_d, back_e, back_f],
        bounds,
        [q_back, o_back, k_back, v_back],
    )
    grad_gate_up, grad_down = grad_gate_up.swapaxes(-1, -2), grad_down.swapaxes(-1, -2)
    return (
        layer_out,
        grad_tokens,
        terms[0],
        terms[2 : 2 + experts].T,
        grad_kv_weight,
        grad_query_weight,
        grad_output_weight,
        terms[1],
        terms[2 + experts : 2 + 2 * experts].T,
        grad_gate_up,
        grad_down,
    )


def solution(mesh):
    placed = (
        P(("fsdp", "ctx"), None),
        P(("fsdp", "ctx"), None),
        P(("fsdp", "ctx"), None),
        P(("fsdp", "ctx"), None),
        P(),
        P("ctx"),
        P("ctx", None),
        P(None, "ctx", ("fsdp", "tp")),
        P(None, "ctx", ("fsdp", "tp")),
        P(None, "ctx", ("fsdp", "tp")),
        P("ctx"),
        P("ctx", None),
        P(None, None, "ctx", ("fsdp", "tp")),
        P(None, "ctx", ("fsdp", "tp")),
    )
    return jax.shard_map(
        per_device,
        mesh=mesh,
        in_specs=placed,
        out_specs=(
            P(("fsdp", "ctx"), None),
            P(("fsdp", "ctx"), None),
            P(("fsdp", "ctx")),
            P(("fsdp", "ctx"), None),
            P(None, "ctx", ("fsdp", "tp")),
            P(None, "ctx", ("fsdp", "tp")),
            P(None, "ctx", ("fsdp", "tp")),
            P(("fsdp", "ctx")),
            P(("fsdp", "ctx"), None),
            P(None, None, "ctx", ("fsdp", "tp")),
            P(None, "ctx", ("fsdp", "tp")),
        ),
        check_vma=False,
    )
```
